32 devices in a mesh: dp: 4 (over z), tr: 2 (over core), tc: 4 (over y, x).
Axes of the slice: x: 2, y: 2, z: 4, core: 2. Of those that a mesh axis runs over, the one named last changes fastest.
Arguments:
- tokens: float32 [4, 32, 32, 384], P('dp', 'tr', 'tc'), may hold values from -6 to 6
- condition: float32 [4, 384], P('dp'), may hold values from -6 to 6
- cotangent: float32 [4, 32, 32, 384], P('dp', 'tr', 'tc'), may hold values from -6 to 6
- ada_weight: bfloat16 [2, 384, 2304], replicated, may hold values from -0.3125 to 0.3125
- ada_bias: float32 [2, 2304], replicated, may hold values from -1.5 to 1.5
- conv_weight: float32 [2, 3, 3, 384], replicated, may hold values from -2 to 2
- conv_bias: float32 [2, 384], replicated, may hold values from -1.5 to 1.5
- query_weight: bfloat16 [2, 384, 384], replicated, may hold values from -0.3125 to 0.3125
- key_weight: bfloat16 [2, 384, 384], replicated, may hold values from -0.3125 to 0.3125
- value_weight: bfloat16 [2, 384, 384], replicated, may hold values from -0.3125 to 0.3125
- out_weight: bfloat16 [2, 384, 384], replicated, may hold values from -0.3125 to 0.3125
- gate_weight: float32 [2, 384, 6], replicated, may hold values from -0.3125 to 0.3125
- gate_bias: float32 [2, 6], replicated, may hold values from -3 to 3
- up_weight: bfloat16 [2, 384, 1536], replicated, may hold values from -0.3125 to 0.3125
- up_bias: float32 [2, 1536], replicated, may hold values from -1.5 to 1.5
- down_weight: bfloat16 [2, 1536, 384], replicated, may hold values from -0.15625 to 0.15625
- down_bias: float32 [2, 384], replicated, may hold values from -1.5 to 1.5
Outputs:
- output: float32 [4, 32, 32, 384], P('dp', 'tr', 'tc')
- grad_tokens: float32 [4, 32, 32, 384], P('dp', 'tr', 'tc')
- grad_ada_weight: float32 [2, 384, 2304], P(None, 'dp', ('tr', 'tc'))
- grad_ada_bias: float32 [2, 2304], replicated
- grad_conv_weight: float32 [2, 3, 3, 384], replicated
- grad_conv_bias: float32 [2, 384], replicated
- grad_query_weight: float32 [2, 384, 384], P(None, 'dp', ('tr', 'tc'))
- grad_key_weight: float32 [2, 384, 384], P(None, 'dp', ('tr', 'tc'))
- grad_value_weight: float32 [2, 384, 384], P(None, 'dp', ('tr', 'tc'))
- grad_out_weight: float32 [2, 384, 384], P(None, 'dp', ('tr', 'tc'))
- grad_gate_weight: float32 [2, 384, 6], replicated
- grad_gate_bias: float32 [2, 6], replicated
- grad_up_weight: float32 [2, 384, 1536], P(None, 'dp', ('tr', 'tc'))
- grad_up_bias: float32 [2, 1536], replicated
- grad_down_weight: float32 [2, 1536, 384], P(None, 'dp', ('tr', 'tc'))
- grad_down_bias: float32 [2, 384], replicated
The draws below stay inside these ranges and needn't reach their ends.
All inputs are finite; a program needn't handle non-finite values.
Results may differ from the reference program's by a relative error of at most 0.024.
Values may be sent and summed in bfloat16 or wider, within the bound.
No kernel may reach another device: no remote copies, remote signals or barrier semaphores. Data moves between devices by JAX's collectives and lax.ppermute only.
A program may use at most 192 MiB of HBM per device.

```python
import jax
import jax.numpy as jnp
from jax import lax

D = 384
HEADS = 6
FF = 1536
GRID = 32
IMAGES = 4


def block_scale(own_key, shape, pieces, low, top_value):
    loudness = 1.0
    for axis_at, blocks in pieces:
        draws = jax.random.uniform(jax.random.fold_in(jax.random.fold_in(own_key, 6), axis_at), (blocks,), jnp.float32, low / len(pieces), top_value / len(pieces))
        loudness = loudness * jnp.repeat(jnp.exp(draws), shape[axis_at] // blocks).reshape((-1,) + (1,) * (len(shape) - 1 - axis_at))
    return loudness


def gaussian(stream_key, shape, deviation, bound, shards=(), kind=jnp.bfloat16):
    drawn = deviation * jax.random.normal(stream_key, shape, jnp.float32)
    if shards:
        drawn = drawn * block_scale(stream_key, shape, shards, -0.22, 0.18)
    return jnp.clip(drawn, -bound, bound).astype(kind)


def setup_inputs(seed: int = 0) -> dict:
    seeds = jax.random.split(jax.random.key(seed), 18)
    return {
        "tokens": gaussian(seeds[0], (IMAGES, GRID, GRID, D), 1.0, 6.0, ((0, 4), (1, 2), (2, 4)), jnp.float32),
        "condition": gaussian(seeds[1], (IMAGES, D), 1.0, 6.0, ((0, 4),), jnp.float32),
        "cotangent": gaussian(seeds[2], (IMAGES, GRID, GRID, D), 1.0, 6.0, ((0, 4), (1, 2), (2, 4)), jnp.float32),
        "ada_weight": gaussian(seeds[3], (2, D, 6 * D), D ** -0.5, 0.3125),
        "ada_bias": gaussian(seeds[4], (2, 6 * D), 0.3, 1.5, (), jnp.float32),
        "conv_weight": gaussian(seeds[5], (2, 3, 3, D), 9 ** -0.5, 2.0, (), jnp.float32),
        "conv_bias": gaussian(seeds[6], (2, D), 0.3, 1.5, (), jnp.float32),
        "query_weight": gaussian(seeds[7], (2, D, D), D ** -0.5, 0.3125),
        "key_weight": gaussian(seeds[8], (2, D, D), D ** -0.5, 0.3125),
        "value_weight": gaussian(seeds[9], (2, D, D), D ** -0.5, 0.3125),
        "out_weight": gaussian(seeds[10], (2, D, D), D ** -0.5, 0.3125),
        "gate_weight": gaussian(seeds[11], (2, D, HEADS), D ** -0.5, 0.3125, (), jnp.float32),
        "gate_bias": jnp.clip(jax.random.uniform(seeds[12], (2, HEADS), jnp.float32, -3.0, 3.0), -3.0, 3.0),
        "up_weight": gaussian(seeds[13], (2, D, FF), D ** -0.5, 0.3125),
        "up_bias": gaussian(seeds[14], (2, FF), 0.3, 1.5, (), jnp.float32),
        "down_weight": gaussian(seeds[15], (2, FF, D), FF ** -0.5, 0.15625),
        "down_bias": gaussian(seeds[16], (2, D), 0.3, 1.5, (), jnp.float32),
    }


HIGH = lax.Precision.HIGHEST
EPS = 1e-06
GATE_NORM = 16.0

@jax.custom_vjp
def low(v):
    return lax.optimization_barrier(v.astype(jnp.bfloat16)).astype(jnp.float32)

@jax.custom_vjp
def low_back(v):
    return v

def low_keep(v):
    return (low(v), None)

def low_pass(kept, grad):
    return (grad,)

def back_keep(v):
    return (v, None)

def back_low(kept, grad):
    return (low(grad),)
low.defvjp(low_keep, low_pass)
low_back.defvjp(back_keep, back_low)

def matmul(left, right):
    return jnp.matmul(left, right, precision=HIGH)

def layer_norm(values):
    center = values - lax.optimization_barrier(jnp.mean(values, axis=-1, keepdims=True))
    return center * lax.rsqrt(lax.optimization_barrier(jnp.mean(center * center, axis=-1, keepdims=True)) + EPS)

def modulate(activation, shift_part, scale_part):
    return layer_norm(activation) * (1.0 + scale_part) + shift_part

def to_lines(array, column, head_count):
    if column:
        array = jnp.swapaxes(array, 1, 2)
    images, outer, inner_len, model_width = array.shape
    return array.reshape(images * outer, inner_len, head_count, model_width // head_count)

def from_lines(line_rows, column, images):
    count_lines, inner_len, head_count, head_width = line_rows.shape
    array = line_rows.reshape(images, count_lines // images, inner_len, head_count * head_width)
    if column:
        array = jnp.swapaxes(array, 1, 2)
    return array

def decay_table(log_gate):
    cumulative = jnp.cumsum(log_gate, axis=1)
    by_head = jnp.swapaxes(cumulative, 1, 2)
    length = log_gate.shape[1]
    causal = lax.broadcasted_iota(jnp.int32, (length, length), 0) >= lax.broadcasted_iota(jnp.int32, (length, length), 1)
    spread = by_head[:, :, :, None] - by_head[:, :, None, :]
    return (cumulative, jnp.where(causal, jnp.exp(jnp.where(causal, spread, 0.0)), 0.0))

def line_mix(queries, keys_in, values_in, log_gate):
    cumulative, decays = decay_table(log_gate)
    scores = jnp.einsum('nthd,nshd->nhts', queries, keys_in, precision=HIGH) * queries.shape[-1] ** (-0.5)
    return jnp.einsum('nhts,nshd->nthd', scores * decays, values_in, precision=HIGH)

def conv_grid(padded, kernel):
    rows_in = padded.shape[1] - 2
    cols_in = padded.shape[2] - 2
    summed = jnp.zeros(padded.shape[:1] + (rows_in, cols_in) + padded.shape[3:], jnp.float32)
    for row_off in range(3):
        for col_off in range(3):
            summed = summed + padded[:, row_off:row_off + rows_in, col_off:col_off + cols_in, :] * kernel[row_off, col_off]
    return summed

def block(activation, cond_act, layer, column):
    ada_weight, ada_bias, conv_weight, conv_bias, query_weight, key_weight, value_weight, out_weight, gate_weight, gate_bias, up_weight, up_bias, down_weight, down_bias = layer
    model_width = activation.shape[-1]
    head_count = gate_bias.shape[-1]
    images = activation.shape[0]
    modulation = matmul(cond_act, ada_weight) + ada_bias
    segments = [modulation[:, None, None, segment * model_width:(segment + 1) * model_width] for segment in range(6)]
    shift_one, scale_one, gate_one, shift_two, scale_two, gate_two = segments
    normed = low(modulate(activation, shift_one, scale_one))
    padded = jnp.pad(normed, ((0, 0), (1, 1), (1, 1), (0, 0)))
    mixed = low(low_back(conv_grid(padded, conv_weight) + conv_bias))
    queries = low(low_back(matmul(mixed, query_weight)))
    keys_all = low(low_back(matmul(mixed, key_weight)))
    values_all = low(low_back(matmul(mixed, value_weight)))
    log_gate = jax.nn.log_sigmoid(matmul(mixed, gate_weight) + gate_bias) / GATE_NORM
    mixed_lines = line_mix(to_lines(queries, column, head_count), to_lines(keys_all, column, head_count), to_lines(values_all, column, head_count), to_lines(log_gate, column, head_count)[..., 0])
    attended = from_lines(mixed_lines, column, images)
    branch = low_back(matmul(low(attended), out_weight))
    resid = activation + gate_one * branch
    normed_two = low(modulate(resid, shift_two, scale_two))
    pre_act = low_back(matmul(normed_two, up_weight) + up_bias)
    hidden = low(jax.nn.gelu(pre_act, approximate=True))
    mlp_out = low_back(matmul(hidden, down_weight) + down_bias)
    return resid + gate_two * mlp_out

def forward_pass(activation, cond_act, weight_list):
    for block_id in range(2):
        layer = [member[block_id] for member in weight_list]
        activation = block(activation, cond_act, layer, block_id == 1)
    return activation

def reference(tokens, condition, cotangent, ada_weight, ada_bias, conv_weight, conv_bias, query_weight, key_weight, value_weight, out_weight, gate_weight, gate_bias, up_weight, up_bias, down_weight, down_bias):
    weight_list = tuple((member.astype(jnp.float32) for member in (ada_weight, ada_bias, conv_weight, conv_bias, query_weight, key_weight, value_weight, out_weight, gate_weight, gate_bias, up_weight, up_bias, down_weight, down_bias)))
    cond_act = low(jax.nn.silu(condition))
    group_size = 4
    groups = tokens.shape[0] // group_size

    def regroup(array):
        return array.reshape((groups, group_size) + array.shape[1:])

    def step(summed, inputs):
        tok_group, cond_group, cot_group = inputs

        def apply(activation, weights):
            return forward_pass(activation, cond_group, weights)
        result, pullback = jax.vjp(apply, tok_group, weight_list)
        grad_tok, grad_weights = pullback(cot_group)
        summed = tuple((left + right for left, right in zip(summed, grad_weights)))
        return (summed, (result, grad_tok))
    initial = tuple((jnp.zeros_like(member) for member in weight_list))
    summed, (outputs, grads) = lax.scan(step, initial, (regroup(tokens), regroup(cond_act), regroup(cotangent)))
    output = outputs.reshape(tokens.shape)
    grad_tokens = grads.reshape(tokens.shape)
    return (output, grad_tokens, summed[0], summed[1], summed[2], summed[3], summed[4], summed[5], summed[6], summed[7], summed[8], summed[9], summed[10], summed[11], summed[12], summed[13])
```

```python
import functools
import inspect
import math

import jax
import jax.numpy as jnp
from jax import lax
from jax.experimental import pallas as pl
from jax.experimental.pallas import tpu as pltpu
from jax.sharding import PartitionSpec as P

BF = jnp.bfloat16
F32 = jnp.float32
EPS = 1e-06
GATE_NORM = 16.0
HALO = 2
GELU_A = 0.7978845608028654
GELU_B = 0.044715
NEG = -1e30
VMEM_SPARE = 3 * 1024 * 1024
SMALL = 32


def mm(a, b):
    return jnp.dot(a, b, preferred_element_type=F32)


def mm_rt(a, b):
    return lax.dot_general(a, b, (((1,), (1,)), ((), ())), preferred_element_type=F32)


def mm_lt(a, b):
    return lax.dot_general(a, b, (((0,), (0,)), ((), ())), preferred_element_type=F32)


def hi_lo(x):
    hi = x.astype(BF)
    return hi, (x - hi.astype(F32)).astype(BF)


def normalize(x):
    center = x - jnp.mean(x, axis=-1, keepdims=True)
    rstd = lax.rsqrt(jnp.mean(center * center, axis=-1, keepdims=True) + EPS)
    return center * rstd, rstd


def normalize_back(g_y, y, rstd):
    return rstd * (
        g_y - jnp.mean(g_y, axis=-1, keepdims=True) - y * jnp.mean(g_y * y, axis=-1, keepdims=True)
    )


def iota(shape, dim):
    return lax.broadcasted_iota(jnp.int32, shape, dim)


def names(function):
    return tuple(inspect.signature(function).parameters)


class Table(dict):
    __getattr__ = dict.__getitem__


class Geo:
    def __init__(self, mesh, tokens, up):
        self.n_dp, self.n_tr, self.n_tc = (mesh.shape[a] for a in ("dp", "tr", "tc"))
        self.images, self.own, self.tile = (tokens[0] // self.n_dp, tokens[1] // self.n_tr, tokens[2] // self.n_tc)
        self.pos = tokens[2]
        self.d = tokens[3]
        self.ff = up[2]
        self.win = self.own + HALO
        self.t = self.win * self.pos
        self.to = self.own * self.pos
        self.lt = self.d // 128
        self.pairs = self.d // 128
        self.group = 64
        self.groups = self.t // self.group
        self.ch = 3 * self.pos
        self.chunks = self.t // self.ch
        self.big = 192
        self.bigs = self.t // self.big
        self.fc = 512
        self.fcs = self.ff // self.fc
        self.shift = self.pos - self.win
        self.rows = self.d // self.n_dp
        self.rp = -(-self.rows // 16) * 16
        self.rab = -(-(self.rp + self.rp // 2) // 16) * 16
        self.steps = self.n_dp.bit_length() - 1
        self.cols = self.d // (self.n_tr * self.n_tc)
        self.upc = self.ff // (self.n_tr * self.n_tc)


def kernel_taps(w, blk):
    at = slice(blk, blk + 1)
    return [[w.cw[a, b, at, :] if blk == 0 else w.cw[b, a, at, :] for b in range(3)] for a in range(3)]


def gate_rows(g, w, blk):
    heads = w.gw.shape[0]
    rows = [w.gw[h, blk : blk + 1, :] for h in range(heads)]
    return hi_lo(jnp.concatenate(rows + [jnp.zeros((128 - heads, g.d), F32)], axis=0))


def front(g, x, mod, base, w, s):
    d, pos, ch = g.d, g.pos, g.ch
    shift, scale = mod[base : base + 1, :], 1.0 + mod[base + 1 : base + 2, :]
    zero = jnp.zeros((pos, d), BF)
    s.pad[0:pos, :] = zero
    s.pad[g.t + pos : g.t + 2 * pos, :] = zero
    for i in range(g.chunks):
        rows = slice(i * ch, (i + 1) * ch)
        y, _ = normalize(x[rows, :])
        s.pad[pos + i * ch : pos + (i + 1) * ch, :] = (y * scale + shift).astype(BF)
    at = iota((ch, 1), 0) % pos
    first, last = at == 0, at == pos - 1
    taps = kernel_taps(w, base // 8)
    blk = base // 8
    bias = w.cb[blk : blk + 1, :]
    for i in range(g.chunks):
        wide = s.pad[i * ch : i * ch + ch + 2 * pos, :].astype(F32)
        lines = [wide[a * pos : a * pos + ch, :] for a in range(3)]
        v = [sum(lines[a] * taps[a][b] for a in range(3)) for b in range(3)]
        mixed = v[1] + bias
        mixed = mixed + jnp.where(first, 0.0, pltpu.roll(v[0], 1, 0))
        mixed = mixed + jnp.where(last, 0.0, pltpu.roll(v[2], ch - 1, 0))
        s.mixed[i * ch : (i + 1) * ch, :] = mixed.astype(BF)
    for out, weight in ((s.q, w.wq), (s.k, w.wk), (s.v, w.wv)):
        out[...] = mm(s.mixed[...], weight[...]).astype(BF)
    g_hi, g_lo = gate_rows(g, w, blk)
    mixed = s.mixed[...]
    heads = w.gb.shape[1]
    bias = jnp.concatenate([w.gb[blk : blk + 1, :], jnp.zeros((1, 128 - heads), F32)], axis=1)
    pre = mm_rt(mixed, g_hi) + mm_rt(mixed, g_lo) + bias
    s.gp[...] = pre
    run = (jnp.minimum(pre, 0.0) - jnp.log1p(jnp.exp(-jnp.abs(pre)))) * (1.0 / GATE_NORM)
    at = iota((g.t, 1), 0) % pos
    step = 1
    while step < pos:
        run = run + jnp.where(at >= step, pltpu.roll(run, step, 0), 0.0)
        step *= 2
    s.cum[0 : g.t, :] = run


def decay_rows(g, s):
    lane = iota((1, 128), 1)
    found = {}
    for m in range((g.t + 127) // 128):
        full = s.cum[m * 128 : (m + 1) * 128, :].T
        for j in range(g.pairs):
            one, two = full[2 * j : 2 * j + 1, :], full[2 * j + 1 : 2 * j + 2, :]
            lo_row = jnp.where(lane < 64, one, pltpu.roll(two, 64, 1))
            hi_row = jnp.where(lane < 64, pltpu.roll(one, 64, 1), two)
            found[2 * m, j] = lo_row
            found[2 * m + 1, j] = hi_row
    return found


def pair_masks(g):
    row, lane = iota((64, 128), 0), iota((64, 128), 1)
    src = lane % 64
    same = (row // g.pos) == (src // g.pos)
    return lane < 64, same & (row >= src), same & (row > src)


def split_heads(block, low_half):
    zero = jnp.zeros_like(block)
    return jnp.concatenate([jnp.where(low_half, block, zero), jnp.where(low_half, zero, block)], axis=0)


def pair_blocks(g):
    for grp in range(g.groups):
        for j in range(g.pairs):
            yield grp, slice(grp * 64, grp * 64 + 64), j, slice(j * 128, j * 128 + 128)


def pair_decay(s, source, grp, j, low_half, causal):
    rows = slice(grp * 64, grp * 64 + 64)
    ct = jnp.where(low_half, s.cum[rows, 2 * j : 2 * j + 1], s.cum[rows, 2 * j + 1 : 2 * j + 2])
    return jnp.exp(jnp.where(causal, ct - source[grp, j], NEG)) * 0.125


def attend(g, s):
    low_half, causal, _ = pair_masks(g)
    source = decay_rows(g, s)
    for grp, rows, j, lanes in pair_blocks(g):
        scores = mm_rt(s.q[rows, lanes], split_heads(s.k[rows, lanes], low_half))
        decay = pair_decay(s, source, grp, j, low_half, causal)
        s.decay[rows, lanes] = decay.astype(BF)
        s.prob[rows, lanes] = (scores * decay).astype(BF)
    for _, rows, _, lanes in pair_blocks(g):
        s.att[rows, lanes] = mm(s.prob[rows, lanes], split_heads(s.v[rows, lanes], low_half)).astype(BF)


def tail(g, x, mod, base, w, s, emit):
    gate_one, gate_two = mod[base + 2 : base + 3, :], mod[base + 5 : base + 6, :]
    shift, scale = mod[base + 3 : base + 4, :], 1.0 + mod[base + 4 : base + 5, :]
    for i in range(g.bigs):
        rows = slice(i * g.big, (i + 1) * g.big)
        branch = mm(s.att[rows, :], w.wo[...])
        s.branch[rows, :] = branch.astype(BF)
        resid = x[rows, :] + gate_one * branch
        s.resid[rows, :] = resid
        y, _ = normalize(resid)
        s.n2[rows, :] = (y * scale + shift).astype(BF)
    for f in range(g.fcs):
        fl = slice(f * g.fc, (f + 1) * g.fc)
        for i in range(g.bigs):
            rows = slice(i * g.big, (i + 1) * g.big)
            pre = mm(s.n2[rows, :], w.up[:, fl]) + w.upb[base // 8 : base // 8 + 1, fl]
            sq = pre * pre
            th = jnp.tanh(pre * (GELU_A + (GELU_A * GELU_B) * sq))
            half = 0.5 * (1.0 + th)
            s.hid[rows, fl] = (pre * half).astype(BF)
            inner = GELU_A + (3.0 * GELU_A * GELU_B) * sq
            s.gel[rows, fl] = (half + (0.5 * pre) * (1.0 - th * th) * inner).astype(s.gel.dtype)
    for i in range(g.bigs):
        rows = slice(i * g.big, (i + 1) * g.big)
        mlp = mm(s.hid[rows, :], w.down[...]) + w.downb[base // 8 : base // 8 + 1, :]
        s.mlp[rows, :] = mlp.astype(s.mlp.dtype)
        emit(i, s.resid[rows, :] + gate_two * mlp)


def select_cols(width, source, half, tc, c, n_tc, lanes):
    row, lane = iota((source, 2 * half), 0), iota((source, 2 * half), 1)
    core = jnp.where(lane < half, c, 1 - c)
    inside = lane % half - lanes
    want = (core * n_tc + tc) * width + inside
    hit = (row == want) & (inside >= 0) & (inside < width)
    return jnp.where(hit, 1.0, 0.0).astype(BF)


def own_sum(g, c, ref, lanes=None):
    start = pl.multiple_of(c * (HALO * g.pos), HALO * g.pos)
    if lanes is None:
        return ref[pl.ds(start, g.to), :]
    return ref[pl.ds(start, g.to), lanes]


def colsum(a):
    return jnp.sum(a.astype(F32), axis=0, keepdims=True)


def lay(g, dst, lane0, value):
    lanes = slice(lane0, lane0 + value.shape[1])
    if g.rp == g.rows:
        dst[:, lanes] = value.astype(dst.dtype)
        return
    for n in range(g.n_dp):
        part = value[n * g.rows : (n + 1) * g.rows, :]
        pad = jnp.zeros((g.rp - g.rows, value.shape[1]), F32)
        dst[n * g.rp : (n + 1) * g.rp, lanes] = jnp.concatenate([part, pad], axis=0).astype(dst.dtype)


def ffn_back(g, c, tc, g_out, mod, base, w, s, o):
    gate_one, gate_two = mod[base + 2 : base + 3, :], mod[base + 5 : base + 6, :]
    scale = 1.0 + mod[base + 4 : base + 5, :]
    for i in range(g.bigs):
        rows = slice(i * g.big, (i + 1) * g.big)
        s.gmlp[rows, :] = (gate_two * g_out[rows, :]).astype(BF)
    for f in range(g.fcs):
        fl = slice(f * g.fc, (f + 1) * g.fc)
        for i in range(g.bigs):
            rows = slice(i * g.big, (i + 1) * g.big)
            g_hid = mm_rt(s.gmlp[rows, :], w.down[fl, :])
            s.gpre[rows, fl] = (s.gel[rows, fl].astype(F32) * g_hid).astype(BF)
    for i in range(g.bigs):
        rows = slice(i * g.big, (i + 1) * g.big)
        g_n2 = mm_rt(s.gpre[rows, :], w.up[...])
        y, rstd = normalize(s.resid[rows, :])
        g_res = g_out[rows, :] + normalize_back(g_n2 * scale, y, rstd)
        s.gres[rows, :] = g_res
        s.tmp1[rows, :] = g_n2
        s.tmp2[rows, :] = g_n2 * y
        s.gbr[rows, :] = (gate_one * g_res).astype(BF)
    own = functools.partial(own_sum, g, c)
    small = o.small
    small[2:3, :] = colsum(own(s.gres) * own(s.branch).astype(F32))
    small[3:4, :] = colsum(own(s.tmp1))
    small[4:5, :] = colsum(own(s.tmp2))
    small[5:6, :] = colsum(own(g_out) * own(s.mlp).astype(F32))
    for f in range(g.ff // g.d):
        small[18 + f : 19 + f, :] = colsum(own(s.gpre, slice(f * g.d, (f + 1) * g.d)))
    small[22:23, :] = colsum(own(s.gmlp))
    sel = mm(own(s.gpre), select_cols(g.upc, g.ff, 256, tc, c, g.n_tc, 0)).astype(BF)
    s.upg[...] = mm_lt(own(s.n2), sel)
    sel = mm(own(s.gmlp), select_cols(g.cols, g.d, 64, tc, c, g.n_tc, 0)).astype(BF)
    s.dn[...] = mm_lt(own(s.hid), sel)
    lane = iota((g.rows, 128), 1)
    per = g.ff // g.d
    for dd in range(g.n_dp):
        up = slice(dd * g.rows, (dd + 1) * g.rows)
        down = [s.dn[(dd * per + j) * g.rows : (dd * per + j + 1) * g.rows, :] for j in range(per)]
        for at, shift, dst in ((0, 0, o.keep), (256, 64, o.send)):
            to = slice(dd * g.rp, dd * g.rp + g.rows)
            one, two, three, four = (
                pltpu.roll(part, (lanes - shift) % 128, 1) for part, lanes in zip(down, (64, 112, 32, 80))
            )
            mid = jnp.where(lane < 112, one, two)
            dst[to, 0:128] = s.upg[up, at : at + 128].astype(dst.dtype)
            dst[to, 128:256] = jnp.where(lane < 64, s.upg[up, at + 128 : at + 256], mid).astype(dst.dtype)
            end = jnp.where(lane < 80, three, four)
            dst[to, 256:384] = jnp.where(lane < 32, two, end).astype(dst.dtype)


def attn_core(g, w, s):
    low_half, causal, strict = pair_masks(g)
    s.gatt[...] = mm_rt(s.gbr[...], w.wo[...]).astype(BF)
    row, col = iota((64, 64), 0), iota((64, 64), 1)
    later = jnp.where((row // g.pos == col // g.pos) & (col >= row), 1.0, 0.0).astype(BF)
    head_of = iota((g.d, 128), 0) // 64
    to_head = jnp.where(head_of == iota((g.d, 128), 1), 1.0, 0.0).astype(BF)
    for _, rows, _, lanes in pair_blocks(g):
        d_p = mm_rt(s.gatt[rows, lanes], split_heads(s.v[rows, lanes], low_half))
        s.dlow[rows, lanes] = (d_p * s.decay[rows, lanes].astype(F32)).astype(BF)
        s.wlow[rows, lanes] = (d_p * s.prob[rows, lanes].astype(F32)).astype(BF)
    strict3 = jnp.concatenate([strict] * g.pairs, axis=1)
    for grp in range(g.groups):
        rows = slice(grp * 64, grp * 64 + 64)
        s.ulow[rows, :] = jnp.where(strict3, mm(later, s.wlow[rows, :]), 0.0).astype(BF)
    for _, rows, j, lanes in pair_blocks(g):
        km = split_heads(s.k[rows, lanes], low_half)
        s.gqkv[rows, j * 128 : j * 128 + 128] = mm(s.dlow[rows, lanes], km).astype(BF)
    for _, rows, j, lanes in pair_blocks(g):
        both = mm_lt(s.dlow[rows, lanes], s.q[rows, lanes])
        s.gqkv[rows, g.d + j * 128 : g.d + j * 128 + 128] = jnp.where(
            low_half, both[0:64, :], both[64:128, :]
        ).astype(BF)
    for _, rows, j, lanes in pair_blocks(g):
        both = mm_lt(s.prob[rows, lanes], s.gatt[rows, lanes])
        s.gqkv[rows, 2 * g.d + j * 128 : 2 * g.d + j * 128 + 128] = jnp.where(
            low_half, both[0:64, :], both[64:128, :]
        ).astype(BF)
    g_log = mm(s.ulow[...], to_head)
    s.ggp[...] = g_log * (jax.nn.sigmoid(-s.gp[...]) * (1.0 / GATE_NORM))


def proj_grads(g, c, tc, s, o, lane0):
    own = functools.partial(own_sum, g, c)
    small = o.small
    sel = jnp.zeros((g.to, 512), F32)
    for n in range(3):
        sel = sel + mm(
            own(s.gqkv, slice(n * g.d, (n + 1) * g.d)),
            select_cols(g.cols, g.d, 256, tc, c, g.n_tc, n * g.cols),
        )
    grads = mm_lt(own(s.mixed), sel.astype(BF))
    sel = mm(own(s.gbr), select_cols(g.cols, g.d, 256, tc, c, g.n_tc, 3 * g.cols)).astype(BF)
    grads = grads + mm_lt(own(s.att), sel)
    lay(g, o.keep, lane0, grads[:, 0:256])
    lay(g, o.send, lane0, grads[:, 256:512])
    gg = own(s.ggp)
    hi, lo = hi_lo(gg)
    mixed = own(s.mixed)
    gate = mm_lt(hi, mixed) + mm_lt(lo, mixed)
    small[23:29, :] = gate[0:6, :]
    small[29:30, 0:128] = colsum(gg)
    small[29:30, 128 : g.d] = jnp.zeros((1, g.d - 128), F32)


def mixed_back(g, blk, w, s):
    pos, d = g.pos, g.d
    w_hi, w_lo = gate_rows(g, w, blk)
    zero = jnp.zeros((pos, d), F32)
    s.gpad[0:pos, :] = zero
    s.gpad[g.t + pos : g.t + 2 * pos, :] = zero
    for i in range(g.bigs):
        rows = slice(i * g.big, (i + 1) * g.big)
        hi, lo = hi_lo(s.ggp[rows, :])
        total = mm(hi, w_hi) + mm(lo, w_hi) + mm(hi, w_lo)
        for n, weight in enumerate((w.wq, w.wk, w.wv)):
            total = total + mm_rt(s.gqkv[rows, n * d : (n + 1) * d], weight[...])
        s.gpad[pos + i * g.big : pos + (i + 1) * g.big, :] = total.astype(BF).astype(F32)


def conv_back(g, c, x, mod, base, w, s, o, emit):
    pos, ch, d = g.pos, g.ch, g.d
    own = functools.partial(own_sum, g, c)
    small = o.small
    at = iota((ch, 1), 0) % pos
    first, last = at == 0, at == pos - 1
    taps = kernel_taps(w, base // 8)
    scale = 1.0 + mod[base + 1 : base + 2, :]
    for i in range(g.chunks):
        rows = slice(i * ch, (i + 1) * ch)
        lines = [s.gpad[i * ch + a * pos : i * ch + a * pos + ch, :] for a in range(3)]
        v = [sum(lines[2 - a] * taps[a][b] for a in range(3)) for b in range(3)]
        g_n = v[1]
        g_n = g_n + jnp.where(last, 0.0, pltpu.roll(v[0], ch - 1, 0))
        g_n = g_n + jnp.where(first, 0.0, pltpu.roll(v[2], 1, 0))
        y, rstd = normalize(x[rows, :])
        s.tmp1[rows, :] = g_n
        s.tmp2[rows, :] = g_n * y
        emit(i, s.gres[rows, :] + normalize_back(g_n * scale, y, rstd))
    small[0:1, :] = colsum(own(s.tmp1))
    small[1:2, :] = colsum(own(s.tmp2))


def kernel_grads(g, c, mod, s, o):
    pos, d = g.pos, g.d
    small = o.small
    oc = 4 * pos
    at = iota((oc, 1), 0) % pos
    first, last = at == 0, at == pos - 1
    sums = [jnp.zeros((8, d), F32) for _ in range(10)]
    for i in range(g.to // oc):
        start = c * (HALO * pos) + i * oc
        mid = s.gpad[pl.ds(pl.multiple_of(start + pos, pos), oc), :]
        shifted = [
            jnp.where(last, 0.0, pltpu.roll(mid, oc - 1, 0)),
            mid,
            jnp.where(first, 0.0, pltpu.roll(mid, 1, 0)),
        ]
        for a in range(3):
            line = s.pad[pl.ds(pl.multiple_of(start + a * pos, pos), oc), :].astype(F32)
            for b in range(3):
                sums[3 * a + b] = sums[3 * a + b] + jnp.sum((line * shifted[b]).reshape(oc // 8, 8, d), axis=0)
        sums[9] = sums[9] + jnp.sum(mid.reshape(oc // 8, 8, d), axis=0)
    for n in range(10):
        small[8 + n : 9 + n, :] = jnp.sum(sums[n], axis=0, keepdims=True)
    small[6:7, :] = mod[6:7, :]
    small[7:8, :] = jnp.zeros((1, d), F32)
    small[30:SMALL, :] = jnp.zeros((SMALL - 30, d), F32)


def attn_back(g, c, tc, x, mod, base, w, s, o, lane0, emit):
    attn_core(g, w, s)
    proj_grads(g, c, tc, s, o, lane0)
    mixed_back(g, base // 8, w, s)
    conv_back(g, c, x, mod, base, w, s, o, emit)
    kernel_grads(g, c, mod, s, o)


def k_prep(g, s):
    c = s.meta[0]
    t = s.tok[0].reshape(g.own * g.tile, g.d).astype(BF)
    s.tokb[...] = t
    s.cotb[...] = s.cot[0].reshape(g.own * g.tile, g.d).astype(BF)
    edge = HALO * g.tile

    @pl.when(c == 0)
    def _():
        s.halo[...] = t[g.own * g.tile - edge :, :]

    @pl.when(c == 1)
    def _():
        s.halo[...] = t[0:edge, :]


def k_extend(g, s):
    c = s.meta[0]
    edge = HALO * g.tile
    own = g.own * g.tile
    s.ext[pl.ds(pl.multiple_of(c * edge, edge), own), :] = s.tokb[...]
    s.ext[pl.ds(pl.multiple_of((1 - c) * own, edge), edge), :] = s.halo[...]
    s.ext[own + edge : own + edge + own, :] = s.cotb[...]


def k_modulate(g, s):
    mod = s.mod
    act = jax.nn.silu(s.cond[...]).astype(BF)
    rows = jnp.broadcast_to(act, (16, g.d))
    for b in range(2):
        for n in range(6):
            lanes = slice(n * g.d, (n + 1) * g.d)
            out = mm(rows, s.ada_w[b, :, lanes])[0:1, :] + s.ada_b[b : b + 1, lanes]
            mod[b * 8 + n : b * 8 + n + 1, :] = out
        mod[b * 8 + 6 : b * 8 + 7, :] = act.astype(F32)
        mod[b * 8 + 7 : b * 8 + 8, :] = jnp.zeros((1, g.d), F32)


def place_tiles(g, s, lo, lines, dst):
    tc = s.meta[1]
    for k in range(g.n_tc):
        part = s.tiles[k][lo : lo + lines * g.tile, :].astype(F32)
        off = (tc ^ k) * g.tile
        for i in range(lines):
            dst[pl.ds(pl.multiple_of(i * g.pos + off, g.tile), g.tile), :] = part[i * g.tile : (i + 1) * g.tile, :]


def turn(g, ref, start, dst):
    block = ref[pl.ds(start, g.to), :].reshape(g.own, g.pos, g.d)
    dst[...] = jnp.swapaxes(block, 0, 1).reshape(g.to, g.d)


def part_of(g, ref, core):
    return ref[pl.ds(pl.multiple_of(core * (g.shift * g.own), g.own), g.win * g.own), :]


STACKED = names(lambda wq, wk, wv, wo, up, down: None)


FRONT_W = names(lambda cw, cb, wq, wk, wv, gw, gb: None)
TAIL_W = names(lambda wo, up, upb, down, downb: None)
SAVE = names(lambda x, mixed, q, k, v, gp, att, branch, resid, n2, hid, gel, mlp, prob, decay, pad: None)


def save_shapes(g):
    t, d, ff = g.t, g.d, g.ff
    return Table(
        x=((t, d), F32),
        mixed=((t, d), BF),
        q=((t, d), BF),
        k=((t, d), BF),
        v=((t, d), BF),
        gp=((t, 128), F32),
        att=((t, d), BF),
        branch=((t, d), BF),
        resid=((t, d), F32),
        n2=((t, d), BF),
        hid=((t, ff), BF),
        gel=((t, ff), BF),
        mlp=((t, d), BF),
        prob=((t, d), BF),
        decay=((t, d), BF),
        pad=((t + 2 * g.pos, d), BF),
        cum=(((t + 127) // 128 * 128, 128), F32),
    )


def back_shapes(g):
    t, d, ff = g.t, g.d, g.ff
    return Table(
        gmlp=((t, d), BF),
        gpre=((t, ff), BF),
        gres=((t, d), F32),
        tmp1=((t, d), F32),
        tmp2=((t, d), F32),
        gbr=((t, d), BF),
        dn=((ff, 128), F32),
        upg=((d, 512), F32),
        gatt=((t, d), BF),
        dlow=((t, d), BF),
        wlow=((t, d), BF),
        ulow=((t, d), BF),
        gqkv=((t, 3 * d), BF),
        ggp=((t, 128), F32),
        gpad=((t + 2 * g.pos, d), F32),
    )


def k_first(g, s):
    c = s.meta[0]
    x, mod, turned = s.x, s.mod, s.turned
    place_tiles(g, s, 0, g.win, x)
    s.cum[g.t :, :] = jnp.zeros((s.cum.shape[0] - g.t, 128), F32)
    front(g, x, mod, 0, s, s)
    attend(g, s)

    def emit(i, value):
        s.mid[i * g.big : (i + 1) * g.big, :] = value

    tail(g, x, mod, 0, s, s, emit)
    place_tiles(g, s, g.win * g.tile, g.own, s.cot_full)
    half = g.win * g.own
    turn(g, s.cot_full, 0, turned)
    s.keep_cot[...] = part_of(g, turned, c)
    s.send[half : 2 * half, :] = part_of(g, turned, 1 - c).astype(BF)
    turn(g, s.mid, pl.multiple_of(c * (HALO * g.pos), g.pos), turned)
    s.keep_mid[...] = part_of(g, turned, c)
    s.send[0:half, :] = part_of(g, turned, 1 - c).astype(BF)


def weave(g, c, keep, recv, lo, dst):
    for i in range(g.win):
        rows = slice(i * g.own, (i + 1) * g.own)
        a = pl.multiple_of(i * g.pos + c * g.own, g.own)
        b = pl.multiple_of(i * g.pos + (1 - c) * g.own, g.own)
        dst[pl.ds(a, g.own), :] = keep[rows, :].astype(F32)
        dst[pl.ds(b, g.own), :] = recv[lo + i * g.own : lo + (i + 1) * g.own, :].astype(F32)


def k_second(g, s):
    c, tc = s.meta[0], s.meta[1]
    x, mod, turned = s.x, s.mod, s.turned
    half = g.win * g.own
    weave(g, c, s.keep_mid, s.recv, 0, x)
    weave(g, c, s.keep_cot, s.recv, half, s.gout)
    s.cum[g.t :, :] = jnp.zeros((s.cum.shape[0] - g.t, 128), F32)
    front(g, x, mod, 8, s, s)
    attend(g, s)

    def emit(i, value):
        s.three[i * g.big : (i + 1) * g.big, :] = value

    tail(g, x, mod, 8, s, s, emit)
    turn(g, s.three, pl.multiple_of(c * (HALO * g.pos), g.pos), turned)
    at = (tc * g.tile) % g.own
    for r in range(g.own):
        rows = slice(r * g.tile, (r + 1) * g.tile)
        mine = pl.multiple_of((c * g.own + r) * g.own + at, g.tile)
        theirs = pl.multiple_of(((1 - c) * g.own + r) * g.own + at, g.tile)
        s.tile_keep[rows, :] = turned[pl.ds(mine, g.tile), :]
        s.tile_send[rows, :] = turned[pl.ds(theirs, g.tile), :]


def k_ffn_back(g, base, s):
    c, tc = s.meta[0], s.meta[1]
    if base == 0:
        weave(g, c, s.g_keep, s.g_recv, 0, s.gout)
    s.small[...] = jnp.zeros((SMALL, g.d), F32)
    ffn_back(g, c, tc, s.gout, s.mod, base, s, s, s)


def k_core(g, base, s):
    c, tc = s.meta[0], s.meta[1]
    attn_core(g, s, s)
    mixed_back(g, base // 8, s, s)
    s.small[...] = s.small_in[...]

    def emit(i, value):
        s.gin[i * g.ch : (i + 1) * g.ch, :] = value

    conv_back(g, c, s.x, s.mod, base, s, s, s, emit)
    turned = s.turned
    turn(g, s.gin, pl.multiple_of(c * (HALO * g.pos), g.pos), turned)
    if base:
        s.g_keep[...] = part_of(g, turned, c)
        s.g_send[...] = part_of(g, turned, 1 - c).astype(BF)
        return
    size = g.tile * g.own
    block = turned[pl.ds(pl.multiple_of(tc * size, size), size), :]
    s.tile[...] = jnp.swapaxes(block.reshape(g.tile, g.own, g.d), 0, 1).reshape(size, g.d)


def k_weights(g, base, s):
    c, tc = s.meta[0], s.meta[1]
    s.small[...] = s.small_in[...]
    proj_grads(g, c, tc, s, s, 0)
    kernel_grads(g, c, s.mod, s, s)


def both_cores(s):
    both = s.small[...] + s.small_recv[...]
    return jnp.where(iota(both.shape, 0) == 6, s.small[...], both)


def side_by_side(g, part):
    half = g.rp // 2
    return jnp.concatenate([part[0:half, 0:192], part[half:, 0:192]], axis=1)


def k_join(g, both, s):
    bit = s.meta[2] % 2
    s.sum_a[...] = s.keep_a[...] + s.recv_a[...].astype(F32)
    size, half = g.rp, g.rp // 2
    if both:
        size = g.rab
        s.sum_b[...] = s.keep_b[...] + s.recv_b[...].astype(F32)
        small = both_cores(s)
        s.apart[...], s.summed[...] = small[0:8, :], small[8:SMALL, :]
        end = (g.n_dp // 2) * size
        s.send[end : end + 24, :] = small[8:SMALL, :].astype(BF)
        s.send[end + 24 : end + 32, :] = small[0:8, :].astype(BF)
    for m in range(g.n_dp // 2):
        for which, dst in ((bit, s.held), (1 - bit, s.send)):
            rows = pl.ds(pl.multiple_of((2 * m + which) * g.rp, g.rp), g.rp)
            dst[m * size : m * size + g.rp, :] = s.sum_a[rows, :].astype(dst.dtype)
            if both:
                packed = side_by_side(g, s.sum_b[rows, :])
                rest = size - g.rp - half
                if rest:
                    packed = jnp.concatenate([packed, jnp.zeros((rest, g.d), F32)], axis=0)
                dst[m * size + g.rp : (m + 1) * size, :] = packed.astype(dst.dtype)


def k_step(g, step, size, s):
    parts = g.n_dp >> (step + 1)
    s.total[...] = s.got[...] + s.recv[0 : parts * size, :].astype(F32)
    blocks = 8 << step
    both = size == g.rab
    end = parts * size
    if both:
        summed = s.was_summed[...] + s.recv[end : end + 24, :].astype(F32)
        s.summed[...] = summed
        s.apart[0:blocks, :] = s.was_apart[...]
        s.apart[blocks : 2 * blocks, :] = s.recv[end + 24 : end + 24 + blocks, :].astype(F32)
    if parts == 1:
        return
    bit = (s.meta[2] // (2 << step)) % 2
    for m in range(parts // 2):
        for which, dst in ((bit, s.held), (1 - bit, s.send)):
            rows = pl.ds(pl.multiple_of((2 * m + which) * size, size), size)
            dst[m * size : (m + 1) * size, :] = s.total[rows, :].astype(dst.dtype)
    if both:
        end = (parts // 2) * size
        s.send[end : end + 24, :] = summed.astype(BF)
        s.send[end + 24 : end + 24 + 2 * blocks, :] = s.apart[...].astype(BF)


def k_last(g, s):
    me = s.meta[2]
    s.sum_b[...] = s.keep_b[...] + s.recv_b[...].astype(F32)
    small = both_cores(s)
    for k in range(g.n_dp):
        rows = pl.ds(pl.multiple_of((me ^ k) * g.rp, g.rp), g.rp)
        out = s.parts[k]
        out[0:SMALL, :] = small.astype(out.dtype)
        out[SMALL:, :] = side_by_side(g, s.sum_b[rows, :]).astype(out.dtype)


def finish(g, b, s, ab, proj, summed, apart):
    c, tc, me = s.meta[0], s.meta[1], s.meta[2]
    idx = c * g.n_tc + tc
    rp, rows, half = g.rp, g.rows, g.rp // 2
    acc, acct = s.acc, s.acct
    s.up_weight[b] = ab[0:rows, 0 : g.upc]
    acc[0:rp, 0:384] = ab
    acc[0:half, 384:576] = proj[:, 0:192]
    acc[half:rp, 384:576] = proj[:, 192:384]
    for n in range(1, 5):
        acct[n * 128 : (n + 1) * 128, :] = acc[:, n * 128 : (n + 1) * 128].T
    for j in range(g.ff // g.d):
        at = 192 + g.cols * j
        s.down_weight[b, :, j * rows : (j + 1) * rows] = acct[at : at + g.cols, 0:rows]
    for j, ref in enumerate((s.query, s.key, s.value, s.proj)):
        at = 384 + g.cols * j
        ref[b] = acct[at : at + g.cols, 0:rows]
    for a in range(3):
        for e in range(3):
            at = 3 * a + e if b == 0 else 3 * e + a
            s.conv_weight[a, e, b : b + 1, :] = summed[at : at + 1, :]
    s.conv_bias[b : b + 1, :] = summed[9:10, :]
    for m in range(g.ff // g.d):
        s.up_bias[b : b + 1, m * g.d : (m + 1) * g.d] = summed[10 + m : 11 + m, :]
    s.down_bias[b : b + 1, :] = summed[14:15, :]
    for h in range(6):
        s.gate_weight[h, b : b + 1, :] = summed[15 + h : 16 + h, :]
    s.row[...] = jnp.broadcast_to(summed[21:22, :], (8, g.d))
    s.gate_bias[b : b + 1, :] = s.row[0:1, 0:6]
    width = 6 * g.d // (g.n_tr * g.n_tc)
    wide = 384
    prod = jnp.zeros((g.d, wide), F32)
    total = apart[0]
    for part in apart[1:]:
        total = total + part
    for m in range(6):
        s.ada_bias[b : b + 1, m * g.d : (m + 1) * g.d] = total[m : m + 1, :]
    for part in apart:
        flat = jnp.concatenate([part[m : m + 1, :] for m in range(6)], axis=1)
        s.gms[...] = jnp.broadcast_to(flat, (8, 6 * g.d))
        full = pltpu.roll(s.gms[...], 6 * g.d - idx * width, 1)
        cond = jnp.broadcast_to(part[6:7, :], (8, g.d)).T
        prod = prod + cond[:, 0:1] * full[0:1, 0:wide]
    prod = pltpu.roll(prod, g.d - me * rows, 0)
    s.ada_weight[b] = prod[0:rows, 0:width]


FINAL = names(
    lambda ada_weight, ada_bias, conv_weight, conv_bias, query, key, value, proj, gate_weight, gate_bias,
    up_weight, up_bias, down_weight, down_bias: None
)
BY_ROW = names(lambda ada_bias, conv_bias, gate_bias, up_bias, down_bias: None)
INNER = names(lambda conv_weight, gate_weight: None)


def k_final_one(g, s):
    c, tc = s.meta[0], s.meta[1]
    near = (tc * g.tile) // g.own == c

    @pl.when(near)
    def _():
        s.out[0] = s.tile_keep[...].reshape(g.own, g.tile, g.d)

    @pl.when(jnp.logical_not(near))
    def _():
        s.out[0] = s.tile_recv[...].reshape(g.own, g.tile, g.d)

    half = g.rp // 2
    total = s.got[...]
    apart = [s.apart[8 * n : 8 * n + 8, :] for n in range(g.n_dp)]
    finish(g, 1, s, total[0 : g.rp, :], total[g.rp : g.rp + half, :], s.summed[...], apart)


def k_final(g, s):
    for name in FINAL:
        src, dst = s.first[name], s[name]
        if name in BY_ROW:
            dst[1:2, :] = src[1:2, :]
        elif name in INNER:
            lead = (slice(None),) * (len(dst.shape) - 2)
            dst[lead + (slice(1, 2),)] = src[lead + (slice(1, 2),)]
        else:
            dst[1] = src[1]
    ab = s.held[...] + s.recv[...].astype(F32)
    proj = s.parts[0][SMALL:, :]
    summed = s.parts[0][8:SMALL, :]
    apart = []
    for k, part in enumerate(s.parts):
        wide = part[...].astype(F32)
        apart.append(wide[0:8, :])
        if k:
            summed = summed + wide[8:SMALL, :]
            proj = proj + wide[SMALL:, :]
    finish(g, 0, s, ab, proj, summed, apart)


def padded_bytes(shape, dtype):
    shape = (1,) * (2 - len(shape)) + tuple(shape)
    rows, lanes = -(-shape[-2] // 16) * 16, -(-shape[-1] // 128) * 128
    return math.prod(shape[:-2]) * rows * lanes * jnp.dtype(dtype).itemsize


def call(us, kernel, ins, outs, scratch=(), weights=(), block=0, spare=VMEM_SPARE):
    ins = Table(ins, **dict(weights))
    ins, outs, scratch = dict(ins), dict(outs), dict(scratch)
    flat, tree = jax.tree.flatten(ins)
    spread_outs = [o if isinstance(o, list) else [o] for o in outs.values()]
    flat_outs = [o for group in spread_outs for o in group]
    meta = ins.get("meta")

    def run(*refs):
        refs = list(refs)

        def take(n):
            got = refs[:n]
            del refs[:n]
            return got

        table = Table(jax.tree.unflatten(tree, take(len(flat))))
        for name, ref in table.items():
            if name in STACKED:
                table[name] = ref.at[block]
        for name, o in outs.items():
            table[name] = take(len(o)) if isinstance(o, list) else take(1)[0]
        table.update(zip(scratch, refs))
        kernel(table)

    held = [(a.shape, a.dtype) for a in flat] + flat_outs + list(scratch.values())
    need = sum(padded_bytes(*h) for h in held)
    results = pl.pallas_call(
        run,
        in_specs=[pl.BlockSpec(memory_space=pltpu.SMEM if a is meta else pltpu.VMEM) for a in flat],
        out_specs=[pl.BlockSpec(memory_space=pltpu.VMEM)] * len(flat_outs),
        out_shape=[jax.ShapeDtypeStruct(*o) for o in flat_outs],
        scratch_shapes=[pltpu.VMEM(*sc) for sc in scratch.values()],
        compiler_params=pltpu.CompilerParams(vmem_limit_bytes=need + need // 16 + spare),
        cost_estimate=pl.CostEstimate(flops=int(us * 1e9), bytes_accessed=int(us * 3e6), transcendentals=0),
    )(*flat)
    results = list(results)
    found = Table()
    for name, o in outs.items():
        if isinstance(o, list):
            found[name] = results[: len(o)]
            del results[: len(o)]
        else:
            found[name] = results.pop(0)
    return found


def body(
    g,
    tokens,
    condition,
    cotangent,
    ada_weight,
    ada_bias,
    conv_weight,
    conv_bias,
    query_weight,
    key_weight,
    value_weight,
    out_weight,
    gate_weight,
    gate_bias,
    up_weight,
    up_bias,
    down_weight,
    down_bias,
):
    d, ff, t = g.d, g.ff, g.t
    meta = jnp.stack(
        [lax.axis_index("tr"), lax.axis_index("tc"), lax.axis_index("dp"), jnp.int32(0)]
    ).astype(jnp.int32)

    def xor(axis, k):
        return [(i, i ^ k) for i in range(lax.axis_size(axis))]

    def other(array):
        return lax.ppermute(array, "tr", [(0, 1), (1, 0)])

    part = functools.partial
    tile, half, deep = g.own * g.tile, g.win * g.own, g.n_dp * g.rp
    shapes, backs = save_shapes(g), back_shapes(g)
    weights = Table(
        wq=query_weight,
        wk=key_weight,
        wv=value_weight,
        wo=out_weight,
        gw=jnp.transpose(gate_weight, (2, 0, 1)),
        gb=gate_bias,
        cw=jnp.transpose(conv_weight, (1, 2, 0, 3)),
        cb=conv_bias,
        up=up_weight,
        upb=up_bias,
        down=down_weight,
        downb=down_bias,
    )

    def pick(table, names):
        return {n: table[n] for n in names}

    r = call(
        1,
        part(k_prep, g),
        Table(meta=meta, tok=tokens, cot=cotangent),
        Table(tokb=((tile, d), BF), cotb=((tile, d), BF), halo=((HALO * g.tile, d), BF)),
    )
    ext = call(
        1,
        part(k_extend, g),
        Table(meta=meta, tokb=r.tokb, cotb=r.cotb, halo=other(r.halo)),
        Table(ext=((half // 2 + tile, d), BF)),
    ).ext
    ext, condition = lax.optimization_barrier((ext, condition))
    tiles = [ext] + [lax.ppermute(ext, "tc", xor("tc", k)) for k in range(1, g.n_tc)]
    mod = call(
        1,
        part(k_modulate, g),
        Table(cond=condition, ada_w=ada_weight, ada_b=ada_bias),
        Table(mod=((16, d), F32)),
    ).mod
    base_ins = Table(meta=meta, mod=mod)
    save0 = call(
        8,
        part(k_first, g),
        Table(**base_ins, tiles=tiles),
        Table(
            keep_mid=((half, d), F32),
            keep_cot=((half, d), F32),
            send=((2 * half, d), BF),
            **pick(shapes, SAVE),
        ),
        Table(mid=((t, d), F32), cot_full=((g.to, d), F32), turned=((g.to, d), F32), cum=shapes.cum),
        pick(weights, FRONT_W + TAIL_W),
        0,
    )
    save1 = call(
        8,
        part(k_second, g),
        Table(**base_ins, **pick(save0, names(lambda keep_mid, keep_cot: None)), recv=other(save0.send)),
        Table(
            tile_keep=((tile, d), F32),
            tile_send=((tile, d), F32),
            gout=((t, d), F32),
            **pick(shapes, SAVE),
        ),
        Table(three=((t, d), F32), turned=((g.to, d), F32), cum=shapes.cum),
        pick(weights, FRONT_W + TAIL_W),
        1,
    )
    tile_recv = other(save1.tile_send)

    def ffn(b, save, ins):
        return call(
            4,
            part(k_ffn_back, g, 8 * b),
            Table(**base_ins, **ins, **pick(save, names(lambda gel, resid, branch, mlp, n2, hid: None))),
            Table(
                gres=backs.gres,
                gbr=backs.gbr,
                keep=((deep, d), F32),
                send=((deep, d), BF),
                small=((SMALL, d), F32),
            ),
            Table(**pick(backs, names(lambda gmlp, gpre, tmp1, tmp2, dn, upg: None)), **({} if b else Table(gout=((t, d), F32)))),
            pick(weights, names(lambda down, up: None)),
            b,
        )

    def core(b, save, f):
        ends = Table(g_keep=((half, d), F32), g_send=((half, d), BF)) if b else Table(tile=((tile, d), F32))
        return call(
            4,
            part(k_core, g, 8 * b),
            Table(
                **base_ins,
                **pick(f, names(lambda gres, gbr: None)),
                small_in=f.small,
                **pick(save, names(lambda x, q, k, v, gp, prob, decay: None)),
            ),
            Table(**ends, **pick(backs, names(lambda gqkv, ggp, gpad: None)), small=((SMALL, d), F32)),
            Table(
                **pick(backs, names(lambda gatt, dlow, wlow, ulow, tmp1, tmp2: None)),
                gin=((t, d), F32),
                turned=((g.to, d), F32),
            ),
            pick(weights, names(lambda wo, wq, wk, wv, gw, cw: None)),
            b,
        )

    def wgrads(b, save, f, e):
        return call(
            2,
            part(k_weights, g, 8 * b),
            Table(
                **base_ins,
                small_in=e.small,
                **pick(e, names(lambda gqkv, ggp, gpad: None)),
                gbr=f.gbr,
                **pick(save, names(lambda mixed, att, pad: None)),
            ),
            Table(keep=((deep, 256), F32), send=((deep, 256), BF), small=((SMALL, d), F32)),
        )

    def last_of(h):
        return Table(
            keep_b=h.keep,
            recv_b=other(h.send),
            small=h.small,
            small_recv=other(h.small),
        )

    def join(f, h=None):
        size, end = (g.rab, 32) if h else (g.rp, 0)
        rest = Table(apart=((8, d), F32), summed=((24, d), F32)) if h else Table()
        found = call(
            1,
            part(k_join, g, h is not None),
            Table(meta=meta, keep_a=f.keep, recv_a=f.recv, **(last_of(h) if h else {})),
            Table(
                held=((g.n_dp // 2 * size, d), F32),
                send=((g.n_dp // 2 * size + end, d), BF),
                **rest,
            ),
            Table(sum_a=((deep, d), F32), **(Table(sum_b=((deep, 256), F32)) if h else {})),
        )
        return Table(found, size=size)

    def hop(state, step):
        return Table(state, recv=lax.ppermute(state.send, "dp", xor("dp", 1 << step)))

    def take(state, step):
        size, parts = state.size, g.n_dp >> (step + 1)
        both = size == g.rab
        blocks = 16 << step
        end = -(-(24 + blocks) // 16) * 16 if both else 0
        outs, scratch = Table(), Table()
        total = ((parts * size, d), F32)
        if parts > 1:
            outs = Table(held=((parts // 2 * size, d), F32), send=((parts // 2 * size + end, d), BF))
            scratch = Table(total=total)
        else:
            outs = Table(total=total)
        ins = Table(meta=meta, got=state.held, recv=state.recv)
        if both:
            ins = Table(ins, was_apart=state.apart, was_summed=state.summed)
            outs = Table(outs, apart=((blocks, d), F32), summed=((24, d), F32))
        return Table(call(1, part(k_step, g, step, size), ins, outs, scratch), size=size)

    def spread(parts):
        return [parts[0]] + [lax.ppermute(parts[k], "dp", xor("dp", k)) for k in range(1, g.n_dp)]

    f1 = ffn(1, save1, Table(gout=save1.gout))
    f1 = Table(f1, recv=other(f1.send))
    e1 = core(1, save1, f1)
    g_recv = other(e1.g_send)
    h1 = wgrads(1, save1, f1, e1)
    f0 = ffn(0, save0, Table(g_keep=e1.g_keep, g_recv=g_recv))
    f0 = Table(f0, recv=other(f0.send))
    one = join(f1, h1)
    gres, send = lax.optimization_barrier((f0.gres, one.send))
    f0, one = Table(f0, gres=gres), hop(Table(one, send=send), 0)
    e0 = core(0, save0, f0)
    one, two = take(one, 0), join(f0)
    if g.steps > 1:
        small, send_one, send_two = lax.optimization_barrier((e0.small, one.send, two.send))
        e0, one, two = Table(e0, small=small), Table(one, send=send_one), Table(two, send=send_two)
    if g.steps > 1:
        one = hop(one, 1)
    two = hop(two, 0)
    h0 = wgrads(0, save0, f0, e0)
    for step in range(1, g.steps):
        two = hop(take(two, step - 1), step)
        if step > 1:
            one = hop(take(one, step - 1), step)
    if g.steps > 1:
        one = take(one, g.steps - 1)
    parts0 = spread(
        call(
            1,
            part(k_last, g),
            Table(meta=meta, **last_of(h0)),
            Table(parts=[((SMALL + g.rp // 2, d), BF if k else F32) for k in range(g.n_dp)]),
            Table(sum_b=((deep, 256), F32)),
        ).parts
    )
    n_cols = g.n_tr * g.n_tc
    shards = ((2, g.cols, g.rows), F32)
    final_shapes = dict(
        zip(
            FINAL,
            (
                ((2, g.rows, 6 * d // n_cols), F32),
                ((2, 6 * d), F32),
                ((3, 3, 2, d), F32),
                ((2, d), F32),
                shards,
                shards,
                shards,
                shards,
                ((6, 2, d), F32),
                ((2, 6), F32),
                ((2, g.rows, g.upc), F32),
                ((2, ff), F32),
                ((2, g.cols, ff // g.n_dp), F32),
                ((2, d), F32),
            ),
        )
    )
    scratch = Table(acc=((128, 640), F32), acct=((640, 128), F32), row=((8, d), F32), gms=((8, 6 * d), F32))
    first = call(
        3,
        part(k_final_one, g),
        Table(
            meta=meta,
            tile_keep=save1.tile_keep,
            tile_recv=tile_recv,
            got=one.total,
            apart=one.apart,
            summed=one.summed,
        ),
        Table(final_shapes, out=(tokens.shape, F32)),
        scratch,
        spare=6 * VMEM_SPARE,
    )
    output = first.out
    finals = call(
        3,
        part(k_final, g),
        Table(
            meta=meta,
            held=two.held,
            recv=two.recv,
            parts=parts0,
            first={n: first[n] for n in FINAL},
        ),
        final_shapes,
        scratch,
        spare=6 * VMEM_SPARE,
    )
    finals = [finals[n] for n in FINAL]
    finals[2] = jnp.transpose(finals[2], (2, 0, 1, 3))
    finals[8] = jnp.transpose(finals[8], (1, 2, 0))
    for n in (4, 5, 6, 7, 12):
        finals[n] = jnp.swapaxes(finals[n], 1, 2)
    return (output, e0.tile.reshape(tokens.shape)) + tuple(finals)


def solution(mesh):
    everywhere = P()
    tiles = P("dp", "tr", "tc", None)
    cut = P(None, "dp", ("tr", "tc"))
    in_specs = (tiles, P("dp", None), tiles) + (everywhere,) * 14
    out_specs = (tiles, tiles, cut, P(), P(), P(), cut, cut, cut, cut, P(), P(), cut, P(), cut, P())

    def program(*arrays):
        g = Geo(mesh, arrays[0].shape, arrays[13].shape)
        run = functools.partial(body, g)
        return jax.shard_map(run, mesh=mesh, in_specs=in_specs, out_specs=out_specs, check_vma=False)(*arrays)

    return program
```

```python
import functools
import inspect
import math

import jax
import jax.numpy as jnp
from jax import lax
from jax.experimental import pallas as pl
from jax.experimental.pallas import tpu as pltpu
from jax.sharding import PartitionSpec as P

BF = jnp.bfloat16
F32 = jnp.float32
EPS = 1e-06
GATE_NORM = 16.0
HALO = 2
GELU_A = 0.7978845608028654
GELU_B = 0.044715
NEG = -1e30
VMEM_SPARE = 3 * 1024 * 1024
SMALL = 32


def mm(a, b):
    return jnp.dot(a, b, preferred_element_type=F32)


def mm_rt(a, b):
    return lax.dot_general(a, b, (((1,), (1,)), ((), ())), preferred_element_type=F32)


def mm_lt(a, b):
    return lax.dot_general(a, b, (((0,), (0,)), ((), ())), preferred_element_type=F32)


def hi_lo(x):
    hi = x.astype(BF)
    return hi, (x - hi.astype(F32)).astype(BF)


def normalize(x):
    center = x - jnp.mean(x, axis=-1, keepdims=True)
    rstd = lax.rsqrt(jnp.mean(center * center, axis=-1, keepdims=True) + EPS)
    return center * rstd, rstd


def normalize_back(g_y, y, rstd):
    return rstd * (
        g_y - jnp.mean(g_y, axis=-1, keepdims=True) - y * jnp.mean(g_y * y, axis=-1, keepdims=True)
    )


def iota(shape, dim):
    return lax.broadcasted_iota(jnp.int32, shape, dim)


def names(function):
    return tuple(inspect.signature(function).parameters)


class Table(dict):
    __getattr__ = dict.__getitem__


class Geo:
    def __init__(self, mesh, tokens, up):
        self.n_dp, self.n_tr, self.n_tc = (mesh.shape[a] for a in ("dp", "tr", "tc"))
        self.images, self.own, self.tile = (tokens[0] // self.n_dp, tokens[1] // self.n_tr, tokens[2] // self.n_tc)
        self.pos = tokens[2]
        self.d = tokens[3]
        self.ff = up[2]
        self.win = self.own + HALO
        self.t = self.win * self.pos
        self.to = self.own * self.pos
        self.lt = self.d // 128
        self.pairs = self.d // 128
        self.group = 64
        self.groups = self.t // self.group
        self.ch = 3 * self.pos
        self.chunks = self.t // self.ch
        self.big = 192
        self.bigs = self.t // self.big
        self.fc = 512
        self.fcs = self.ff // self.fc
        self.shift = self.pos - self.win
        self.rows = self.d // self.n_dp
        self.rp = -(-self.rows // 16) * 16
        self.rab = -(-(self.rp + self.rp // 2) // 16) * 16
        self.steps = self.n_dp.bit_length() - 1
        self.cols = self.d // (self.n_tr * self.n_tc)
        self.upc = self.ff // (self.n_tr * self.n_tc)


def kernel_taps(w, blk):
    at = slice(blk, blk + 1)
    return [[w.cw[a, b, at, :] if blk == 0 else w.cw[b, a, at, :] for b in range(3)] for a in range(3)]


def gate_rows(g, w, blk):
    heads = w.gw.shape[0]
    rows = [w.gw[h, blk : blk + 1, :] for h in range(heads)]
    return hi_lo(jnp.concatenate(rows + [jnp.zeros((128 - heads, g.d), F32)], axis=0))


def front(g, x, mod, base, w, s):
    d, pos, ch = g.d, g.pos, g.ch
    shift, scale = mod[base : base + 1, :], 1.0 + mod[base + 1 : base + 2, :]
    zero = jnp.zeros((pos, d), BF)
    s.pad[0:pos, :] = zero
    s.pad[g.t + pos : g.t + 2 * pos, :] = zero
    for i in range(g.chunks):
        rows = slice(i * ch, (i + 1) * ch)
        y, _ = normalize(x[rows, :])
        s.pad[pos + i * ch : pos + (i + 1) * ch, :] = (y * scale + shift).astype(BF)
    at = iota((ch, 1), 0) % pos
    first, last = at == 0, at == pos - 1
    taps = kernel_taps(w, base // 8)
    blk = base // 8
    bias = w.cb[blk : blk + 1, :]
    for i in range(g.chunks):
        wide = s.pad[i * ch : i * ch + ch + 2 * pos, :].astype(F32)
        lines = [wide[a * pos : a * pos + ch, :] for a in range(3)]
        v = [sum(lines[a] * taps[a][b] for a in range(3)) for b in range(3)]
        mixed = v[1] + bias
        mixed = mixed + jnp.where(first, 0.0, pltpu.roll(v[0], 1, 0))
        mixed = mixed + jnp.where(last, 0.0, pltpu.roll(v[2], ch - 1, 0))
        s.mixed[i * ch : (i + 1) * ch, :] = mixed.astype(BF)
    for out, weight in ((s.q, w.wq), (s.k, w.wk), (s.v, w.wv)):
        out[...] = mm(s.mixed[...], weight[...]).astype(BF)
    g_hi, g_lo = gate_rows(g, w, blk)
    mixed = s.mixed[...]
    heads = w.gb.shape[1]
    bias = jnp.concatenate([w.gb[blk : blk + 1, :], jnp.zeros((1, 128 - heads), F32)], axis=1)
    pre = mm_rt(mixed, g_hi) + mm_rt(mixed, g_lo) + bias
    s.gp[...] = pre
    run = (jnp.minimum(pre, 0.0) - jnp.log1p(jnp.exp(-jnp.abs(pre)))) * (1.0 / GATE_NORM)
    at = iota((g.t, 1), 0) % pos
    step = 1
    while step < pos:
        run = run + jnp.where(at >= step, pltpu.roll(run, step, 0), 0.0)
        step *= 2
    s.cum[0 : g.t, :] = run


def decay_rows(g, s):
    lane = iota((1, 128), 1)
    found = {}
    for m in range((g.t + 127) // 128):
        full = s.cum[m * 128 : (m + 1) * 128, :].T
        for j in range(g.pairs):
            one, two = full[2 * j : 2 * j + 1, :], full[2 * j + 1 : 2 * j + 2, :]
            lo_row = jnp.where(lane < 64, one, pltpu.roll(two, 64, 1))
            hi_row = jnp.where(lane < 64, pltpu.roll(one, 64, 1), two)
            found[2 * m, j] = lo_row
            found[2 * m + 1, j] = hi_row
    return found


def pair_masks(g):
    row, lane = iota((64, 128), 0), iota((64, 128), 1)
    src = lane % 64
    same = (row // g.pos) == (src // g.pos)
    return lane < 64, same & (row >= src), same & (row > src)


def split_heads(block, low_half):
    zero = jnp.zeros_like(block)
    return jnp.concatenate([jnp.where(low_half, block, zero), jnp.where(low_half, zero, block)], axis=0)


def pair_blocks(g):
    for grp in range(g.groups):
        for j in range(g.pairs):
            yield grp, slice(grp * 64, grp * 64 + 64), j, slice(j * 128, j * 128 + 128)


def pair_decay(s, source, grp, j, low_half, causal):
    rows = slice(grp * 64, grp * 64 + 64)
    ct = jnp.where(low_half, s.cum[rows, 2 * j : 2 * j + 1], s.cum[rows, 2 * j + 1 : 2 * j + 2])
    return jnp.exp(jnp.where(causal, ct - source[grp, j], NEG)) * 0.125


def attend(g, s):
    low_half, causal, _ = pair_masks(g)
    source = decay_rows(g, s)
    for grp, rows, j, lanes in pair_blocks(g):
        scores = mm_rt(s.q[rows, lanes], split_heads(s.k[rows, lanes], low_half))
        decay = pair_decay(s, source, grp, j, low_half, causal)
        s.decay[rows, lanes] = decay.astype(BF)
        s.prob[rows, lanes] = (scores * decay).astype(BF)
    for _, rows, _, lanes in pair_blocks(g):
        s.att[rows, lanes] = mm(s.prob[rows, lanes], split_heads(s.v[rows, lanes], low_half)).astype(BF)


def tail(g, x, mod, base, w, s, emit):
    gate_one, gate_two = mod[base + 2 : base + 3, :], mod[base + 5 : base + 6, :]
    shift, scale = mod[base + 3 : base + 4, :], 1.0 + mod[base + 4 : base + 5, :]
    for i in range(g.bigs):
        rows = slice(i * g.big, (i + 1) * g.big)
        branch = mm(s.att[rows, :], w.wo[...])
        s.branch[rows, :] = branch.astype(BF)
        resid = x[rows, :] + gate_one * branch
        s.resid[rows, :] = resid
        y, _ = normalize(resid)
        s.n2[rows, :] = (y * scale + shift).astype(BF)
    for f in range(g.fcs):
        fl = slice(f * g.fc, (f + 1) * g.fc)
        for i in range(g.bigs):
            rows = slice(i * g.big, (i + 1) * g.big)
            pre = mm(s.n2[rows, :], w.up[:, fl]) + w.upb[base // 8 : base // 8 + 1, fl]
            sq = pre * pre
            th = jnp.tanh(pre * (GELU_A + (GELU_A * GELU_B) * sq))
            half = 0.5 * (1.0 + th)
            s.hid[rows, fl] = (pre * half).astype(BF)
            inner = GELU_A + (3.0 * GELU_A * GELU_B) * sq
            s.gel[rows, fl] = (half + (0.5 * pre) * (1.0 - th * th) * inner).astype(s.gel.dtype)
    for i in range(g.bigs):
        rows = slice(i * g.big, (i + 1) * g.big)
        mlp = mm(s.hid[rows, :], w.down[...]) + w.downb[base // 8 : base // 8 + 1, :]
        s.mlp[rows, :] = mlp.astype(s.mlp.dtype)
        emit(i, s.resid[rows, :] + gate_two * mlp)


def select_cols(width, source, half, tc, c, n_tc, lanes):
    row, lane = iota((source, 2 * half), 0), iota((source, 2 * half), 1)
    core = jnp.where(lane < half, c, 1 - c)
    inside = lane % half - lanes
    want = (core * n_tc + tc) * width + inside
    hit = (row == want) & (inside >= 0) & (inside < width)
    return jnp.where(hit, 1.0, 0.0).astype(BF)


def own_sum(g, c, ref, lanes=None):
    start = pl.multiple_of(c * (HALO * g.pos), HALO * g.pos)
    if lanes is None:
        return ref[pl.ds(start, g.to), :]
    return ref[pl.ds(start, g.to), lanes]


def colsum(a):
    return jnp.sum(a.astype(F32), axis=0, keepdims=True)


def lay(g, dst, lane0, value):
    lanes = slice(lane0, lane0 + value.shape[1])
    if g.rp == g.rows:
        dst[:, lanes] = value.astype(dst.dtype)
        return
    for n in range(g.n_dp):
        part = value[n * g.rows : (n + 1) * g.rows, :]
        pad = jnp.zeros((g.rp - g.rows, value.shape[1]), F32)
        dst[n * g.rp : (n + 1) * g.rp, lanes] = jnp.concatenate([part, pad], axis=0).astype(dst.dtype)


def ffn_back(g, c, tc, g_out, mod, base, w, s, o):
    gate_one, gate_two = mod[base + 2 : base + 3, :], mod[base + 5 : base + 6, :]
    scale = 1.0 + mod[base + 4 : base + 5, :]
    for i in range(g.bigs):
        rows = slice(i * g.big, (i + 1) * g.big)
        s.gmlp[rows, :] = (gate_two * g_out[rows, :]).astype(BF)
    for f in range(g.fcs):
        fl = slice(f * g.fc, (f + 1) * g.fc)
        for i in range(g.bigs):
            rows = slice(i * g.big, (i + 1) * g.big)
            g_hid = mm_rt(s.gmlp[rows, :], w.down[fl, :])
            s.gpre[rows, fl] = (s.gel[rows, fl].astype(F32) * g_hid).astype(BF)
    for i in range(g.bigs):
        rows = slice(i * g.big, (i + 1) * g.big)
        g_n2 = mm_rt(s.gpre[rows, :], w.up[...])
        y, rstd = normalize(s.resid[rows, :])
        g_res = g_out[rows, :] + normalize_back(g_n2 * scale, y, rstd)
        s.gres[rows, :] = g_res
        s.tmp1[rows, :] = g_n2
        s.tmp2[rows, :] = g_n2 * y
        s.gbr[rows, :] = (gate_one * g_res).astype(BF)
    own = functools.partial(own_sum, g, c)
    small = o.small
    small[2:3, :] = colsum(own(s.gres) * own(s.branch).astype(F32))
    small[3:4, :] = colsum(own(s.tmp1))
    small[4:5, :] = colsum(own(s.tmp2))
    small[5:6, :] = colsum(own(g_out) * own(s.mlp).astype(F32))
    for f in range(g.ff // g.d):
        small[18 + f : 19 + f, :] = colsum(own(s.gpre, slice(f * g.d, (f + 1) * g.d)))
    small[22:23, :] = colsum(own(s.gmlp))
    n2 = own(s.n2)
    for at, core in ((0, c), (256, 1 - c)):
        first = (core * g.n_tc + tc) * g.upc
        lanes = pl.ds(pl.multiple_of(first // 128 * 128, 128), 256)
        grads = mm_lt(n2, own(s.gpre, lanes))
        s.upg[:, at : at + 256] = jnp.where(first % 128 == 0, grads, pltpu.roll(grads, 192, 1))
    sel = mm(own(s.gmlp), select_cols(g.cols, g.d, 64, tc, c, g.n_tc, 0)).astype(BF)
    s.dn[...] = mm_lt(own(s.hid), sel)
    lane = iota((g.rows, 128), 1)
    per = g.ff // g.d
    for dd in range(g.n_dp):
        up = slice(dd * g.rows, (dd + 1) * g.rows)
        down = [s.dn[(dd * per + j) * g.rows : (dd * per + j + 1) * g.rows, :] for j in range(per)]
        for at, shift, dst in ((0, 0, o.keep), (256, 64, o.send)):
            to = slice(dd * g.rp, dd * g.rp + g.rows)
            one, two, three, four = (
                pltpu.roll(part, (lanes - shift) % 128, 1) for part, lanes in zip(down, (64, 112, 32, 80))
            )
            mid = jnp.where(lane < 112, one, two)
            dst[to, 0:128] = s.upg[up, at : at + 128].astype(dst.dtype)
            dst[to, 128:256] = jnp.where(lane < 64, s.upg[up, at + 128 : at + 256], mid).astype(dst.dtype)
            end = jnp.where(lane < 80, three, four)
            dst[to, 256:384] = jnp.where(lane < 32, two, end).astype(dst.dtype)


def attn_core(g, w, s):
    low_half, causal, strict = pair_masks(g)
    s.gatt[...] = mm_rt(s.gbr[...], w.wo[...]).astype(BF)
    row, col = iota((64, 64), 0), iota((64, 64), 1)
    later = jnp.where((row // g.pos == col // g.pos) & (col >= row), 1.0, 0.0).astype(BF)
    head_of = iota((g.d, 128), 0) // 64
    to_head = jnp.where(head_of == iota((g.d, 128), 1), 1.0, 0.0).astype(BF)
    for _, rows, _, lanes in pair_blocks(g):
        d_p = mm_rt(s.gatt[rows, lanes], split_heads(s.v[rows, lanes], low_half))
        s.dlow[rows, lanes] = (d_p * s.decay[rows, lanes].astype(F32)).astype(BF)
        s.wlow[rows, lanes] = (d_p * s.prob[rows, lanes].astype(F32)).astype(BF)
    strict3 = jnp.concatenate([strict] * g.pairs, axis=1)
    for grp in range(g.groups):
        rows = slice(grp * 64, grp * 64 + 64)
        s.ulow[rows, :] = jnp.where(strict3, mm(later, s.wlow[rows, :]), 0.0).astype(BF)
    for _, rows, j, lanes in pair_blocks(g):
        km = split_heads(s.k[rows, lanes], low_half)
        s.gqkv[rows, j * 128 : j * 128 + 128] = mm(s.dlow[rows, lanes], km).astype(BF)
    for _, rows, j, lanes in pair_blocks(g):
        both = mm_lt(s.dlow[rows, lanes], s.q[rows, lanes])
        s.gqkv[rows, g.d + j * 128 : g.d + j * 128 + 128] = jnp.where(
            low_half, both[0:64, :], both[64:128, :]
        ).astype(BF)
    for _, rows, j, lanes in pair_blocks(g):
        both = mm_lt(s.prob[rows, lanes], s.gatt[rows, lanes])
        s.gqkv[rows, 2 * g.d + j * 128 : 2 * g.d + j * 128 + 128] = jnp.where(
            low_half, both[0:64, :], both[64:128, :]
        ).astype(BF)
    g_log = mm(s.ulow[...], to_head)
    s.ggp[...] = g_log * (jax.nn.sigmoid(-s.gp[...]) * (1.0 / GATE_NORM))


def proj_grads(g, c, tc, s, o, lane0):
    own = functools.partial(own_sum, g, c)
    small = o.small
    pick_cols = select_cols(g.cols, g.d, 64, tc, c, g.n_tc, 0)
    sel = [mm(own(s.gqkv, slice(n * g.d, (n + 1) * g.d)), pick_cols).astype(BF) for n in range(3)]
    sel_out = mm(own(s.gbr), pick_cols).astype(BF)
    grads = mm_lt(own(s.mixed), jnp.concatenate(sel, axis=1))
    three = mm_lt(own(s.att), sel_out)
    zero, one, two = (grads[:, n * 128 : (n + 1) * 128] for n in range(3))
    lane = iota((g.d, 128), 1)
    for shift, dst in ((0, o.keep), (64, o.send)):
        q, k, v, out = (
            pltpu.roll(part, (lanes - shift) % 128, 1)
            for part, lanes in ((zero, 0), (one, 48), (two, 96), (three, 16))
        )
        lay(g, dst, lane0, jnp.where(lane < 48, q, jnp.where(lane < 96, k, v)))
        lay(g, dst, lane0 + 128, jnp.where(lane < 16, v, out))
    gg = own(s.ggp)
    hi, lo = hi_lo(gg)
    mixed = own(s.mixed)
    gate = mm_lt(hi, mixed) + mm_lt(lo, mixed)
    small[23:29, :] = gate[0:6, :]
    small[29:30, 0:128] = colsum(gg)
    small[29:30, 128 : g.d] = jnp.zeros((1, g.d - 128), F32)


def mixed_back(g, blk, w, s):
    pos, d = g.pos, g.d
    w_hi, w_lo = gate_rows(g, w, blk)
    zero = jnp.zeros((pos, d), F32)
    s.gpad[0:pos, :] = zero
    s.gpad[g.t + pos : g.t + 2 * pos, :] = zero
    for i in range(g.bigs):
        rows = slice(i * g.big, (i + 1) * g.big)
        hi, lo = hi_lo(s.ggp[rows, :])
        total = mm(hi, w_hi) + mm(lo, w_hi) + mm(hi, w_lo)
        for n, weight in enumerate((w.wq, w.wk, w.wv)):
            total = total + mm_rt(s.gqkv[rows, n * d : (n + 1) * d], weight[...])
        s.gpad[pos + i * g.big : pos + (i + 1) * g.big, :] = total.astype(BF).astype(F32)


def conv_back(g, c, x, mod, base, w, s, o, emit):
    pos, ch, d = g.pos, g.ch, g.d
    own = functools.partial(own_sum, g, c)
    small = o.small
    at = iota((ch, 1), 0) % pos
    first, last = at == 0, at == pos - 1
    taps = kernel_taps(w, base // 8)
    scale = 1.0 + mod[base + 1 : base + 2, :]
    for i in range(g.chunks):
        rows = slice(i * ch, (i + 1) * ch)
        lines = [s.gpad[i * ch + a * pos : i * ch + a * pos + ch, :] for a in range(3)]
        v = [sum(lines[2 - a] * taps[a][b] for a in range(3)) for b in range(3)]
        g_n = v[1]
        g_n = g_n + jnp.where(last, 0.0, pltpu.roll(v[0], ch - 1, 0))
        g_n = g_n + jnp.where(first, 0.0, pltpu.roll(v[2], 1, 0))
        y, rstd = normalize(x[rows, :])
        s.tmp1[rows, :] = g_n
        s.tmp2[rows, :] = g_n * y
        emit(i, s.gres[rows, :] + normalize_back(g_n * scale, y, rstd))
    small[0:1, :] = colsum(own(s.tmp1))
    small[1:2, :] = colsum(own(s.tmp2))


def kernel_grads(g, c, mod, s, o):
    pos, d = g.pos, g.d
    small = o.small
    oc = 4 * pos
    at = iota((oc, 1), 0) % pos
    first, last = at == 0, at == pos - 1
    sums = [jnp.zeros((8, d), F32) for _ in range(10)]
    for i in range(g.to // oc):
        start = c * (HALO * pos) + i * oc
        mid = s.gpad[pl.ds(pl.multiple_of(start + pos, pos), oc), :]
        shifted = [
            jnp.where(last, 0.0, pltpu.roll(mid, oc - 1, 0)),
            mid,
            jnp.where(first, 0.0, pltpu.roll(mid, 1, 0)),
        ]
        for a in range(3):
            line = s.pad[pl.ds(pl.multiple_of(start + a * pos, pos), oc), :].astype(F32)
            for b in range(3):
                sums[3 * a + b] = sums[3 * a + b] + jnp.sum((line * shifted[b]).reshape(oc // 8, 8, d), axis=0)
        sums[9] = sums[9] + jnp.sum(mid.reshape(oc // 8, 8, d), axis=0)
    for n in range(10):
        small[8 + n : 9 + n, :] = jnp.sum(sums[n], axis=0, keepdims=True)
    small[6:7, :] = mod[6:7, :]
    small[7:8, :] = jnp.zeros((1, d), F32)
    small[30:SMALL, :] = jnp.zeros((SMALL - 30, d), F32)


def attn_back(g, c, tc, x, mod, base, w, s, o, lane0, emit):
    attn_core(g, w, s)
    proj_grads(g, c, tc, s, o, lane0)
    mixed_back(g, base // 8, w, s)
    conv_back(g, c, x, mod, base, w, s, o, emit)
    kernel_grads(g, c, mod, s, o)


def k_prep(g, s):
    c = s.meta[0]
    t = s.tok[0].reshape(g.own * g.tile, g.d).astype(BF)
    s.tokb[...] = t
    edge = HALO * g.tile

    @pl.when(c == 0)
    def _():
        s.halo[...] = t[g.own * g.tile - edge :, :]

    @pl.when(c == 1)
    def _():
        s.halo[...] = t[0:edge, :]


def k_cast(g, s):
    s.low[...] = s.cot[0].reshape(g.own * g.tile, g.d).astype(BF)


def k_rows(g, s):
    c, size = s.meta[0], g.own * g.tile
    s.both[pl.ds(pl.multiple_of(c * size, size), size), :] = s.mine[...]
    s.both[pl.ds(pl.multiple_of((1 - c) * size, size), size), :] = s.theirs[...]


def k_stack(s):
    rows = s.mine.shape[0]
    s.both[0:rows, :] = s.mine[...]
    s.both[rows:, :] = s.theirs[...]


def k_extend(g, s):
    c = s.meta[0]
    edge = HALO * g.tile
    own = g.own * g.tile
    s.ext[pl.ds(pl.multiple_of(c * edge, edge), own), :] = s.tokb[...]
    s.ext[pl.ds(pl.multiple_of((1 - c) * own, edge), edge), :] = s.halo[...]


def k_modulate(g, s):
    mod = s.mod
    act = jax.nn.silu(s.cond[...]).astype(BF)
    rows = jnp.broadcast_to(act, (16, g.d))
    for b in range(2):
        for n in range(6):
            lanes = slice(n * g.d, (n + 1) * g.d)
            out = mm(rows, s.ada_w[b, :, lanes])[0:1, :] + s.ada_b[b : b + 1, lanes]
            mod[b * 8 + n : b * 8 + n + 1, :] = out
        mod[b * 8 + 6 : b * 8 + 7, :] = act.astype(F32)
        mod[b * 8 + 7 : b * 8 + 8, :] = jnp.zeros((1, g.d), F32)


def place_tiles(g, s, lo, lines, dst):
    tc = s.meta[1]
    for k in range(g.n_tc):
        part = s.tiles[k][lo : lo + lines * g.tile, :].astype(F32)
        off = (tc ^ k) * g.tile
        for i in range(lines):
            dst[pl.ds(pl.multiple_of(i * g.pos + off, g.tile), g.tile), :] = part[i * g.tile : (i + 1) * g.tile, :]


def turn(g, ref, start, dst):
    block = ref[pl.ds(start, g.to), :].reshape(g.own, g.pos, g.d)
    dst[...] = jnp.swapaxes(block, 0, 1).reshape(g.to, g.d)


def part_of(g, ref, core):
    return ref[pl.ds(pl.multiple_of(core * (g.shift * g.own), g.own), g.win * g.own), :]


STACKED = names(lambda wq, wk, wv, wo, up, down: None)


FRONT_W = names(lambda cw, cb, wq, wk, wv, gw, gb: None)
TAIL_W = names(lambda wo, up, upb, down, downb: None)
SAVE = names(lambda x, mixed, q, k, v, gp, att, branch, resid, n2, hid, gel, mlp, prob, decay, pad: None)


def save_shapes(g):
    t, d, ff = g.t, g.d, g.ff
    return Table(
        x=((t, d), F32),
        mixed=((t, d), BF),
        q=((t, d), BF),
        k=((t, d), BF),
        v=((t, d), BF),
        gp=((t, 128), F32),
        att=((t, d), BF),
        branch=((t, d), BF),
        resid=((t, d), F32),
        n2=((t, d), BF),
        hid=((t, ff), BF),
        gel=((t, ff), BF),
        mlp=((t, d), BF),
        prob=((t, d), BF),
        decay=((t, d), BF),
        pad=((t + 2 * g.pos, d), BF),
        cum=(((t + 127) // 128 * 128, 128), F32),
    )


def back_shapes(g):
    t, d, ff = g.t, g.d, g.ff
    return Table(
        gmlp=((t, d), BF),
        gpre=((t, ff), BF),
        gres=((t, d), F32),
        tmp1=((t, d), F32),
        tmp2=((t, d), F32),
        gbr=((t, d), BF),
        dn=((ff, 128), F32),
        upg=((d, 512), F32),
        gatt=((t, d), BF),
        dlow=((t, d), BF),
        wlow=((t, d), BF),
        ulow=((t, d), BF),
        gqkv=((t, 3 * d), BF),
        ggp=((t, 128), F32),
        gpad=((t + 2 * g.pos, d), F32),
    )


def k_first(g, s):
    c = s.meta[0]
    x, mod, turned = s.x, s.mod, s.turned
    place_tiles(g, s, 0, g.win, x)
    s.cum[g.t :, :] = jnp.zeros((s.cum.shape[0] - g.t, 128), F32)
    front(g, x, mod, 0, s, s)
    attend(g, s)

    def emit(i, value):
        s.mid[i * g.big : (i + 1) * g.big, :] = value

    tail(g, x, mod, 0, s, s, emit)
    turn(g, s.mid, pl.multiple_of(c * (HALO * g.pos), g.pos), turned)
    s.keep_mid[...] = part_of(g, turned, c)
    s.send[...] = part_of(g, turned, 1 - c).astype(BF)


def weave(g, c, keep, recv, dst):
    for i in range(g.win):
        rows = slice(i * g.own, (i + 1) * g.own)
        a = pl.multiple_of(i * g.pos + c * g.own, g.own)
        b = pl.multiple_of(i * g.pos + (1 - c) * g.own, g.own)
        dst[pl.ds(a, g.own), :] = keep[rows, :].astype(F32)
        dst[pl.ds(b, g.own), :] = recv[rows, :].astype(F32)


def k_second(g, s):
    c, tc = s.meta[0], s.meta[1]
    x, mod, turned = s.x, s.mod, s.turned
    weave(g, c, s.keep_mid, s.recv, x)
    s.cum[g.t :, :] = jnp.zeros((s.cum.shape[0] - g.t, 128), F32)
    front(g, x, mod, 8, s, s)
    attend(g, s)

    def emit(i, value):
        s.three[i * g.big : (i + 1) * g.big, :] = value

    tail(g, x, mod, 8, s, s, emit)
    turn(g, s.three, pl.multiple_of(c * (HALO * g.pos), g.pos), turned)
    at = (tc * g.tile) % g.own
    for r in range(g.own):
        rows = slice(r * g.tile, (r + 1) * g.tile)
        mine = pl.multiple_of((c * g.own + r) * g.own + at, g.tile)
        theirs = pl.multiple_of(((1 - c) * g.own + r) * g.own + at, g.tile)
        s.tile_keep[rows, :] = turned[pl.ds(mine, g.tile), :]
        s.tile_send[rows, :] = turned[pl.ds(theirs, g.tile), :]


def k_ffn_back(g, base, s):
    c, tc = s.meta[0], s.meta[1]
    if base == 0:
        weave(g, c, s.g_keep, s.g_recv, s.gout)
    else:
        rows = g.own * g.n_tr
        size = rows * g.tile
        for k in range(g.n_tc):
            src = s.near if k < g.n_tc // 2 else s.far
            at = k % (g.n_tc // 2) * size
            block = src[at : at + size, :].astype(F32).reshape(rows, g.tile, g.d)
            to = pl.ds(pl.multiple_of((tc ^ k) * size, size), size)
            s.columns[to, :] = jnp.swapaxes(block, 0, 1).reshape(size, g.d)
        s.gout[...] = s.columns[pl.ds(pl.multiple_of(c * (g.shift * rows), rows), g.t), :]
    s.small[...] = jnp.zeros((SMALL, g.d), F32)
    ffn_back(g, c, tc, s.gout, s.mod, base, s, s, s)


def k_core(g, base, s):
    c, tc = s.meta[0], s.meta[1]
    s.small[...] = s.small_in[...]
    attn_core(g, s, s)
    proj_grads(g, c, tc, s, s, 0)


def k_conv(g, base, s):
    c, tc = s.meta[0], s.meta[1]
    mixed_back(g, base // 8, s, s)
    s.small[...] = s.small_in[...]

    def emit(i, value):
        s.gin[i * g.ch : (i + 1) * g.ch, :] = value

    conv_back(g, c, s.x, s.mod, base, s, s, s, emit)
    kernel_grads(g, c, s.mod, s, s)
    turned = s.turned
    turn(g, s.gin, pl.multiple_of(c * (HALO * g.pos), g.pos), turned)
    if base:
        s.g_keep[...] = part_of(g, turned, c)
        s.g_send[...] = part_of(g, turned, 1 - c).astype(BF)
        return
    size = g.tile * g.own
    block = turned[pl.ds(pl.multiple_of(tc * size, size), size), :]
    s.tile[...] = jnp.swapaxes(block.reshape(g.tile, g.own, g.d), 0, 1).reshape(size, g.d)


def both_cores(s):
    both = s.small[...] + s.small_recv[...]
    return jnp.where(iota(both.shape, 0) == 6, s.small[...], both)


def side_by_side(g, part):
    half = g.rp // 2
    return jnp.concatenate([part[0:half, 0:192], part[half:, 0:192]], axis=1)


def k_join(g, size, small_too, s):
    bit = s.meta[2] % 2
    half = g.rp // 2
    s.sum_a[...] = s.keep_a[...] + s.recv_a[...].astype(F32)
    if size == g.rab:
        s.sum_b[...] = s.keep_b[...] + s.recv_b[...].astype(F32)
    if small_too:
        small = both_cores(s)
        s.apart[...], s.summed[...] = small[0:8, :], small[8:SMALL, :]
        end = (g.n_dp // 2) * size
        s.send[end : end + 24, :] = small[8:SMALL, :].astype(BF)
        s.send[end + 24 : end + 32, :] = small[0:8, :].astype(BF)
    for m in range(g.n_dp // 2):
        for which, dst in ((bit, s.held), (1 - bit, s.send)):
            rows = pl.ds(pl.multiple_of((2 * m + which) * g.rp, g.rp), g.rp)
            dst[m * size : m * size + g.rp, :] = s.sum_a[rows, :].astype(dst.dtype)
            if size == g.rab:
                packed = side_by_side(g, s.sum_b[rows, :])
                rest = size - g.rp - half
                if rest:
                    packed = jnp.concatenate([packed, jnp.zeros((rest, g.d), F32)], axis=0)
                dst[m * size + g.rp : (m + 1) * size, :] = packed.astype(dst.dtype)


def k_step(g, step, size, small_too, s):
    parts = g.n_dp >> (step + 1)
    s.total[...] = s.got[...] + s.recv[0 : parts * size, :].astype(F32)
    blocks = 8 << step
    end = parts * size
    if small_too:
        summed = s.was_summed[...] + s.recv[end : end + 24, :].astype(F32)
        s.summed[...] = summed
        s.apart[0:blocks, :] = s.was_apart[...]
        s.apart[blocks : 2 * blocks, :] = s.recv[end + 24 : end + 24 + blocks, :].astype(F32)
    if parts == 1:
        return
    bit = (s.meta[2] // (2 << step)) % 2
    for m in range(parts // 2):
        for which, dst in ((bit, s.held), (1 - bit, s.send)):
            rows = pl.ds(pl.multiple_of((2 * m + which) * size, size), size)
            dst[m * size : (m + 1) * size, :] = s.total[rows, :].astype(dst.dtype)
    if small_too:
        end = (parts // 2) * size
        s.send[end : end + 24, :] = summed.astype(BF)
        s.send[end + 24 : end + 24 + 2 * blocks, :] = s.apart[...].astype(BF)


def k_last(g, s):
    me = s.meta[2]
    s.sum_b[...] = s.keep_b[...] + s.recv_b[...].astype(F32)
    small = both_cores(s)
    for k in range(g.n_dp):
        rows = pl.ds(pl.multiple_of((me ^ k) * g.rp, g.rp), g.rp)
        out = s.parts[k]
        out[0:SMALL, :] = small.astype(out.dtype)
        out[SMALL:, :] = side_by_side(g, s.sum_b[rows, :]).astype(out.dtype)


def finish(g, b, s, ab, proj, summed, apart):
    c, tc, me = s.meta[0], s.meta[1], s.meta[2]
    idx = c * g.n_tc + tc
    rp, rows, half = g.rp, g.rows, g.rp // 2
    acc, acct = s.acc, s.acct
    s.up_weight[b] = ab[0:rows, 0 : g.upc]
    acc[0:rp, 0:384] = ab
    acc[0:half, 384:576] = proj[:, 0:192]
    acc[half:rp, 384:576] = proj[:, 192:384]
    for n in range(1, 5):
        acct[n * 128 : (n + 1) * 128, :] = acc[:, n * 128 : (n + 1) * 128].T
    for j in range(g.ff // g.d):
        at = 192 + g.cols * j
        s.down_weight[b, :, j * rows : (j + 1) * rows] = acct[at : at + g.cols, 0:rows]
    for j, ref in enumerate((s.query, s.key, s.value, s.proj)):
        at = 384 + g.cols * j
        ref[b] = acct[at : at + g.cols, 0:rows]
    for a in range(3):
        for e in range(3):
            at = 3 * a + e if b == 0 else 3 * e + a
            s.conv_weight[a, e, b : b + 1, :] = summed[at : at + 1, :]
    s.conv_bias[b : b + 1, :] = summed[9:10, :]
    for m in range(g.ff // g.d):
        s.up_bias[b : b + 1, m * g.d : (m + 1) * g.d] = summed[10 + m : 11 + m, :]
    s.down_bias[b : b + 1, :] = summed[14:15, :]
    for h in range(6):
        s.gate_weight[h, b : b + 1, :] = summed[15 + h : 16 + h, :]
    s.row[...] = jnp.broadcast_to(summed[21:22, :], (8, g.d))
    s.gate_bias[b : b + 1, :] = s.row[0:1, 0:6]
    width = 6 * g.d // (g.n_tr * g.n_tc)
    wide = 384
    prod = jnp.zeros((g.d, wide), F32)
    total = apart[0]
    for part in apart[1:]:
        total = total + part
    for m in range(6):
        s.ada_bias[b : b + 1, m * g.d : (m + 1) * g.d] = total[m : m + 1, :]
    for part in apart:
        flat = jnp.concatenate([part[m : m + 1, :] for m in range(6)], axis=1)
        s.gms[...] = jnp.broadcast_to(flat, (8, 6 * g.d))
        full = pltpu.roll(s.gms[...], 6 * g.d - idx * width, 1)
        cond = jnp.broadcast_to(part[6:7, :], (8, g.d)).T
        prod = prod + cond[:, 0:1] * full[0:1, 0:wide]
    prod = pltpu.roll(prod, g.d - me * rows, 0)
    s.ada_weight[b] = prod[0:rows, 0:width]


FINAL = names(
    lambda ada_weight, ada_bias, conv_weight, conv_bias, query, key, value, proj, gate_weight, gate_bias,
    up_weight, up_bias, down_weight, down_bias: None
)
BY_ROW = names(lambda ada_bias, conv_bias, gate_bias, up_bias, down_bias: None)
INNER = names(lambda conv_weight, gate_weight: None)


def k_final_one(g, s):
    c, tc = s.meta[0], s.meta[1]
    near = (tc * g.tile) // g.own == c

    @pl.when(near)
    def _():
        s.out[0] = s.tile_keep[...].reshape(g.own, g.tile, g.d)

    @pl.when(jnp.logical_not(near))
    def _():
        s.out[0] = s.tile_recv[...].reshape(g.own, g.tile, g.d)

    s.grad[0] = s.tile[...].reshape(g.own, g.tile, g.d)
    half = g.rp // 2
    total = s.got[...]
    apart = [s.apart[8 * n : 8 * n + 8, :] for n in range(g.n_dp)]
    finish(g, 1, s, total[0 : g.rp, :], total[g.rp : g.rp + half, :], s.summed[...], apart)


def k_final(g, s):
    for name in FINAL:
        src, dst = s.first[name], s[name]
        if name in BY_ROW:
            dst[1:2, :] = src[1:2, :]
        elif name in INNER:
            lead = (slice(None),) * (len(dst.shape) - 2)
            dst[lead + (slice(1, 2),)] = src[lead + (slice(1, 2),)]
        else:
            dst[1] = src[1]
    ab = s.got[...]
    proj = s.parts[0][SMALL:, :]
    summed = s.parts[0][8:SMALL, :]
    apart = []
    for k, part in enumerate(s.parts):
        wide = part[...].astype(F32)
        apart.append(wide[0:8, :])
        if k:
            summed = summed + wide[8:SMALL, :]
            proj = proj + wide[SMALL:, :]
    finish(g, 0, s, ab, proj, summed, apart)


def padded_bytes(shape, dtype):
    shape = (1,) * (2 - len(shape)) + tuple(shape)
    rows, lanes = -(-shape[-2] // 16) * 16, -(-shape[-1] // 128) * 128
    return math.prod(shape[:-2]) * rows * lanes * jnp.dtype(dtype).itemsize


def call(us, kernel, ins, outs, scratch=(), weights=(), block=0, spare=VMEM_SPARE):
    ins = Table(ins, **dict(weights))
    ins, outs, scratch = dict(ins), dict(outs), dict(scratch)
    flat, tree = jax.tree.flatten(ins)
    spread_outs = [o if isinstance(o, list) else [o] for o in outs.values()]
    flat_outs = [o for group in spread_outs for o in group]
    meta = ins.get("meta")

    def run(*refs):
        refs = list(refs)

        def take(n):
            got = refs[:n]
            del refs[:n]
            return got

        table = Table(jax.tree.unflatten(tree, take(len(flat))))
        for name, ref in table.items():
            if name in STACKED:
                table[name] = ref.at[block]
        for name, o in outs.items():
            table[name] = take(len(o)) if isinstance(o, list) else take(1)[0]
        table.update(zip(scratch, refs))
        kernel(table)

    held = [(a.shape, a.dtype) for a in flat] + flat_outs + list(scratch.values())
    need = sum(padded_bytes(*h) for h in held)
    results = pl.pallas_call(
        run,
        in_specs=[pl.BlockSpec(memory_space=pltpu.SMEM if a is meta else pltpu.VMEM) for a in flat],
        out_specs=[pl.BlockSpec(memory_space=pltpu.VMEM)] * len(flat_outs),
        out_shape=[jax.ShapeDtypeStruct(*o) for o in flat_outs],
        scratch_shapes=[pltpu.VMEM(*sc) for sc in scratch.values()],
        compiler_params=pltpu.CompilerParams(vmem_limit_bytes=need + need // 16 + spare),
        cost_estimate=pl.CostEstimate(flops=int(us * 1e9), bytes_accessed=int(us * 3e6), transcendentals=0),
    )(*flat)
    results = list(results)
    found = Table()
    for name, o in outs.items():
        if isinstance(o, list):
            found[name] = results[: len(o)]
            del results[: len(o)]
        else:
            found[name] = results.pop(0)
    return found


def body(
    g,
    tokens,
    condition,
    cotangent,
    ada_weight,
    ada_bias,
    conv_weight,
    conv_bias,
    query_weight,
    key_weight,
    value_weight,
    out_weight,
    gate_weight,
    gate_bias,
    up_weight,
    up_bias,
    down_weight,
    down_bias,
):
    d, ff, t = g.d, g.ff, g.t
    meta = jnp.stack(
        [lax.axis_index("tr"), lax.axis_index("tc"), lax.axis_index("dp"), jnp.int32(0)]
    ).astype(jnp.int32)

    def xor(axis, k):
        return [(i, i ^ k) for i in range(lax.axis_size(axis))]

    def other(array):
        return lax.ppermute(array, "tr", [(0, 1), (1, 0)])

    part = functools.partial
    tile, half, deep = g.own * g.tile, g.win * g.own, g.n_dp * g.rp
    shapes, backs = save_shapes(g), back_shapes(g)
    weights = Table(
        wq=query_weight,
        wk=key_weight,
        wv=value_weight,
        wo=out_weight,
        gw=jnp.transpose(gate_weight, (2, 0, 1)),
        gb=gate_bias,
        cw=jnp.transpose(conv_weight, (1, 2, 0, 3)),
        cb=conv_bias,
        up=up_weight,
        upb=up_bias,
        down=down_weight,
        downb=down_bias,
    )

    def pick(table, names):
        return {n: table[n] for n in names}

    r = call(
        1,
        part(k_prep, g),
        Table(meta=meta, tok=tokens),
        Table(tokb=((tile, d), BF), halo=((HALO * g.tile, d), BF)),
    )
    halo = other(r.halo)
    cot = call(1, part(k_cast, g), Table(cot=cotangent), Table(low=((tile, d), BF))).low
    cot_recv = other(cot)
    ext = call(
        1,
        part(k_extend, g),
        Table(meta=meta, tokb=r.tokb, halo=halo),
        Table(ext=((half // 2, d), BF)),
    ).ext
    cot = call(
        1,
        part(k_rows, g),
        Table(meta=meta, mine=cot, theirs=cot_recv),
        Table(both=((2 * tile, d), BF)),
    ).both
    ext, condition = lax.optimization_barrier((ext, condition))
    tiles = [ext] + [lax.ppermute(ext, "tc", xor("tc", k)) for k in range(1, g.n_tc)]

    def double(array, step):
        got = lax.ppermute(array, "tc", xor("tc", 1 << step))
        shape = (2 * array.shape[0], d)
        return array, got, lambda: call(1, k_stack, Table(mine=array, theirs=got), Table(both=(shape, BF))).both

    ext_done, cot = lax.optimization_barrier((ext, cot))
    stack = double(cot, 0)[2]
    mod = call(
        1,
        part(k_modulate, g),
        Table(cond=condition, ada_w=ada_weight, ada_b=ada_bias),
        Table(mod=((16, d), F32)),
    ).mod
    base_ins = Table(meta=meta, mod=mod)
    save0 = call(
        8,
        part(k_first, g),
        Table(**base_ins, tiles=tiles),
        Table(
            keep_mid=((half, d), F32),
            send=((half, d), BF),
            **pick(shapes, SAVE),
        ),
        Table(mid=((t, d), F32), turned=((g.to, d), F32), cum=shapes.cum),
        pick(weights, FRONT_W + TAIL_W),
        0,
    )
    cot, _ = lax.optimization_barrier((stack(), save0.send))
    near, far, _ = double(cot, 1)
    save1 = call(
        8,
        part(k_second, g),
        Table(**base_ins, keep_mid=save0.keep_mid, recv=other(save0.send)),
        Table(
            tile_keep=((tile, d), F32),
            tile_send=((tile, d), F32),
            **pick(shapes, SAVE),
        ),
        Table(three=((t, d), F32), turned=((g.to, d), F32), cum=shapes.cum),
        pick(weights, FRONT_W + TAIL_W),
        1,
    )
    tile_recv = other(save1.tile_send)

    def ffn(b, save, ins):
        return call(
            4,
            part(k_ffn_back, g, 8 * b),
            Table(**base_ins, **ins, **pick(save, names(lambda gel, resid, branch, mlp, n2, hid: None))),
            Table(
                gres=backs.gres,
                gbr=backs.gbr,
                keep=((deep, d), F32),
                send=((deep, d), BF),
                small=((SMALL, d), F32),
            ),
            Table(**pick(backs, names(lambda gmlp, gpre, tmp1, tmp2, dn, upg: None)), gout=((t, d), F32), **(Table(columns=((g.n_tc * 2 * tile, d), F32)) if b else Table())),
            pick(weights, names(lambda down, up: None)),
            b,
        )

    def core(b, save, f):
        return call(
            4,
            part(k_core, g, 8 * b),
            Table(
                **base_ins,
                gbr=f.gbr,
                small_in=f.small,
                **pick(save, names(lambda q, k, v, gp, prob, decay, mixed, att: None)),
            ),
            Table(
                **pick(backs, names(lambda gqkv, ggp: None)),
                keep=((deep, 256), F32),
                send=((deep, 256), BF),
                small=((SMALL, d), F32),
            ),
            pick(backs, names(lambda gatt, dlow, wlow, ulow: None)),
            pick(weights, names(lambda wo: None)),
            b,
        )

    def conv(b, save, f, e):
        ends = Table(g_keep=((half, d), F32), g_send=((half, d), BF)) if b else Table(tile=((tile, d), F32))
        return call(
            4,
            part(k_conv, g, 8 * b),
            Table(
                **base_ins,
                gres=f.gres,
                small_in=e.small,
                **pick(e, names(lambda gqkv, ggp: None)),
                **pick(save, names(lambda x, pad: None)),
            ),
            Table(**ends, small=((SMALL, d), F32)),
            Table(
                **pick(backs, names(lambda tmp1, tmp2, gpad: None)),
                gin=((t, d), F32),
                turned=((g.to, d), F32),
            ),
            pick(weights, names(lambda wq, wk, wv, gw, cw: None)),
            b,
        )

    def projections(e):
        return Table(keep_b=e.keep, recv_b=other(e.send))

    def smalls(h):
        return Table(small=h.small, small_recv=other(h.small))

    def join(f, e, h):
        size, end = g.rab if e else g.rp, 32 if h else 0
        ins = Table(meta=meta, keep_a=f.keep, recv_a=f.recv)
        outs = Table(held=((g.n_dp // 2 * size, d), F32), send=((g.n_dp // 2 * size + end, d), BF))
        scratch = Table(sum_a=((deep, d), F32))
        if e:
            ins.update(e)
            scratch = Table(scratch, sum_b=((deep, 256), F32))
        if h:
            ins.update(h)
            outs = Table(outs, apart=((8, d), F32), summed=((24, d), F32))
        found = call(1, part(k_join, g, size, h is not None), ins, outs, scratch)
        return Table(found, size=size)

    def hop(state, step):
        return Table(state, recv=lax.ppermute(state.send, "dp", xor("dp", 1 << step)))

    def take(state, step):
        size, parts = state.size, g.n_dp >> (step + 1)
        small_too = state.get(*names(lambda apart: None)) is not None
        blocks = 16 << step
        end = -(-(24 + blocks) // 16) * 16 if small_too else 0
        outs, scratch = Table(), Table()
        total = ((parts * size, d), F32)
        if parts > 1:
            outs = Table(held=((parts // 2 * size, d), F32), send=((parts // 2 * size + end, d), BF))
            scratch = Table(total=total)
        else:
            outs = Table(total=total)
        ins = Table(meta=meta, got=state.held, recv=state.recv)
        if small_too:
            ins = Table(ins, was_apart=state.apart, was_summed=state.summed)
            outs = Table(outs, apart=((blocks, d), F32), summed=((24, d), F32))
        return Table(call(1, part(k_step, g, step, size, small_too), ins, outs, scratch), size=size)

    def spread(parts):
        return [parts[0]] + [lax.ppermute(parts[k], "dp", xor("dp", k)) for k in range(1, g.n_dp)]

    def before(table, *later):
        flat, tree = jax.tree.flatten((dict(table), later))
        return Table(jax.tree.unflatten(tree, lax.optimization_barrier(flat))[0])

    f1 = ffn(1, save1, Table(near=near, far=far))
    f1 = Table(f1, recv=other(f1.send))
    e1 = core(1, save1, f1)
    e1b = projections(e1)
    h1 = conv(1, save1, f1, e1)
    g_recv = other(h1.g_send)
    h1s = smalls(h1)
    one = join(f1, e1b, None)
    h1 = before(h1, one.send)
    one = hop(one, 0)
    f0 = ffn(0, save0, Table(g_keep=h1.g_keep, g_recv=g_recv))
    f0 = Table(f0, recv=other(f0.send))
    one = take(one, 0)
    two = join(f0, None, h1s)
    f0b = before(f0, one.get(*names(lambda send: None)), two.send)
    if g.steps > 1:
        one = hop(one, 1)
    two = hop(two, 0)
    e0 = core(0, save0, f0b)
    e0b = projections(e0)
    two = take(two, 0)
    e0 = before(e0, two.get(*names(lambda send: None)))
    if g.steps > 1:
        two = hop(two, 1)
    h0 = conv(0, save0, f0, e0)
    for step in range(1, g.steps):
        one, two = take(one, step), take(two, step)
        if step + 1 < g.steps:
            one, two = hop(one, step + 1), hop(two, step + 1)
    parts0 = spread(
        call(
            1,
            part(k_last, g),
            Table(meta=meta, **e0b, **smalls(h0)),
            Table(parts=[((SMALL + g.rp // 2, d), BF if k else F32) for k in range(g.n_dp)]),
            Table(sum_b=((deep, 256), F32)),
        ).parts
    )
    n_cols = g.n_tr * g.n_tc
    shards = ((2, g.cols, g.rows), F32)
    final_shapes = dict(
        zip(
            FINAL,
            (
                ((2, g.rows, 6 * d // n_cols), F32),
                ((2, 6 * d), F32),
                ((3, 3, 2, d), F32),
                ((2, d), F32),
                shards,
                shards,
                shards,
                shards,
                ((6, 2, d), F32),
                ((2, 6), F32),
                ((2, g.rows, g.upc), F32),
                ((2, ff), F32),
                ((2, g.cols, ff // g.n_dp), F32),
                ((2, d), F32),
            ),
        )
    )
    scratch = Table(acc=((128, 640), F32), acct=((640, 128), F32), row=((8, d), F32), gms=((8, 6 * d), F32))
    first = call(
        3,
        part(k_final_one, g),
        Table(
            meta=meta,
            tile_keep=save1.tile_keep,
            tile_recv=tile_recv,
            tile=h0.tile,
            got=one.total,
            apart=two.apart,
            summed=two.summed,
        ),
        Table(final_shapes, out=(tokens.shape, F32), grad=(tokens.shape, F32)),
        scratch,
        spare=6 * VMEM_SPARE,
    )
    output = first.out
    finals = call(
        3,
        part(k_final, g),
        Table(
            meta=meta,
            got=two.total,
            parts=parts0,
            first={n: first[n] for n in FINAL},
        ),
        final_shapes,
        scratch,
        spare=6 * VMEM_SPARE,
    )
    finals = [finals[n] for n in FINAL]
    finals[2] = jnp.transpose(finals[2], (2, 0, 1, 3))
    finals[8] = jnp.transpose(finals[8], (1, 2, 0))
    for n in (4, 5, 6, 7, 12):
        finals[n] = jnp.swapaxes(finals[n], 1, 2)
    return (output, first.grad) + tuple(finals)


def solution(mesh):
    everywhere = P()
    tiles = P("dp", "tr", "tc", None)
    cut = P(None, "dp", ("tr", "tc"))
    in_specs = (tiles, P("dp", None), tiles) + (everywhere,) * 14
    out_specs = (tiles, tiles, cut, P(), P(), P(), cut, cut, cut, cut, P(), P(), cut, P(), cut, P())

    def program(*arrays):
        g = Geo(mesh, arrays[0].shape, arrays[13].shape)
        run = functools.partial(body, g)
        return jax.shard_map(run, mesh=mesh, in_specs=in_specs, out_specs=out_specs, check_vma=False)(*arrays)

    return program
```

```python
import functools
import inspect
import math

import jax
import jax.numpy as jnp
from jax import lax
from jax.experimental import pallas as pl
from jax.experimental.pallas import tpu as pltpu
from jax.sharding import PartitionSpec as P

BF = jnp.bfloat16
F32 = jnp.float32
EPS = 1e-06
GATE_NORM = 16.0
HALO = 2
GELU_A = 0.7978845608028654
GELU_B = 0.044715
NEG = -1e30
VMEM_SPARE = 3 * 1024 * 1024
SMALL = 32


def mm(a, b):
    return jnp.dot(a, b, preferred_element_type=F32)


def mm_rt(a, b):
    return lax.dot_general(a, b, (((1,), (1,)), ((), ())), preferred_element_type=F32)


def mm_lt(a, b):
    return lax.dot_general(a, b, (((0,), (0,)), ((), ())), preferred_element_type=F32)


def hi_lo(x):
    hi = x.astype(BF)
    return hi, (x - hi.astype(F32)).astype(BF)


def normalize(x):
    center = x - jnp.mean(x, axis=-1, keepdims=True)
    rstd = lax.rsqrt(jnp.mean(center * center, axis=-1, keepdims=True) + EPS)
    return center * rstd, rstd


def normalize_back(g_y, y, rstd):
    return rstd * (
        g_y - jnp.mean(g_y, axis=-1, keepdims=True) - y * jnp.mean(g_y * y, axis=-1, keepdims=True)
    )


def iota(shape, dim):
    return lax.broadcasted_iota(jnp.int32, shape, dim)


def names(function):
    return tuple(inspect.signature(function).parameters)


class Table(dict):
    __getattr__ = dict.__getitem__


class Geo:
    def __init__(self, mesh, tokens, up):
        self.n_dp, self.n_tr, self.n_tc = (mesh.shape[a] for a in ("dp", "tr", "tc"))
        self.images, self.own, self.tile = (tokens[0] // self.n_dp, tokens[1] // self.n_tr, tokens[2] // self.n_tc)
        self.pos = tokens[2]
        self.d = tokens[3]
        self.ff = up[2]
        self.win = self.own + HALO
        self.t = self.win * self.pos
        self.to = self.own * self.pos
        self.lt = self.d // 128
        self.pairs = self.d // 128
        self.group = 64
        self.groups = self.t // self.group
        self.ch = 3 * self.pos
        self.chunks = self.t // self.ch
        self.big = 192
        self.bigs = self.t // self.big
        self.fc = 512
        self.fcs = self.ff // self.fc
        self.shift = self.pos - self.win
        self.rows = self.d // self.n_dp
        self.rp = -(-self.rows // 16) * 16
        self.rab = -(-(self.rp + self.rp // 2) // 16) * 16
        self.steps = self.n_dp.bit_length() - 1
        self.cols = self.d // (self.n_tr * self.n_tc)
        self.upc = self.ff // (self.n_tr * self.n_tc)


def kernel_taps(w, blk):
    at = slice(blk, blk + 1)
    return [[w.cw[a, b, at, :] if blk == 0 else w.cw[b, a, at, :] for b in range(3)] for a in range(3)]


def gate_rows(g, w, blk):
    heads = w.gw.shape[0]
    rows = [w.gw[h, blk : blk + 1, :] for h in range(heads)]
    return hi_lo(jnp.concatenate(rows + [jnp.zeros((128 - heads, g.d), F32)], axis=0))


def front(g, x, mod, base, w, s):
    d, pos, ch = g.d, g.pos, g.ch
    shift, scale = mod[base : base + 1, :], 1.0 + mod[base + 1 : base + 2, :]
    zero = jnp.zeros((pos, d), BF)
    s.pad[0:pos, :] = zero
    s.pad[g.t + pos : g.t + 2 * pos, :] = zero
    for i in range(g.chunks):
        rows = slice(i * ch, (i + 1) * ch)
        y, _ = normalize(x[rows, :])
        s.pad[pos + i * ch : pos + (i + 1) * ch, :] = (y * scale + shift).astype(BF)
    at = iota((ch, 1), 0) % pos
    first, last = at == 0, at == pos - 1
    taps = kernel_taps(w, base // 8)
    blk = base // 8
    bias = w.cb[blk : blk + 1, :]
    for i in range(g.chunks):
        wide = s.pad[i * ch : i * ch + ch + 2 * pos, :].astype(F32)
        lines = [wide[a * pos : a * pos + ch, :] for a in range(3)]
        v = [sum(lines[a] * taps[a][b] for a in range(3)) for b in range(3)]
        mixed = v[1] + bias
        mixed = mixed + jnp.where(first, 0.0, pltpu.roll(v[0], 1, 0))
        mixed = mixed + jnp.where(last, 0.0, pltpu.roll(v[2], ch - 1, 0))
        s.mixed[i * ch : (i + 1) * ch, :] = mixed.astype(BF)
    for out, weight in ((s.q, w.wq), (s.k, w.wk), (s.v, w.wv)):
        out[...] = mm(s.mixed[...], weight[...]).astype(BF)
    g_hi, g_lo = gate_rows(g, w, blk)
    mixed = s.mixed[...]
    heads = w.gb.shape[1]
    bias = jnp.concatenate([w.gb[blk : blk + 1, :], jnp.zeros((1, 128 - heads), F32)], axis=1)
    pre = mm_rt(mixed, g_hi) + mm_rt(mixed, g_lo) + bias
    s.gp[...] = pre
    run = (jnp.minimum(pre, 0.0) - jnp.log1p(jnp.exp(-jnp.abs(pre)))) * (1.0 / GATE_NORM)
    at = iota((g.t, 1), 0) % pos
    step = 1
    while step < pos:
        run = run + jnp.where(at >= step, pltpu.roll(run, step, 0), 0.0)
        step *= 2
    s.cum[0 : g.t, :] = run


def decay_rows(g, s):
    lane = iota((1, 128), 1)
    found = {}
    for m in range((g.t + 127) // 128):
        full = s.cum[m * 128 : (m + 1) * 128, :].T
        for j in range(g.pairs):
            one, two = full[2 * j : 2 * j + 1, :], full[2 * j + 1 : 2 * j + 2, :]
            lo_row = jnp.where(lane < 64, one, pltpu.roll(two, 64, 1))
            hi_row = jnp.where(lane < 64, pltpu.roll(one, 64, 1), two)
            found[2 * m, j] = lo_row
            found[2 * m + 1, j] = hi_row
    return found


def pair_masks(g):
    row, lane = iota((64, 128), 0), iota((64, 128), 1)
    src = lane % 64
    same = (row // g.pos) == (src // g.pos)
    return lane < 64, same & (row >= src), same & (row > src)


def split_heads(block, low_half):
    zero = jnp.zeros_like(block)
    return jnp.concatenate([jnp.where(low_half, block, zero), jnp.where(low_half, zero, block)], axis=0)


def pair_blocks(g):
    for grp in range(g.groups):
        for j in range(g.pairs):
            yield grp, slice(grp * 64, grp * 64 + 64), j, slice(j * 128, j * 128 + 128)


def pair_decay(s, source, grp, j, low_half, causal):
    rows = slice(grp * 64, grp * 64 + 64)
    ct = jnp.where(low_half, s.cum[rows, 2 * j : 2 * j + 1], s.cum[rows, 2 * j + 1 : 2 * j + 2])
    return jnp.exp(jnp.where(causal, ct - source[grp, j], NEG)) * 0.125


def attend(g, s):
    low_half, causal, _ = pair_masks(g)
    source = decay_rows(g, s)
    for grp, rows, j, lanes in pair_blocks(g):
        scores = mm_rt(s.q[rows, lanes], split_heads(s.k[rows, lanes], low_half))
        decay = pair_decay(s, source, grp, j, low_half, causal)
        s.decay[rows, lanes] = decay.astype(BF)
        s.prob[rows, lanes] = (scores * decay).astype(BF)
    for _, rows, _, lanes in pair_blocks(g):
        s.att[rows, lanes] = mm(s.prob[rows, lanes], split_heads(s.v[rows, lanes], low_half)).astype(BF)


def tail(g, x, mod, base, w, s, emit):
    gate_one, gate_two = mod[base + 2 : base + 3, :], mod[base + 5 : base + 6, :]
    shift, scale = mod[base + 3 : base + 4, :], 1.0 + mod[base + 4 : base + 5, :]
    for i in range(g.bigs):
        rows = slice(i * g.big, (i + 1) * g.big)
        branch = mm(s.att[rows, :], w.wo[...])
        s.branch[rows, :] = branch.astype(BF)
        resid = x[rows, :] + gate_one * branch
        s.resid[rows, :] = resid
        y, _ = normalize(resid)
        s.n2[rows, :] = (y * scale + shift).astype(BF)
    for f in range(g.fcs):
        fl = slice(f * g.fc, (f + 1) * g.fc)
        for i in range(g.bigs):
            rows = slice(i * g.big, (i + 1) * g.big)
            pre = mm(s.n2[rows, :], w.up[:, fl]) + w.upb[base // 8 : base // 8 + 1, fl]
            sq = pre * pre
            half = 0.5 * jnp.tanh(pre * (GELU_A + (GELU_A * GELU_B) * sq)) + 0.5
            hid = pre * half
            s.hid[rows, fl] = hid.astype(BF)
            inner = 2.0 * GELU_A + (6.0 * GELU_A * GELU_B) * sq
            s.gel[rows, fl] = (half + hid * (1.0 - half) * inner).astype(s.gel.dtype)
    for i in range(g.bigs):
        rows = slice(i * g.big, (i + 1) * g.big)
        mlp = mm(s.hid[rows, :], w.down[...]) + w.downb[base // 8 : base // 8 + 1, :]
        s.mlp[rows, :] = mlp.astype(s.mlp.dtype)
        emit(i, s.resid[rows, :] + gate_two * mlp)


def select_cols(width, source, half, tc, c, n_tc, lanes):
    row, lane = iota((source, 2 * half), 0), iota((source, 2 * half), 1)
    core = jnp.where(lane < half, c, 1 - c)
    inside = lane % half - lanes
    want = (core * n_tc + tc) * width + inside
    hit = (row == want) & (inside >= 0) & (inside < width)
    return jnp.where(hit, 1.0, 0.0).astype(BF)


def own_sum(g, c, ref, lanes=None):
    start = pl.multiple_of(c * (HALO * g.pos), HALO * g.pos)
    if lanes is None:
        return ref[pl.ds(start, g.to), :]
    return ref[pl.ds(start, g.to), lanes]


def colsum(a):
    return jnp.sum(a.astype(F32), axis=0, keepdims=True)


def lay(g, dst, lane0, value):
    lanes = slice(lane0, lane0 + value.shape[1])
    if g.rp == g.rows:
        dst[:, lanes] = value.astype(dst.dtype)
        return
    for n in range(g.n_dp):
        part = value[n * g.rows : (n + 1) * g.rows, :]
        pad = jnp.zeros((g.rp - g.rows, value.shape[1]), F32)
        dst[n * g.rp : (n + 1) * g.rp, lanes] = jnp.concatenate([part, pad], axis=0).astype(dst.dtype)


def ffn_back(g, c, tc, g_out, mod, base, w, s, o):
    gate_one, gate_two = mod[base + 2 : base + 3, :], mod[base + 5 : base + 6, :]
    scale = 1.0 + mod[base + 4 : base + 5, :]
    for i in range(g.bigs):
        rows = slice(i * g.big, (i + 1) * g.big)
        s.gmlp[rows, :] = (gate_two * g_out[rows, :]).astype(BF)
    for f in range(g.fcs):
        fl = slice(f * g.fc, (f + 1) * g.fc)
        for i in range(g.bigs):
            rows = slice(i * g.big, (i + 1) * g.big)
            g_hid = mm_rt(s.gmlp[rows, :], w.down[fl, :])
            s.gpre[rows, fl] = (s.gel[rows, fl].astype(F32) * g_hid).astype(BF)
    for i in range(g.bigs):
        rows = slice(i * g.big, (i + 1) * g.big)
        g_n2 = mm_rt(s.gpre[rows, :], w.up[...])
        y, rstd = normalize(s.resid[rows, :])
        g_res = g_out[rows, :] + normalize_back(g_n2 * scale, y, rstd)
        s.gres[rows, :] = g_res
        s.tmp1[rows, :] = g_n2
        s.tmp2[rows, :] = g_n2 * y
        s.gbr[rows, :] = (gate_one * g_res).astype(BF)
    own = functools.partial(own_sum, g, c)
    small = o.small
    small[2:3, :] = colsum(own(s.gres) * own(s.branch).astype(F32))
    small[3:4, :] = colsum(own(s.tmp1))
    small[4:5, :] = colsum(own(s.tmp2))
    small[5:6, :] = colsum(own(g_out) * own(s.mlp).astype(F32))
    for f in range(g.ff // g.d):
        small[18 + f : 19 + f, :] = colsum(own(s.gpre, slice(f * g.d, (f + 1) * g.d)))
    small[22:23, :] = colsum(own(s.gmlp))
    n2 = own(s.n2)
    for at, core in ((0, c), (256, 1 - c)):
        first = (core * g.n_tc + tc) * g.upc
        lanes = pl.ds(pl.multiple_of(first // 128 * 128, 128), 256)
        grads = mm_lt(n2, own(s.gpre, lanes))
        s.upg[:, at : at + 256] = jnp.where(first % 128 == 0, grads, pltpu.roll(grads, 192, 1))
    sel = mm(own(s.gmlp), select_cols(g.cols, g.d, 64, tc, c, g.n_tc, 0)).astype(BF)
    s.dn[...] = mm_lt(own(s.hid), sel)
    lane = iota((g.rows, 128), 1)
    per = g.ff // g.d
    for dd in range(g.n_dp):
        up = slice(dd * g.rows, (dd + 1) * g.rows)
        down = [s.dn[(dd * per + j) * g.rows : (dd * per + j + 1) * g.rows, :] for j in range(per)]
        for at, shift, dst in ((0, 0, o.keep), (256, 64, o.send)):
            to = slice(dd * g.rp, dd * g.rp + g.rows)
            one, two, three, four = (
                pltpu.roll(part, (lanes - shift) % 128, 1) for part, lanes in zip(down, (64, 112, 32, 80))
            )
            mid = jnp.where(lane < 112, one, two)
            dst[to, 0:128] = s.upg[up, at : at + 128].astype(dst.dtype)
            dst[to, 128:256] = jnp.where(lane < 64, s.upg[up, at + 128 : at + 256], mid).astype(dst.dtype)
            end = jnp.where(lane < 80, three, four)
            dst[to, 256:384] = jnp.where(lane < 32, two, end).astype(dst.dtype)


def attn_core(g, w, s):
    low_half, causal, strict = pair_masks(g)
    s.gatt[...] = mm_rt(s.gbr[...], w.wo[...]).astype(BF)
    row, col = iota((64, 64), 0), iota((64, 64), 1)
    later = jnp.where((row // g.pos == col // g.pos) & (col >= row), 1.0, 0.0).astype(BF)
    head_of = iota((g.d, 128), 0) // 64
    to_head = jnp.where(head_of == iota((g.d, 128), 1), 1.0, 0.0).astype(BF)
    for _, rows, _, lanes in pair_blocks(g):
        d_p = mm_rt(s.gatt[rows, lanes], split_heads(s.v[rows, lanes], low_half))
        s.dlow[rows, lanes] = (d_p * s.decay[rows, lanes].astype(F32)).astype(BF)
        s.wlow[rows, lanes] = (d_p * s.prob[rows, lanes].astype(F32)).astype(BF)
    strict3 = jnp.concatenate([strict] * g.pairs, axis=1)
    for grp in range(g.groups):
        rows = slice(grp * 64, grp * 64 + 64)
        s.ulow[rows, :] = jnp.where(strict3, mm(later, s.wlow[rows, :]), 0.0).astype(BF)
    for _, rows, j, lanes in pair_blocks(g):
        km = split_heads(s.k[rows, lanes], low_half)
        s.gqkv[rows, j * 128 : j * 128 + 128] = mm(s.dlow[rows, lanes], km).astype(BF)
    for _, rows, j, lanes in pair_blocks(g):
        both = mm_lt(s.dlow[rows, lanes], s.q[rows, lanes])
        s.gqkv[rows, g.d + j * 128 : g.d + j * 128 + 128] = jnp.where(
            low_half, both[0:64, :], both[64:128, :]
        ).astype(BF)
    for _, rows, j, lanes in pair_blocks(g):
        both = mm_lt(s.prob[rows, lanes], s.gatt[rows, lanes])
        s.gqkv[rows, 2 * g.d + j * 128 : 2 * g.d + j * 128 + 128] = jnp.where(
            low_half, both[0:64, :], both[64:128, :]
        ).astype(BF)
    g_log = mm(s.ulow[...], to_head)
    s.ggp[...] = g_log * (jax.nn.sigmoid(-s.gp[...]) * (1.0 / GATE_NORM))


def proj_grads(g, c, tc, s, o, lane0):
    own = functools.partial(own_sum, g, c)
    small = o.small
    pick_cols = select_cols(g.cols, g.d, 64, tc, c, g.n_tc, 0)
    sel = [mm(own(s.gqkv, slice(n * g.d, (n + 1) * g.d)), pick_cols).astype(BF) for n in range(3)]
    sel_out = mm(own(s.gbr), pick_cols).astype(BF)
    grads = mm_lt(own(s.mixed), jnp.concatenate(sel, axis=1))
    three = mm_lt(own(s.att), sel_out)
    zero, one, two = (grads[:, n * 128 : (n + 1) * 128] for n in range(3))
    lane = iota((g.d, 128), 1)
    for shift, dst in ((0, o.keep), (64, o.send)):
        q, k, v, out = (
            pltpu.roll(part, (lanes - shift) % 128, 1)
            for part, lanes in ((zero, 0), (one, 48), (two, 96), (three, 16))
        )
        lay(g, dst, lane0, jnp.where(lane < 48, q, jnp.where(lane < 96, k, v)))
        lay(g, dst, lane0 + 128, jnp.where(lane < 16, v, out))
    gg = own(s.ggp)
    hi, lo = hi_lo(gg)
    mixed = own(s.mixed)
    gate = mm_lt(hi, mixed) + mm_lt(lo, mixed)
    small[23:29, :] = gate[0:6, :]
    small[29:30, 0:128] = colsum(gg)
    small[29:30, 128 : g.d] = jnp.zeros((1, g.d - 128), F32)


def mixed_back(g, blk, w, s):
    pos, d = g.pos, g.d
    w_hi, w_lo = gate_rows(g, w, blk)
    zero = jnp.zeros((pos, d), F32)
    s.gpad[0:pos, :] = zero
    s.gpad[g.t + pos : g.t + 2 * pos, :] = zero
    for i in range(g.bigs):
        rows = slice(i * g.big, (i + 1) * g.big)
        hi, lo = hi_lo(s.ggp[rows, :])
        total = mm(hi, w_hi) + mm(lo, w_hi) + mm(hi, w_lo)
        for n, weight in enumerate((w.wq, w.wk, w.wv)):
            total = total + mm_rt(s.gqkv[rows, n * d : (n + 1) * d], weight[...])
        s.gpad[pos + i * g.big : pos + (i + 1) * g.big, :] = total.astype(BF).astype(F32)


def conv_back(g, c, x, mod, base, w, s, o, emit):
    pos, ch, d = g.pos, g.ch, g.d
    own = functools.partial(own_sum, g, c)
    small = o.small
    at = iota((ch, 1), 0) % pos
    first, last = at == 0, at == pos - 1
    taps = kernel_taps(w, base // 8)
    scale = 1.0 + mod[base + 1 : base + 2, :]
    for i in range(g.chunks):
        rows = slice(i * ch, (i + 1) * ch)
        lines = [s.gpad[i * ch + a * pos : i * ch + a * pos + ch, :] for a in range(3)]
        v = [sum(lines[2 - a] * taps[a][b] for a in range(3)) for b in range(3)]
        g_n = v[1]
        g_n = g_n + jnp.where(last, 0.0, pltpu.roll(v[0], ch - 1, 0))
        g_n = g_n + jnp.where(first, 0.0, pltpu.roll(v[2], 1, 0))
        y, rstd = normalize(x[rows, :])
        s.tmp1[rows, :] = g_n
        s.tmp2[rows, :] = g_n * y
        emit(i, s.gres[rows, :] + normalize_back(g_n * scale, y, rstd))
    small[0:1, :] = colsum(own(s.tmp1))
    small[1:2, :] = colsum(own(s.tmp2))


def kernel_grads(g, c, mod, s, o):
    pos, d = g.pos, g.d
    small = o.small
    oc = 4 * pos
    at = iota((oc, 1), 0) % pos
    first, last = at == 0, at == pos - 1
    sums = [jnp.zeros((8, d), F32) for _ in range(10)]
    for i in range(g.to // oc):
        start = c * (HALO * pos) + i * oc
        mid = s.gpad[pl.ds(pl.multiple_of(start + pos, pos), oc), :]
        shifted = [
            jnp.where(last, 0.0, pltpu.roll(mid, oc - 1, 0)),
            mid,
            jnp.where(first, 0.0, pltpu.roll(mid, 1, 0)),
        ]
        for a in range(3):
            line = s.pad[pl.ds(pl.multiple_of(start + a * pos, pos), oc), :].astype(F32)
            for b in range(3):
                sums[3 * a + b] = sums[3 * a + b] + jnp.sum((line * shifted[b]).reshape(oc // 8, 8, d), axis=0)
        sums[9] = sums[9] + jnp.sum(mid.reshape(oc // 8, 8, d), axis=0)
    for n in range(10):
        small[8 + n : 9 + n, :] = jnp.sum(sums[n], axis=0, keepdims=True)
    small[6:7, :] = mod[6:7, :]
    small[7:8, :] = jnp.zeros((1, d), F32)
    small[30:SMALL, :] = jnp.zeros((SMALL - 30, d), F32)


def attn_back(g, c, tc, x, mod, base, w, s, o, lane0, emit):
    attn_core(g, w, s)
    proj_grads(g, c, tc, s, o, lane0)
    mixed_back(g, base // 8, w, s)
    conv_back(g, c, x, mod, base, w, s, o, emit)
    kernel_grads(g, c, mod, s, o)


def k_prep(g, s):
    c = s.meta[0]
    t = s.tok[0].reshape(g.own * g.tile, g.d).astype(BF)
    s.tokb[...] = t
    edge = HALO * g.tile

    @pl.when(c == 0)
    def _():
        s.halo[...] = t[g.own * g.tile - edge :, :]

    @pl.when(c == 1)
    def _():
        s.halo[...] = t[0:edge, :]


def k_cast(g, s):
    s.low[...] = s.cot[0].reshape(g.own * g.tile, g.d).astype(BF)


def k_rows(g, s):
    c, size = s.meta[0], g.own * g.tile
    s.both[pl.ds(pl.multiple_of(c * size, size), size), :] = s.mine[...]
    s.both[pl.ds(pl.multiple_of((1 - c) * size, size), size), :] = s.theirs[...]


def k_stack(s):
    rows = s.mine.shape[0]
    s.both[0:rows, :] = s.mine[...]
    s.both[rows:, :] = s.theirs[...]


def k_extend(g, s):
    c = s.meta[0]
    edge = HALO * g.tile
    own = g.own * g.tile
    s.ext[pl.ds(pl.multiple_of(c * edge, edge), own), :] = s.tokb[...]
    s.ext[pl.ds(pl.multiple_of((1 - c) * own, edge), edge), :] = s.halo[...]


def k_modulate(g, s):
    mod = s.mod
    act = jax.nn.silu(s.cond[...]).astype(BF)
    rows = jnp.broadcast_to(act, (16, g.d))
    for b in range(2):
        for n in range(6):
            lanes = slice(n * g.d, (n + 1) * g.d)
            out = mm(rows, s.ada_w[b, :, lanes])[0:1, :] + s.ada_b[b : b + 1, lanes]
            mod[b * 8 + n : b * 8 + n + 1, :] = out
        mod[b * 8 + 6 : b * 8 + 7, :] = act.astype(F32)
        mod[b * 8 + 7 : b * 8 + 8, :] = jnp.zeros((1, g.d), F32)


def place_tiles(g, s, lo, lines, dst):
    tc = s.meta[1]
    for k in range(g.n_tc):
        part = s.tiles[k][lo : lo + lines * g.tile, :].astype(F32)
        off = (tc ^ k) * g.tile
        for i in range(lines):
            dst[pl.ds(pl.multiple_of(i * g.pos + off, g.tile), g.tile), :] = part[i * g.tile : (i + 1) * g.tile, :]


def turn(g, ref, start, dst):
    block = ref[pl.ds(start, g.to), :].reshape(g.own, g.pos, g.d)
    dst[...] = jnp.swapaxes(block, 0, 1).reshape(g.to, g.d)


def part_of(g, ref, core):
    return ref[pl.ds(pl.multiple_of(core * (g.shift * g.own), g.own), g.win * g.own), :]


STACKED = names(lambda wq, wk, wv, wo, up, down: None)


class Refs:
    def __init__(self, table, block, sources, buffers, sems):
        self.__dict__.update(table)
        self.buffers, self.copies = buffers, {}
        for n, (name, src) in enumerate(sources.items()):
            src = src.at[block] if name in STACKED else src
            self.copies[name] = pltpu.make_async_copy(src, buffers[name], sems.at[n])
            self.copies[name].start()

    def __getattr__(self, name):
        copy = self.copies.pop(name, None)
        if copy is not None:
            copy.wait()
        return self.buffers[name]

    def __getitem__(self, name):
        return getattr(self, name)

    def finish(self):
        for name in list(self.copies):
            getattr(self, name)


FRONT_W = names(lambda cw, cb, wq, wk, wv, gw, gb: None)
TAIL_W = names(lambda wo, up, upb, down, downb: None)
SAVE = names(lambda x, mixed, q, k, v, gp, att, branch, resid, n2, hid, gel, mlp, prob, decay, pad: None)


def save_shapes(g):
    t, d, ff = g.t, g.d, g.ff
    return Table(
        x=((t, d), F32),
        mixed=((t, d), BF),
        q=((t, d), BF),
        k=((t, d), BF),
        v=((t, d), BF),
        gp=((t, 128), F32),
        att=((t, d), BF),
        branch=((t, d), BF),
        resid=((t, d), F32),
        n2=((t, d), BF),
        hid=((t, ff), BF),
        gel=((t, ff), BF),
        mlp=((t, d), BF),
        prob=((t, d), BF),
        decay=((t, d), BF),
        pad=((t + 2 * g.pos, d), BF),
        cum=(((t + 127) // 128 * 128, 128), F32),
    )


def back_shapes(g):
    t, d, ff = g.t, g.d, g.ff
    return Table(
        gmlp=((t, d), BF),
        gpre=((t, ff), BF),
        gres=((t, d), F32),
        tmp1=((t, d), F32),
        tmp2=((t, d), F32),
        gbr=((t, d), BF),
        dn=((ff, 128), F32),
        upg=((d, 512), F32),
        gatt=((t, d), BF),
        dlow=((t, d), BF),
        wlow=((t, d), BF),
        ulow=((t, d), BF),
        gqkv=((t, 3 * d), BF),
        ggp=((t, 128), F32),
        gpad=((t + 2 * g.pos, d), F32),
    )


def k_first(g, s):
    c = s.meta[0]
    x, mod, turned = s.x, s.mod, s.turned
    place_tiles(g, s, 0, g.win, x)
    s.cum[g.t :, :] = jnp.zeros((s.cum.shape[0] - g.t, 128), F32)
    front(g, x, mod, 0, s, s)
    attend(g, s)

    def emit(i, value):
        s.mid[i * g.big : (i + 1) * g.big, :] = value

    tail(g, x, mod, 0, s, s, emit)
    turn(g, s.mid, pl.multiple_of(c * (HALO * g.pos), g.pos), turned)
    s.keep_mid[...] = part_of(g, turned, c)
    s.send[...] = part_of(g, turned, 1 - c).astype(BF)


def weave(g, c, keep, recv, dst):
    for i in range(g.win):
        rows = slice(i * g.own, (i + 1) * g.own)
        a = pl.multiple_of(i * g.pos + c * g.own, g.own)
        b = pl.multiple_of(i * g.pos + (1 - c) * g.own, g.own)
        dst[pl.ds(a, g.own), :] = keep[rows, :].astype(F32)
        dst[pl.ds(b, g.own), :] = recv[rows, :].astype(F32)


def k_second(g, s):
    c, tc = s.meta[0], s.meta[1]
    x, mod, turned = s.x, s.mod, s.turned
    weave(g, c, s.keep_mid, s.recv, x)
    s.cum[g.t :, :] = jnp.zeros((s.cum.shape[0] - g.t, 128), F32)
    front(g, x, mod, 8, s, s)
    attend(g, s)

    def emit(i, value):
        s.three[i * g.big : (i + 1) * g.big, :] = value

    tail(g, x, mod, 8, s, s, emit)
    turn(g, s.three, pl.multiple_of(c * (HALO * g.pos), g.pos), turned)
    at = (tc * g.tile) % g.own
    for r in range(g.own):
        rows = slice(r * g.tile, (r + 1) * g.tile)
        mine = pl.multiple_of((c * g.own + r) * g.own + at, g.tile)
        theirs = pl.multiple_of(((1 - c) * g.own + r) * g.own + at, g.tile)
        s.tile_keep[rows, :] = turned[pl.ds(mine, g.tile), :]
        s.tile_send[rows, :] = turned[pl.ds(theirs, g.tile), :]


def k_ffn_back(g, base, s):
    c, tc = s.meta[0], s.meta[1]
    if base == 0:
        weave(g, c, s.g_keep, s.g_recv, s.gout)
    else:
        rows = g.own * g.n_tr
        size = rows * g.tile
        for k in range(g.n_tc):
            src = s.near if k < g.n_tc // 2 else s.far
            at = k % (g.n_tc // 2) * size
            block = src[at : at + size, :].astype(F32).reshape(rows, g.tile, g.d)
            to = pl.ds(pl.multiple_of((tc ^ k) * size, size), size)
            s.columns[to, :] = jnp.swapaxes(block, 0, 1).reshape(size, g.d)
        s.gout[...] = s.columns[pl.ds(pl.multiple_of(c * (g.shift * rows), rows), g.t), :]
    s.small[...] = jnp.zeros((SMALL, g.d), F32)
    ffn_back(g, c, tc, s.gout, s.mod, base, s, s, s)


def k_core(g, base, s):
    c, tc = s.meta[0], s.meta[1]
    s.small[...] = s.small_in[...]
    attn_core(g, s, s)
    proj_grads(g, c, tc, s, s, 0)


def k_conv(g, base, s):
    c, tc = s.meta[0], s.meta[1]
    mixed_back(g, base // 8, s, s)
    s.small[...] = s.small_in[...]

    def emit(i, value):
        s.gin[i * g.ch : (i + 1) * g.ch, :] = value

    conv_back(g, c, s.x, s.mod, base, s, s, s, emit)
    kernel_grads(g, c, s.mod, s, s)
    turned = s.turned
    turn(g, s.gin, pl.multiple_of(c * (HALO * g.pos), g.pos), turned)
    if base:
        s.g_keep[...] = part_of(g, turned, c)
        s.g_send[...] = part_of(g, turned, 1 - c).astype(BF)
        return
    size = g.tile * g.own
    block = turned[pl.ds(pl.multiple_of(tc * size, size), size), :]
    s.tile[...] = jnp.swapaxes(block.reshape(g.tile, g.own, g.d), 0, 1).reshape(size, g.d)


def both_cores(s):
    both = s.small[...] + s.small_recv[...]
    return jnp.where(iota(both.shape, 0) == 6, s.small[...], both)


def side_by_side(g, part):
    half = g.rp // 2
    return jnp.concatenate([part[0:half, 0:192], part[half:, 0:192]], axis=1)


def k_join(g, size, small_too, s):
    bit = s.meta[2] % 2
    half = g.rp // 2
    s.sum_a[...] = s.keep_a[...] + s.recv_a[...].astype(F32)
    if size == g.rab:
        s.sum_b[...] = s.keep_b[...] + s.recv_b[...].astype(F32)
    if small_too:
        small = both_cores(s)
        s.apart[...], s.summed[...] = small[0:8, :], small[8:SMALL, :]
        end = (g.n_dp // 2) * size
        s.send[end : end + 24, :] = small[8:SMALL, :].astype(BF)
        s.send[end + 24 : end + 32, :] = small[0:8, :].astype(BF)
    for m in range(g.n_dp // 2):
        for which, dst in ((bit, s.held), (1 - bit, s.send)):
            rows = pl.ds(pl.multiple_of((2 * m + which) * g.rp, g.rp), g.rp)
            dst[m * size : m * size + g.rp, :] = s.sum_a[rows, :].astype(dst.dtype)
            if size == g.rab:
                packed = side_by_side(g, s.sum_b[rows, :])
                rest = size - g.rp - half
                if rest:
                    packed = jnp.concatenate([packed, jnp.zeros((rest, g.d), F32)], axis=0)
                dst[m * size + g.rp : (m + 1) * size, :] = packed.astype(dst.dtype)


def k_step(g, step, size, small_too, s):
    parts = g.n_dp >> (step + 1)
    s.total[...] = s.got[...] + s.recv[0 : parts * size, :].astype(F32)
    blocks = 8 << step
    end = parts * size
    if small_too:
        summed = s.was_summed[...] + s.recv[end : end + 24, :].astype(F32)
        s.summed[...] = summed
        s.apart[0:blocks, :] = s.was_apart[...]
        s.apart[blocks : 2 * blocks, :] = s.recv[end + 24 : end + 24 + blocks, :].astype(F32)
    if parts == 1:
        return
    bit = (s.meta[2] // (2 << step)) % 2
    for m in range(parts // 2):
        for which, dst in ((bit, s.held), (1 - bit, s.send)):
            rows = pl.ds(pl.multiple_of((2 * m + which) * size, size), size)
            dst[m * size : (m + 1) * size, :] = s.total[rows, :].astype(dst.dtype)
    if small_too:
        end = (parts // 2) * size
        s.send[end : end + 24, :] = summed.astype(BF)
        s.send[end + 24 : end + 24 + 2 * blocks, :] = s.apart[...].astype(BF)


def k_last(g, s):
    me = s.meta[2]
    s.sum_b[...] = s.keep_b[...] + s.recv_b[...].astype(F32)
    small = both_cores(s)
    for k in range(g.n_dp):
        rows = pl.ds(pl.multiple_of((me ^ k) * g.rp, g.rp), g.rp)
        out = s.parts[k]
        out[0:SMALL, :] = small.astype(out.dtype)
        out[SMALL:, :] = side_by_side(g, s.sum_b[rows, :]).astype(out.dtype)


def finish(g, b, s, ab, proj, summed, apart):
    c, tc, me = s.meta[0], s.meta[1], s.meta[2]
    idx = c * g.n_tc + tc
    rp, rows, half = g.rp, g.rows, g.rp // 2
    acc, acct = s.acc, s.acct
    s.up_weight[b] = ab[0:rows, 0 : g.upc]
    acc[0:rp, 0:384] = ab
    acc[0:half, 384:576] = proj[:, 0:192]
    acc[half:rp, 384:576] = proj[:, 192:384]
    for n in range(1, 5):
        acct[n * 128 : (n + 1) * 128, :] = acc[:, n * 128 : (n + 1) * 128].T
    for j in range(g.ff // g.d):
        at = 192 + g.cols * j
        s.down_weight[b, :, j * rows : (j + 1) * rows] = acct[at : at + g.cols, 0:rows]
    for j, ref in enumerate((s.query, s.key, s.value, s.proj)):
        at = 384 + g.cols * j
        ref[b] = acct[at : at + g.cols, 0:rows]
    for a in range(3):
        for e in range(3):
            at = 3 * a + e if b == 0 else 3 * e + a
            s.conv_weight[a, e, b : b + 1, :] = summed[at : at + 1, :]
    s.conv_bias[b : b + 1, :] = summed[9:10, :]
    for m in range(g.ff // g.d):
        s.up_bias[b : b + 1, m * g.d : (m + 1) * g.d] = summed[10 + m : 11 + m, :]
    s.down_bias[b : b + 1, :] = summed[14:15, :]
    for h in range(6):
        s.gate_weight[h, b : b + 1, :] = summed[15 + h : 16 + h, :]
    s.row[...] = jnp.broadcast_to(summed[21:22, :], (8, g.d))
    s.gate_bias[b : b + 1, :] = s.row[0:1, 0:6]
    width = 6 * g.d // (g.n_tr * g.n_tc)
    wide = 384
    prod = jnp.zeros((rp, wide), F32)
    total = apart[0]
    for part in apart[1:]:
        total = total + part
    for m in range(6):
        s.ada_bias[b : b + 1, m * g.d : (m + 1) * g.d] = total[m : m + 1, :]
    pieces = []
    for m in range(6):
        lines = [part[m : m + 1, :] for part in apart]
        pieces.append(jnp.concatenate(lines + [jnp.zeros((-len(apart) % 8, g.d), F32)] * (len(apart) % 8 > 0), axis=0))
    s.gms[...] = jnp.concatenate(pieces, axis=1)
    full = pltpu.roll(s.gms[...], 6 * g.d - idx * width, 1)
    for k in range(g.n_dp):
        cond = s.cond[k * rp : (k + 1) * rp, :]
        prod = prod + jnp.concatenate([cond] * (wide // 128), axis=1) * full[k : k + 1, 0:wide]
    s.ada_weight[b] = prod[0:rows, 0:width]


FINAL = names(
    lambda ada_weight, ada_bias, conv_weight, conv_bias, query, key, value, proj, gate_weight, gate_bias,
    up_weight, up_bias, down_weight, down_bias: None
)
BY_ROW = names(lambda ada_bias, conv_bias, gate_bias, up_bias, down_bias: None)
INNER = names(lambda conv_weight, gate_weight: None)


def k_final_one(g, s):
    c, tc = s.meta[0], s.meta[1]
    near = (tc * g.tile) // g.own == c

    @pl.when(near)
    def _():
        s.out[0] = s.tile_keep[...].reshape(g.own, g.tile, g.d)

    @pl.when(jnp.logical_not(near))
    def _():
        s.out[0] = s.tile_recv[...].reshape(g.own, g.tile, g.d)

    s.grad[0] = s.tile[...].reshape(g.own, g.tile, g.d)
    half = g.rp // 2
    total = s.got[...]
    apart = [s.apart[8 * n : 8 * n + 8, :] for n in range(g.n_dp)]
    for k, part in enumerate(apart):
        column = jnp.broadcast_to(part[6:7, :], (128, g.d)).T
        column = pltpu.roll(column, g.d - s.meta[2] * g.rows, 0)
        s.cond[k * g.rp : (k + 1) * g.rp, :] = column[0 : g.rp, :]
    finish(g, 1, s, total[0 : g.rp, :], total[g.rp : g.rp + half, :], s.summed[...], apart)


def k_final(g, s):
    for name in FINAL:
        src, dst = s.first[name], s[name]
        if name in BY_ROW:
            dst[1:2, :] = src[1:2, :]
        elif name in INNER:
            lead = (slice(None),) * (len(dst.shape) - 2)
            dst[lead + (slice(1, 2),)] = src[lead + (slice(1, 2),)]
        else:
            dst[1] = src[1]
    ab = s.got[...]
    proj = s.parts[0][SMALL:, :]
    summed = s.parts[0][8:SMALL, :]
    apart = []
    for k, part in enumerate(s.parts):
        wide = part[...].astype(F32)
        apart.append(wide[0:8, :])
        if k:
            summed = summed + wide[8:SMALL, :]
            proj = proj + wide[SMALL:, :]
    finish(g, 0, s, ab, proj, summed, apart)


def padded_bytes(shape, dtype):
    shape = (1,) * (2 - len(shape)) + tuple(shape)
    rows, lanes = -(-shape[-2] // 16) * 16, -(-shape[-1] // 128) * 128
    return math.prod(shape[:-2]) * rows * lanes * jnp.dtype(dtype).itemsize


def call(us, kernel, ins, outs, scratch=(), weights=(), block=0, spare=VMEM_SPARE, fetch=()):
    ins = Table(ins, **dict(weights))
    ins, outs, scratch = dict(ins), dict(outs), dict(scratch)
    sources = {n: ins.pop(n) for n in fetch}
    buffers = {n: (a.shape[1:] if n in STACKED else a.shape, a.dtype) for n, a in sources.items()}
    flat, tree = jax.tree.flatten(ins)
    spread_outs = [o if isinstance(o, list) else [o] for o in outs.values()]
    flat_outs = [o for group in spread_outs for o in group]
    meta = ins.get("meta")

    def run(*refs):
        refs = list(refs)

        def take(n):
            got = refs[:n]
            del refs[:n]
            return got

        table = Table(jax.tree.unflatten(tree, take(len(flat))))
        hbm = dict(zip(sources, take(len(sources))))
        for name, ref in table.items():
            if name in STACKED:
                table[name] = ref.at[block]
        for name, o in outs.items():
            table[name] = take(len(o)) if isinstance(o, list) else take(1)[0]
        table.update(zip(scratch, take(len(scratch))))
        held = dict(zip(buffers, take(len(buffers))))
        s = Refs(table, block, hbm, held, refs[0] if refs else None)
        kernel(s)
        s.finish()

    held = [(a.shape, a.dtype) for a in flat] + flat_outs + list(scratch.values()) + list(buffers.values())
    need = sum(padded_bytes(*h) for h in held)
    results = pl.pallas_call(
        run,
        in_specs=[pl.BlockSpec(memory_space=pltpu.SMEM if a is meta else pltpu.VMEM) for a in flat]
        + [pl.BlockSpec(memory_space=pl.ANY)] * len(sources),
        out_specs=[pl.BlockSpec(memory_space=pltpu.VMEM)] * len(flat_outs),
        out_shape=[jax.ShapeDtypeStruct(*o) for o in flat_outs],
        scratch_shapes=[pltpu.VMEM(*sc) for sc in (*scratch.values(), *buffers.values())]
        + [pltpu.SemaphoreType.DMA((len(sources),))] * bool(sources),
        compiler_params=pltpu.CompilerParams(vmem_limit_bytes=need + need // 16 + spare),
        cost_estimate=pl.CostEstimate(flops=int(us * 1e9), bytes_accessed=int(us * 3e6), transcendentals=0),
    )(*flat, *sources.values())
    results = list(results)
    found = Table()
    for name, o in outs.items():
        if isinstance(o, list):
            found[name] = results[: len(o)]
            del results[: len(o)]
        else:
            found[name] = results.pop(0)
    return found


def body(
    g,
    tokens,
    condition,
    cotangent,
    ada_weight,
    ada_bias,
    conv_weight,
    conv_bias,
    query_weight,
    key_weight,
    value_weight,
    out_weight,
    gate_weight,
    gate_bias,
    up_weight,
    up_bias,
    down_weight,
    down_bias,
):
    d, ff, t = g.d, g.ff, g.t
    meta = jnp.stack(
        [lax.axis_index("tr"), lax.axis_index("tc"), lax.axis_index("dp"), jnp.int32(0)]
    ).astype(jnp.int32)

    def xor(axis, k):
        return [(i, i ^ k) for i in range(lax.axis_size(axis))]

    def other(array):
        return lax.ppermute(array, "tr", [(0, 1), (1, 0)])

    part = functools.partial
    tile, half, deep = g.own * g.tile, g.win * g.own, g.n_dp * g.rp
    shapes, backs = save_shapes(g), back_shapes(g)
    weights = Table(
        wq=query_weight,
        wk=key_weight,
        wv=value_weight,
        wo=out_weight,
        gw=jnp.transpose(gate_weight, (2, 0, 1)),
        gb=gate_bias,
        cw=jnp.transpose(conv_weight, (1, 2, 0, 3)),
        cb=conv_bias,
        up=up_weight,
        upb=up_bias,
        down=down_weight,
        downb=down_bias,
    )

    def pick(table, names):
        return {n: table[n] for n in names}

    r = call(
        1,
        part(k_prep, g),
        Table(meta=meta, tok=tokens),
        Table(tokb=((tile, d), BF), halo=((HALO * g.tile, d), BF)),
    )
    halo = other(r.halo)
    cot = call(1, part(k_cast, g), Table(cot=cotangent), Table(low=((tile, d), BF))).low
    cot_recv = other(cot)
    ext = call(
        1,
        part(k_extend, g),
        Table(meta=meta, tokb=r.tokb, halo=halo),
        Table(ext=((half // 2, d), BF)),
    ).ext
    cot = call(
        1,
        part(k_rows, g),
        Table(meta=meta, mine=cot, theirs=cot_recv),
        Table(both=((2 * tile, d), BF)),
    ).both
    ext, condition = lax.optimization_barrier((ext, condition))
    tiles = [ext] + [lax.ppermute(ext, "tc", xor("tc", k)) for k in range(1, g.n_tc)]

    def double(array, step):
        got = lax.ppermute(array, "tc", xor("tc", 1 << step))
        shape = (2 * array.shape[0], d)
        return array, got, lambda: call(1, k_stack, Table(mine=array, theirs=got), Table(both=(shape, BF))).both

    ext_done, cot = lax.optimization_barrier((ext, cot))
    stack = double(cot, 0)[2]
    mod = call(
        1,
        part(k_modulate, g),
        Table(cond=condition, ada_w=ada_weight, ada_b=ada_bias),
        Table(mod=((16, d), F32)),
    ).mod
    base_ins = Table(meta=meta, mod=mod)
    save0 = call(
        8,
        part(k_first, g),
        Table(**base_ins, tiles=tiles),
        Table(
            keep_mid=((half, d), F32),
            send=((half, d), BF),
            **pick(shapes, SAVE),
        ),
        Table(mid=((t, d), F32), turned=((g.to, d), F32), cum=shapes.cum),
        pick(weights, FRONT_W + TAIL_W),
        0,
    )
    cot, _ = lax.optimization_barrier((stack(), save0.send))
    near, far, _ = double(cot, 1)
    save1 = call(
        8,
        part(k_second, g),
        Table(**base_ins, keep_mid=save0.keep_mid, recv=other(save0.send)),
        Table(
            tile_keep=((tile, d), F32),
            tile_send=((tile, d), F32),
            **pick(shapes, SAVE),
        ),
        Table(three=((t, d), F32), turned=((g.to, d), F32), cum=shapes.cum),
        pick(weights, FRONT_W + TAIL_W),
        1,
    )
    tile_recv = other(save1.tile_send)

    def ffn(b, save, ins):
        return call(
            4,
            part(k_ffn_back, g, 8 * b),
            Table(**base_ins, **ins, **pick(save, names(lambda gel, resid, branch, mlp, n2, hid: None))),
            Table(
                gres=backs.gres,
                gbr=backs.gbr,
                keep=((deep, d), F32),
                send=((deep, d), BF),
                small=((SMALL, d), F32),
            ),
            Table(**pick(backs, names(lambda gmlp, gpre, tmp1, tmp2, dn, upg: None)), gout=((t, d), F32), **(Table(columns=((g.n_tc * 2 * tile, d), F32)) if b else Table())),
            pick(weights, names(lambda down, up: None)),
            b,
        )

    def core(b, save, f):
        return call(
            4,
            part(k_core, g, 8 * b),
            Table(
                **base_ins,
                gbr=f.gbr,
                small_in=f.small,
                **pick(save, names(lambda q, k, v, gp, prob, decay, mixed, att: None)),
            ),
            Table(
                **pick(backs, names(lambda gqkv, ggp: None)),
                keep=((deep, 256), F32),
                send=((deep, 256), BF),
                small=((SMALL, d), F32),
            ),
            pick(backs, names(lambda gatt, dlow, wlow, ulow: None)),
            pick(weights, names(lambda wo: None)),
            b,
        )

    def conv(b, save, f, e):
        ends = Table(g_keep=((half, d), F32), g_send=((half, d), BF)) if b else Table(tile=((tile, d), F32))
        return call(
            4,
            part(k_conv, g, 8 * b),
            Table(
                **base_ins,
                gres=f.gres,
                small_in=e.small,
                **pick(e, names(lambda gqkv, ggp: None)),
                **pick(save, names(lambda x, pad: None)),
            ),
            Table(**ends, small=((SMALL, d), F32)),
            Table(
                **pick(backs, names(lambda tmp1, tmp2, gpad: None)),
                gin=((t, d), F32),
                turned=((g.to, d), F32),
            ),
            pick(weights, names(lambda wq, wk, wv, gw, cw: None)),
            b,
        )

    def projections(e):
        return Table(keep_b=e.keep, recv_b=other(e.send))

    def smalls(h):
        return Table(small=h.small, small_recv=other(h.small))

    def join(f, e, h):
        size, end = g.rab if e else g.rp, 32 if h else 0
        ins = Table(meta=meta, keep_a=f.keep, recv_a=f.recv)
        outs = Table(held=((g.n_dp // 2 * size, d), F32), send=((g.n_dp // 2 * size + end, d), BF))
        scratch = Table(sum_a=((deep, d), F32))
        if e:
            ins.update(e)
            scratch = Table(scratch, sum_b=((deep, 256), F32))
        if h:
            ins.update(h)
            outs = Table(outs, apart=((8, d), F32), summed=((24, d), F32))
        found = call(1, part(k_join, g, size, h is not None), ins, outs, scratch)
        return Table(found, size=size)

    def hop(state, step):
        return Table(state, recv=lax.ppermute(state.send, "dp", xor("dp", 1 << step)))

    def take(state, step):
        size, parts = state.size, g.n_dp >> (step + 1)
        small_too = state.get(*names(lambda apart: None)) is not None
        blocks = 16 << step
        end = -(-(24 + blocks) // 16) * 16 if small_too else 0
        outs, scratch = Table(), Table()
        total = ((parts * size, d), F32)
        if parts > 1:
            outs = Table(held=((parts // 2 * size, d), F32), send=((parts // 2 * size + end, d), BF))
            scratch = Table(total=total)
        else:
            outs = Table(total=total)
        ins = Table(meta=meta, got=state.held, recv=state.recv)
        if small_too:
            ins = Table(ins, was_apart=state.apart, was_summed=state.summed)
            outs = Table(outs, apart=((blocks, d), F32), summed=((24, d), F32))
        return Table(call(1, part(k_step, g, step, size, small_too), ins, outs, scratch), size=size)

    def spread(parts):
        return [parts[0]] + [lax.ppermute(parts[k], "dp", xor("dp", k)) for k in range(1, g.n_dp)]

    def before(table, *later):
        flat, tree = jax.tree.flatten((dict(table), later))
        return Table(jax.tree.unflatten(tree, lax.optimization_barrier(flat))[0])

    f1 = ffn(1, save1, Table(near=near, far=far))
    f1 = Table(f1, recv=other(f1.send))
    e1 = core(1, save1, f1)
    e1b = projections(e1)
    h1 = conv(1, save1, f1, e1)
    g_recv = other(h1.g_send)
    h1s = smalls(h1)
    one = join(f1, e1b, None)
    h1 = before(h1, one.send)
    one = hop(one, 0)
    f0 = ffn(0, save0, Table(g_keep=h1.g_keep, g_recv=g_recv))
    f0 = Table(f0, recv=other(f0.send))
    one = take(one, 0)
    two = join(f0, None, h1s)
    f0b = before(f0, one.get(*names(lambda send: None)), two.send)
    if g.steps > 1:
        one = hop(one, 1)
    two = hop(two, 0)
    e0 = core(0, save0, f0b)
    e0b = projections(e0)
    two = take(two, 0)
    e0 = before(e0, two.get(*names(lambda send: None)))
    if g.steps > 1:
        two = hop(two, 1)
    h0 = conv(0, save0, f0, e0)
    for step in range(1, g.steps):
        one, two = take(one, step), take(two, step)
        if step + 1 < g.steps:
            one, two = hop(one, step + 1), hop(two, step + 1)
    parts0 = spread(
        call(
            1,
            part(k_last, g),
            Table(meta=meta, **e0b, **smalls(h0)),
            Table(parts=[((SMALL + g.rp // 2, d), BF if k else F32) for k in range(g.n_dp)]),
            Table(sum_b=((deep, 256), F32)),
        ).parts
    )
    n_cols = g.n_tr * g.n_tc
    shards = ((2, g.cols, g.rows), F32)
    final_shapes = dict(
        zip(
            FINAL,
            (
                ((2, g.rows, 6 * d // n_cols), F32),
                ((2, 6 * d), F32),
                ((3, 3, 2, d), F32),
                ((2, d), F32),
                shards,
                shards,
                shards,
                shards,
                ((6, 2, d), F32),
                ((2, 6), F32),
                ((2, g.rows, g.upc), F32),
                ((2, ff), F32),
                ((2, g.cols, ff // g.n_dp), F32),
                ((2, d), F32),
            ),
        )
    )
    scratch = Table(acc=((128, 640), F32), acct=((640, 128), F32), row=((8, d), F32), gms=((-(-g.n_dp // 8) * 8, 6 * d), F32))
    first = call(
        3,
        part(k_final_one, g),
        Table(
            meta=meta,
            tile_keep=save1.tile_keep,
            tile_recv=tile_recv,
            tile=h0.tile,
            got=one.total,
            apart=two.apart,
            summed=two.summed,
        ),
        Table(final_shapes, out=(tokens.shape, F32), grad=(tokens.shape, F32), cond=((deep, 128), F32)),
        scratch,
        spare=6 * VMEM_SPARE,
    )
    output = first.out
    finals = call(
        3,
        part(k_final, g),
        Table(
            meta=meta,
            got=two.total,
            parts=parts0,
            cond=first.cond,
            first={n: first[n] for n in FINAL},
        ),
        final_shapes,
        scratch,
        spare=6 * VMEM_SPARE,
    )
    finals = [finals[n] for n in FINAL]
    finals[2] = jnp.transpose(finals[2], (2, 0, 1, 3))
    finals[8] = jnp.transpose(finals[8], (1, 2, 0))
    for n in (4, 5, 6, 7, 12):
        finals[n] = jnp.swapaxes(finals[n], 1, 2)
    return (output, first.grad) + tuple(finals)


def solution(mesh):
    everywhere = P()
    tiles = P("dp", "tr", "tc", None)
    cut = P(None, "dp", ("tr", "tc"))
    in_specs = (tiles, P("dp", None), tiles) + (everywhere,) * 14
    out_specs = (tiles, tiles, cut, P(), P(), P(), cut, cut, cut, cut, P(), P(), cut, P(), cut, P())

    def program(*arrays):
        g = Geo(mesh, arrays[0].shape, arrays[13].shape)
        run = functools.partial(body, g)
        return jax.shard_map(run, mesh=mesh, in_specs=in_specs, out_specs=out_specs, check_vma=False)(*arrays)

    return program
```

```python
import functools
import inspect
import math

import jax
import jax.numpy as jnp
from jax import lax
from jax.experimental import pallas as pl
from jax.experimental.pallas import tpu as pltpu
from jax.sharding import PartitionSpec as P

BF = jnp.bfloat16
F32 = jnp.float32
EPS = 1e-06
GATE_NORM = 16.0
HALO = 2
GELU_A = 0.7978845608028654
GELU_B = 0.044715
NEG = -1e30
VMEM_SPARE = 3 * 1024 * 1024
SMALL = 32


def mm(a, b):
    return jnp.dot(a, b, preferred_element_type=F32)


def mm_rt(a, b):
    return lax.dot_general(a, b, (((1,), (1,)), ((), ())), preferred_element_type=F32)


def mm_lt(a, b):
    return lax.dot_general(a, b, (((0,), (0,)), ((), ())), preferred_element_type=F32)


def hi_lo(x):
    hi = x.astype(BF)
    return hi, (x - hi.astype(F32)).astype(BF)


def normalize(x):
    center = x - jnp.mean(x, axis=-1, keepdims=True)
    rstd = lax.rsqrt(jnp.mean(center * center, axis=-1, keepdims=True) + EPS)
    return center * rstd, rstd


def normalize_back(g_y, y, rstd):
    return rstd * (
        g_y - jnp.mean(g_y, axis=-1, keepdims=True) - y * jnp.mean(g_y * y, axis=-1, keepdims=True)
    )


def iota(shape, dim):
    return lax.broadcasted_iota(jnp.int32, shape, dim)


def names(function):
    return tuple(inspect.signature(function).parameters)


class Table(dict):
    __getattr__ = dict.__getitem__


class Geo:
    def __init__(self, mesh, tokens, up):
        self.n_dp, self.n_tr, self.n_tc = (mesh.shape[a] for a in ("dp", "tr", "tc"))
        self.images, self.own, self.tile = (tokens[0] // self.n_dp, tokens[1] // self.n_tr, tokens[2] // self.n_tc)
        self.pos = tokens[2]
        self.d = tokens[3]
        self.ff = up[2]
        self.win = self.own + HALO
        self.t = self.win * self.pos
        self.to = self.own * self.pos
        self.lt = self.d // 128
        self.pairs = self.d // 128
        self.group = 64
        self.groups = self.t // self.group
        self.ch = 3 * self.pos
        self.chunks = self.t // self.ch
        self.big = 288
        self.bigs = self.t // self.big
        self.fc = 768
        self.fcs = self.ff // self.fc
        self.shift = self.pos - self.win
        self.rows = self.d // self.n_dp
        self.rp = -(-self.rows // 16) * 16
        self.rab = -(-(self.rp + self.rp // 2) // 16) * 16
        self.steps = self.n_dp.bit_length() - 1
        self.cols = self.d // (self.n_tr * self.n_tc)
        self.upc = self.ff // (self.n_tr * self.n_tc)


def kernel_taps(w, blk):
    at = slice(blk, blk + 1)
    return [[w.cw[a, b, at, :] if blk == 0 else w.cw[b, a, at, :] for b in range(3)] for a in range(3)]


def gate_rows(g, w, blk):
    heads = w.gw.shape[0]
    rows = [w.gw[h, blk : blk + 1, :] for h in range(heads)]
    return hi_lo(jnp.concatenate(rows + [jnp.zeros((128 - heads, g.d), F32)], axis=0))


def front(g, x, mod, base, w, s):
    d, pos, ch = g.d, g.pos, g.ch
    shift, scale = mod[base : base + 1, :], 1.0 + mod[base + 1 : base + 2, :]
    zero = jnp.zeros((pos, d), BF)
    s.pad[0:pos, :] = zero
    s.pad[g.t + pos : g.t + 2 * pos, :] = zero
    for i in range(g.chunks):
        rows = slice(i * ch, (i + 1) * ch)
        y, _ = normalize(x[rows, :])
        s.pad[pos + i * ch : pos + (i + 1) * ch, :] = (y * scale + shift).astype(BF)
    at = iota((ch, 1), 0) % pos
    first, last = at == 0, at == pos - 1
    taps = kernel_taps(w, base // 8)
    blk = base // 8
    bias = w.cb[blk : blk + 1, :]
    for i in range(g.chunks):
        wide = s.pad[i * ch : i * ch + ch + 2 * pos, :].astype(F32)
        lines = [wide[a * pos : a * pos + ch, :] for a in range(3)]
        v = [sum(lines[a] * taps[a][b] for a in range(3)) for b in range(3)]
        mixed = v[1] + bias
        mixed = mixed + jnp.where(first, 0.0, pltpu.roll(v[0], 1, 0))
        mixed = mixed + jnp.where(last, 0.0, pltpu.roll(v[2], ch - 1, 0))
        s.mixed[i * ch : (i + 1) * ch, :] = mixed.astype(BF)
    for out, weight in ((s.q, w.wq), (s.k, w.wk), (s.v, w.wv)):
        out[...] = mm(s.mixed[...], weight[...]).astype(BF)
    g_hi, g_lo = gate_rows(g, w, blk)
    mixed = s.mixed[...]
    heads = w.gb.shape[1]
    bias = jnp.concatenate([w.gb[blk : blk + 1, :], jnp.zeros((1, 128 - heads), F32)], axis=1)
    pre = mm_rt(mixed, g_hi) + mm_rt(mixed, g_lo) + bias
    s.gp[...] = pre
    run = (jnp.minimum(pre, 0.0) - jnp.log1p(jnp.exp(-jnp.abs(pre)))) * (1.0 / GATE_NORM)
    at = iota((g.t, 1), 0) % pos
    step = 1
    while step < pos:
        run = run + jnp.where(at >= step, pltpu.roll(run, step, 0), 0.0)
        step *= 2
    s.cum[0 : g.t, :] = run


def decay_rows(g, s):
    lane = iota((1, 128), 1)
    found = {}
    for m in range((g.t + 127) // 128):
        full = s.cum[m * 128 : (m + 1) * 128, :].T
        for j in range(g.pairs):
            one, two = full[2 * j : 2 * j + 1, :], full[2 * j + 1 : 2 * j + 2, :]
            lo_row = jnp.where(lane < 64, one, pltpu.roll(two, 64, 1))
            hi_row = jnp.where(lane < 64, pltpu.roll(one, 64, 1), two)
            found[2 * m, j] = lo_row
            found[2 * m + 1, j] = hi_row
    return found


def pair_masks(g):
    row, lane = iota((64, 128), 0), iota((64, 128), 1)
    src = lane % 64
    same = (row // g.pos) == (src // g.pos)
    return lane < 64, same & (row >= src), same & (row > src)


def split_heads(block, low_half):
    zero = jnp.zeros_like(block)
    return jnp.concatenate([jnp.where(low_half, block, zero), jnp.where(low_half, zero, block)], axis=0)


def pair_blocks(g):
    for grp in range(g.groups):
        for j in range(g.pairs):
            yield grp, slice(grp * 64, grp * 64 + 64), j, slice(j * 128, j * 128 + 128)


def pair_decay(s, source, grp, j, low_half, causal):
    rows = slice(grp * 64, grp * 64 + 64)
    ct = jnp.where(low_half, s.cum[rows, 2 * j : 2 * j + 1], s.cum[rows, 2 * j + 1 : 2 * j + 2])
    return jnp.exp(jnp.where(causal, ct - source[grp, j], NEG)) * 0.125


def attend(g, s):
    low_half, causal, _ = pair_masks(g)
    source = decay_rows(g, s)
    for grp, rows, j, lanes in pair_blocks(g):
        scores = mm_rt(s.q[rows, lanes], split_heads(s.k[rows, lanes], low_half))
        decay = pair_decay(s, source, grp, j, low_half, causal)
        s.decay[rows, lanes] = decay.astype(BF)
        s.prob[rows, lanes] = (scores * decay).astype(BF)
    for _, rows, _, lanes in pair_blocks(g):
        s.att[rows, lanes] = mm(s.prob[rows, lanes], split_heads(s.v[rows, lanes], low_half)).astype(BF)


def tail(g, x, mod, base, w, s, emit):
    gate_one, gate_two = mod[base + 2 : base + 3, :], mod[base + 5 : base + 6, :]
    shift, scale = mod[base + 3 : base + 4, :], 1.0 + mod[base + 4 : base + 5, :]
    for i in range(g.bigs):
        rows = slice(i * g.big, (i + 1) * g.big)
        branch = mm(s.att[rows, :], w.wo[...])
        s.branch[rows, :] = branch.astype(BF)
        resid = x[rows, :] + gate_one * branch
        s.resid[rows, :] = resid
        y, _ = normalize(resid)
        s.n2[rows, :] = (y * scale + shift).astype(BF)
    for f in range(g.fcs):
        fl = slice(f * g.fc, (f + 1) * g.fc)
        for i in range(g.bigs):
            rows = slice(i * g.big, (i + 1) * g.big)
            pre = mm(s.n2[rows, :], w.up[:, fl]) + w.upb[base // 8 : base // 8 + 1, fl]
            sq = pre * pre
            half = 0.5 * jnp.tanh(pre * (GELU_A + (GELU_A * GELU_B) * sq)) + 0.5
            hid = pre * half
            s.hid[rows, fl] = hid.astype(BF)
            inner = 2.0 * GELU_A + (6.0 * GELU_A * GELU_B) * sq
            s.gel[rows, fl] = (half + hid * (1.0 - half) * inner).astype(s.gel.dtype)
    for i in range(g.bigs):
        rows = slice(i * g.big, (i + 1) * g.big)
        mlp = mm(s.hid[rows, :], w.down[...]) + w.downb[base // 8 : base // 8 + 1, :]
        s.mlp[rows, :] = mlp.astype(s.mlp.dtype)
        emit(i, s.resid[rows, :] + gate_two * mlp)


def select_cols(width, source, half, tc, c, n_tc, lanes):
    row, lane = iota((source, 2 * half), 0), iota((source, 2 * half), 1)
    core = jnp.where(lane < half, c, 1 - c)
    inside = lane % half - lanes
    want = (core * n_tc + tc) * width + inside
    hit = (row == want) & (inside >= 0) & (inside < width)
    return jnp.where(hit, 1.0, 0.0).astype(BF)


def own_sum(g, c, ref, lanes=None):
    start = pl.multiple_of(c * (HALO * g.pos), HALO * g.pos)
    if lanes is None:
        return ref[pl.ds(start, g.to), :]
    return ref[pl.ds(start, g.to), lanes]


def colsum(a):
    return jnp.sum(a.astype(F32), axis=0, keepdims=True)


def lay(g, dst, lane0, value):
    lanes = slice(lane0, lane0 + value.shape[1])
    if g.rp == g.rows:
        dst[:, lanes] = value.astype(dst.dtype)
        return
    for n in range(g.n_dp):
        part = value[n * g.rows : (n + 1) * g.rows, :]
        pad = jnp.zeros((g.rp - g.rows, value.shape[1]), F32)
        dst[n * g.rp : (n + 1) * g.rp, lanes] = jnp.concatenate([part, pad], axis=0).astype(dst.dtype)


def ffn_back(g, c, tc, g_out, mod, base, w, s, o):
    gate_one, gate_two = mod[base + 2 : base + 3, :], mod[base + 5 : base + 6, :]
    scale = 1.0 + mod[base + 4 : base + 5, :]
    for i in range(g.bigs):
        rows = slice(i * g.big, (i + 1) * g.big)
        s.gmlp[rows, :] = (gate_two * g_out[rows, :]).astype(BF)
    for f in range(g.fcs):
        fl = slice(f * g.fc, (f + 1) * g.fc)
        for i in range(g.bigs):
            rows = slice(i * g.big, (i + 1) * g.big)
            g_hid = mm_rt(s.gmlp[rows, :], w.down[fl, :])
            s.gpre[rows, fl] = (s.gel[rows, fl].astype(F32) * g_hid).astype(BF)
    for i in range(g.bigs):
        rows = slice(i * g.big, (i + 1) * g.big)
        g_n2 = mm_rt(s.gpre[rows, :], w.up[...])
        y, rstd = normalize(s.resid[rows, :])
        g_res = g_out[rows, :] + normalize_back(g_n2 * scale, y, rstd)
        s.gres[rows, :] = g_res
        s.tmp1[rows, :] = g_n2
        s.tmp2[rows, :] = g_n2 * y
        s.gbr[rows, :] = (gate_one * g_res).astype(BF)
    own = functools.partial(own_sum, g, c)
    small = o.small
    small[2:3, :] = colsum(own(s.gres) * own(s.branch).astype(F32))
    small[3:4, :] = colsum(own(s.tmp1))
    small[4:5, :] = colsum(own(s.tmp2))
    small[5:6, :] = colsum(own(g_out) * own(s.mlp).astype(F32))
    for f in range(g.ff // g.d):
        small[18 + f : 19 + f, :] = colsum(own(s.gpre, slice(f * g.d, (f + 1) * g.d)))
    small[22:23, :] = colsum(own(s.gmlp))
    n2 = own(s.n2)
    for at, core in ((0, c), (256, 1 - c)):
        first = (core * g.n_tc + tc) * g.upc
        lanes = pl.ds(pl.multiple_of(first // 128 * 128, 128), 256)
        grads = mm_lt(n2, own(s.gpre, lanes))
        s.upg[:, at : at + 256] = jnp.where(first % 128 == 0, grads, pltpu.roll(grads, 192, 1))
    sel = mm(own(s.gmlp), select_cols(g.cols, g.d, 64, tc, c, g.n_tc, 0)).astype(BF)
    s.dn[...] = mm_lt(own(s.hid), sel)
    lane = iota((g.rows, 128), 1)
    per = g.ff // g.d
    for dd in range(g.n_dp):
        up = slice(dd * g.rows, (dd + 1) * g.rows)
        down = [s.dn[(dd * per + j) * g.rows : (dd * per + j + 1) * g.rows, :] for j in range(per)]
        for at, shift, dst in ((0, 0, o.keep), (256, 64, o.send)):
            to = slice(dd * g.rp, dd * g.rp + g.rows)
            one, two, three, four = (
                pltpu.roll(part, (lanes - shift) % 128, 1) for part, lanes in zip(down, (64, 112, 32, 80))
            )
            mid = jnp.where(lane < 112, one, two)
            dst[to, 0:128] = s.upg[up, at : at + 128].astype(dst.dtype)
            dst[to, 128:256] = jnp.where(lane < 64, s.upg[up, at + 128 : at + 256], mid).astype(dst.dtype)
            end = jnp.where(lane < 80, three, four)
            dst[to, 256:384] = jnp.where(lane < 32, two, end).astype(dst.dtype)


def attn_core(g, w, s):
    low_half, causal, strict = pair_masks(g)
    s.gatt[...] = mm_rt(s.gbr[...], w.wo[...]).astype(BF)
    row, col = iota((64, 64), 0), iota((64, 64), 1)
    later = jnp.where((row // g.pos == col // g.pos) & (col >= row), 1.0, 0.0).astype(BF)
    head_of = iota((g.d, 128), 0) // 64
    to_head = jnp.where(head_of == iota((g.d, 128), 1), 1.0, 0.0).astype(BF)
    for _, rows, _, lanes in pair_blocks(g):
        d_p = mm_rt(s.gatt[rows, lanes], split_heads(s.v[rows, lanes], low_half))
        s.dlow[rows, lanes] = (d_p * s.decay[rows, lanes].astype(F32)).astype(BF)
        s.wlow[rows, lanes] = (d_p * s.prob[rows, lanes].astype(F32)).astype(BF)
    strict3 = jnp.concatenate([strict] * g.pairs, axis=1)
    for grp in range(g.groups):
        rows = slice(grp * 64, grp * 64 + 64)
        s.ulow[rows, :] = jnp.where(strict3, mm(later, s.wlow[rows, :]), 0.0).astype(BF)
    for _, rows, j, lanes in pair_blocks(g):
        km = split_heads(s.k[rows, lanes], low_half)
        s.gqkv[rows, j * 128 : j * 128 + 128] = mm(s.dlow[rows, lanes], km).astype(BF)
    for _, rows, j, lanes in pair_blocks(g):
        both = mm_lt(s.dlow[rows, lanes], s.q[rows, lanes])
        s.gqkv[rows, g.d + j * 128 : g.d + j * 128 + 128] = jnp.where(
            low_half, both[0:64, :], both[64:128, :]
        ).astype(BF)
    for _, rows, j, lanes in pair_blocks(g):
        both = mm_lt(s.prob[rows, lanes], s.gatt[rows, lanes])
        s.gqkv[rows, 2 * g.d + j * 128 : 2 * g.d + j * 128 + 128] = jnp.where(
            low_half, both[0:64, :], both[64:128, :]
        ).astype(BF)
    g_log = mm(s.ulow[...], to_head)
    s.ggp[...] = g_log * (jax.nn.sigmoid(-s.gp[...]) * (1.0 / GATE_NORM))


def proj_grads(g, c, tc, s, o, lane0):
    own = functools.partial(own_sum, g, c)
    small = o.small
    pick_cols = select_cols(g.cols, g.d, 64, tc, c, g.n_tc, 0)
    sel = [mm(own(s.gqkv, slice(n * g.d, (n + 1) * g.d)), pick_cols).astype(BF) for n in range(3)]
    sel_out = mm(own(s.gbr), pick_cols).astype(BF)
    grads = mm_lt(own(s.mixed), jnp.concatenate(sel, axis=1))
    three = mm_lt(own(s.att), sel_out)
    zero, one, two = (grads[:, n * 128 : (n + 1) * 128] for n in range(3))
    lane = iota((g.d, 128), 1)
    for shift, dst in ((0, o.keep), (64, o.send)):
        q, k, v, out = (
            pltpu.roll(part, (lanes - shift) % 128, 1)
            for part, lanes in ((zero, 0), (one, 48), (two, 96), (three, 16))
        )
        lay(g, dst, lane0, jnp.where(lane < 48, q, jnp.where(lane < 96, k, v)))
        lay(g, dst, lane0 + 128, jnp.where(lane < 16, v, out))
    gg = own(s.ggp)
    hi, lo = hi_lo(gg)
    mixed = own(s.mixed)
    gate = mm_lt(hi, mixed) + mm_lt(lo, mixed)
    small[23:29, :] = gate[0:6, :]
    small[29:30, 0:128] = colsum(gg)
    small[29:30, 128 : g.d] = jnp.zeros((1, g.d - 128), F32)


def mixed_back(g, blk, w, s):
    pos, d = g.pos, g.d
    w_hi, w_lo = gate_rows(g, w, blk)
    zero = jnp.zeros((pos, d), F32)
    s.gpad[0:pos, :] = zero
    s.gpad[g.t + pos : g.t + 2 * pos, :] = zero
    for i in range(g.bigs):
        rows = slice(i * g.big, (i + 1) * g.big)
        hi, lo = hi_lo(s.ggp[rows, :])
        total = mm(hi, w_hi) + mm(lo, w_hi) + mm(hi, w_lo)
        for n, weight in enumerate((w.wq, w.wk, w.wv)):
            total = total + mm_rt(s.gqkv[rows, n * d : (n + 1) * d], weight[...])
        s.gpad[pos + i * g.big : pos + (i + 1) * g.big, :] = total.astype(BF).astype(F32)


def conv_back(g, c, x, mod, base, w, s, o, emit):
    pos, ch, d = g.pos, g.ch, g.d
    own = functools.partial(own_sum, g, c)
    small = o.small
    at = iota((ch, 1), 0) % pos
    first, last = at == 0, at == pos - 1
    taps = kernel_taps(w, base // 8)
    scale = 1.0 + mod[base + 1 : base + 2, :]
    for i in range(g.chunks):
        rows = slice(i * ch, (i + 1) * ch)
        lines = [s.gpad[i * ch + a * pos : i * ch + a * pos + ch, :] for a in range(3)]
        v = [sum(lines[2 - a] * taps[a][b] for a in range(3)) for b in range(3)]
        g_n = v[1]
        g_n = g_n + jnp.where(last, 0.0, pltpu.roll(v[0], ch - 1, 0))
        g_n = g_n + jnp.where(first, 0.0, pltpu.roll(v[2], 1, 0))
        y, rstd = normalize(x[rows, :])
        s.tmp1[rows, :] = g_n
        s.tmp2[rows, :] = g_n * y
        emit(i, s.gres[rows, :] + normalize_back(g_n * scale, y, rstd))
    small[0:1, :] = colsum(own(s.tmp1))
    small[1:2, :] = colsum(own(s.tmp2))


def kernel_grads(g, c, mod, s, o):
    pos, d = g.pos, g.d
    small = o.small
    oc = 4 * pos
    at = iota((oc, 1), 0) % pos
    first, last = at == 0, at == pos - 1
    sums = [jnp.zeros((8, d), F32) for _ in range(10)]
    for i in range(g.to // oc):
        start = c * (HALO * pos) + i * oc
        mid = s.gpad[pl.ds(pl.multiple_of(start + pos, pos), oc), :]
        shifted = [
            jnp.where(last, 0.0, pltpu.roll(mid, oc - 1, 0)),
            mid,
            jnp.where(first, 0.0, pltpu.roll(mid, 1, 0)),
        ]
        for a in range(3):
            line = s.pad[pl.ds(pl.multiple_of(start + a * pos, pos), oc), :].astype(F32)
            for b in range(3):
                sums[3 * a + b] = sums[3 * a + b] + jnp.sum((line * shifted[b]).reshape(oc // 8, 8, d), axis=0)
        sums[9] = sums[9] + jnp.sum(mid.reshape(oc // 8, 8, d), axis=0)
    for n in range(10):
        small[8 + n : 9 + n, :] = jnp.sum(sums[n], axis=0, keepdims=True)
    small[6:7, :] = mod[6:7, :]
    small[7:8, :] = jnp.zeros((1, d), F32)
    small[30:SMALL, :] = jnp.zeros((SMALL - 30, d), F32)


def attn_back(g, c, tc, x, mod, base, w, s, o, lane0, emit):
    attn_core(g, w, s)
    proj_grads(g, c, tc, s, o, lane0)
    mixed_back(g, base // 8, w, s)
    conv_back(g, c, x, mod, base, w, s, o, emit)
    kernel_grads(g, c, mod, s, o)


def k_prep(g, s):
    c = s.meta[0]
    t = s.tok[0].reshape(g.own * g.tile, g.d).astype(BF)
    s.tokb[...] = t
    edge = HALO * g.tile

    @pl.when(c == 0)
    def _():
        s.halo[...] = t[g.own * g.tile - edge :, :]

    @pl.when(c == 1)
    def _():
        s.halo[...] = t[0:edge, :]


def k_cast(g, s):
    s.low[...] = s.cot[0].reshape(g.own * g.tile, g.d).astype(BF)


def k_rows(g, s):
    c, size = s.meta[0], g.own * g.tile
    s.both[pl.ds(pl.multiple_of(c * size, size), size), :] = s.mine[...]
    s.both[pl.ds(pl.multiple_of((1 - c) * size, size), size), :] = s.theirs[...]


def k_stack(s):
    rows = s.mine.shape[0]
    s.both[0:rows, :] = s.mine[...]
    s.both[rows:, :] = s.theirs[...]


def k_extend(g, s):
    c = s.meta[0]
    edge = HALO * g.tile
    own = g.own * g.tile
    s.ext[pl.ds(pl.multiple_of(c * edge, edge), own), :] = s.tokb[...]
    s.ext[pl.ds(pl.multiple_of((1 - c) * own, edge), edge), :] = s.halo[...]


def k_modulate(g, s):
    mod = s.mod
    act = jax.nn.silu(s.cond[...]).astype(BF)
    rows = jnp.broadcast_to(act, (16, g.d))
    for b in range(2):
        for n in range(6):
            lanes = slice(n * g.d, (n + 1) * g.d)
            out = mm(rows, s.ada_w[b, :, lanes])[0:1, :] + s.ada_b[b : b + 1, lanes]
            mod[b * 8 + n : b * 8 + n + 1, :] = out
        mod[b * 8 + 6 : b * 8 + 7, :] = act.astype(F32)
        mod[b * 8 + 7 : b * 8 + 8, :] = jnp.zeros((1, g.d), F32)


def place_tiles(g, s, lo, lines, dst):
    tc = s.meta[1]
    for k in range(g.n_tc):
        part = s.tiles[k][lo : lo + lines * g.tile, :].astype(F32)
        off = (tc ^ k) * g.tile
        for i in range(lines):
            dst[pl.ds(pl.multiple_of(i * g.pos + off, g.tile), g.tile), :] = part[i * g.tile : (i + 1) * g.tile, :]


def turn(g, ref, start, dst):
    block = ref[pl.ds(start, g.to), :].reshape(g.own, g.pos, g.d)
    dst[...] = jnp.swapaxes(block, 0, 1).reshape(g.to, g.d)


def part_of(g, ref, core):
    return ref[pl.ds(pl.multiple_of(core * (g.shift * g.own), g.own), g.win * g.own), :]


STACKED = names(lambda wq, wk, wv, wo, up, down: None)


class Refs:
    def __init__(self, table, block, sources, buffers, sems):
        self.__dict__.update(table)
        self.buffers, self.copies = buffers, {}
        for n, (name, src) in enumerate(sources.items()):
            src = src.at[block] if name in STACKED else src
            self.copies[name] = pltpu.make_async_copy(src, buffers[name], sems.at[n])
            self.copies[name].start()

    def __getattr__(self, name):
        copy = self.copies.pop(name, None)
        if copy is not None:
            copy.wait()
        return self.buffers[name]

    def __getitem__(self, name):
        return getattr(self, name)

    def finish(self):
        for name in list(self.copies):
            getattr(self, name)


FRONT_W = names(lambda cw, cb, wq, wk, wv, gw, gb: None)
TAIL_W = names(lambda wo, up, upb, down, downb: None)
SAVE = names(lambda x, mixed, q, k, v, gp, att, branch, resid, n2, hid, gel, mlp, prob, decay, pad: None)


def save_shapes(g):
    t, d, ff = g.t, g.d, g.ff
    return Table(
        x=((t, d), F32),
        mixed=((t, d), BF),
        q=((t, d), BF),
        k=((t, d), BF),
        v=((t, d), BF),
        gp=((t, 128), F32),
        att=((t, d), BF),
        branch=((t, d), BF),
        resid=((t, d), F32),
        n2=((t, d), BF),
        hid=((t, ff), BF),
        gel=((t, ff), BF),
        mlp=((t, d), BF),
        prob=((t, d), BF),
        decay=((t, d), BF),
        pad=((t + 2 * g.pos, d), BF),
        cum=(((t + 127) // 128 * 128, 128), F32),
    )


def back_shapes(g):
    t, d, ff = g.t, g.d, g.ff
    return Table(
        gmlp=((t, d), BF),
        gpre=((t, ff), BF),
        gres=((t, d), F32),
        tmp1=((t, d), F32),
        tmp2=((t, d), F32),
        gbr=((t, d), BF),
        dn=((ff, 128), F32),
        upg=((d, 512), F32),
        gatt=((t, d), BF),
        dlow=((t, d), BF),
        wlow=((t, d), BF),
        ulow=((t, d), BF),
        gqkv=((t, 3 * d), BF),
        ggp=((t, 128), F32),
        gpad=((t + 2 * g.pos, d), F32),
    )


def k_first(g, s):
    c = s.meta[0]
    x, mod, turned = s.x, s.mod, s.turned
    place_tiles(g, s, 0, g.win, x)
    s.cum[g.t :, :] = jnp.zeros((s.cum.shape[0] - g.t, 128), F32)
    front(g, x, mod, 0, s, s)
    attend(g, s)

    def emit(i, value):
        s.mid[i * g.big : (i + 1) * g.big, :] = value

    tail(g, x, mod, 0, s, s, emit)
    turn(g, s.mid, pl.multiple_of(c * (HALO * g.pos), g.pos), turned)
    s.keep_mid[...] = part_of(g, turned, c)
    s.send[...] = part_of(g, turned, 1 - c).astype(BF)


def weave(g, c, keep, recv, dst):
    for i in range(g.win):
        rows = slice(i * g.own, (i + 1) * g.own)
        a = pl.multiple_of(i * g.pos + c * g.own, g.own)
        b = pl.multiple_of(i * g.pos + (1 - c) * g.own, g.own)
        dst[pl.ds(a, g.own), :] = keep[rows, :].astype(F32)
        dst[pl.ds(b, g.own), :] = recv[rows, :].astype(F32)


def k_second(g, s):
    c, tc = s.meta[0], s.meta[1]
    x, mod, turned = s.x, s.mod, s.turned
    weave(g, c, s.keep_mid, s.recv, x)
    s.cum[g.t :, :] = jnp.zeros((s.cum.shape[0] - g.t, 128), F32)
    front(g, x, mod, 8, s, s)
    attend(g, s)

    def emit(i, value):
        s.three[i * g.big : (i + 1) * g.big, :] = value

    tail(g, x, mod, 8, s, s, emit)
    turn(g, s.three, pl.multiple_of(c * (HALO * g.pos), g.pos), turned)
    at = (tc * g.tile) % g.own
    for r in range(g.own):
        rows = slice(r * g.tile, (r + 1) * g.tile)
        mine = pl.multiple_of((c * g.own + r) * g.own + at, g.tile)
        theirs = pl.multiple_of(((1 - c) * g.own + r) * g.own + at, g.tile)
        s.tile_keep[rows, :] = turned[pl.ds(mine, g.tile), :]
        s.tile_send[rows, :] = turned[pl.ds(theirs, g.tile), :]


def k_ffn_back(g, base, s):
    c, tc = s.meta[0], s.meta[1]
    if base == 0:
        weave(g, c, s.g_keep, s.g_recv, s.gout)
    else:
        rows = g.own * g.n_tr
        size = rows * g.tile
        for k in range(g.n_tc):
            src = s.near if k < g.n_tc // 2 else s.far
            at = k % (g.n_tc // 2) * size
            block = src[at : at + size, :].astype(F32).reshape(rows, g.tile, g.d)
            to = pl.ds(pl.multiple_of((tc ^ k) * size, size), size)
            s.columns[to, :] = jnp.swapaxes(block, 0, 1).reshape(size, g.d)
        s.gout[...] = s.columns[pl.ds(pl.multiple_of(c * (g.shift * rows), rows), g.t), :]
    s.small[...] = jnp.zeros((SMALL, g.d), F32)
    ffn_back(g, c, tc, s.gout, s.mod, base, s, s, s)


def k_core(g, base, s):
    c, tc = s.meta[0], s.meta[1]
    s.small[...] = s.small_in[...]
    attn_core(g, s, s)
    proj_grads(g, c, tc, s, s, 0)


def k_conv(g, base, s):
    c, tc = s.meta[0], s.meta[1]
    mixed_back(g, base // 8, s, s)
    s.small[...] = s.small_in[...]

    def emit(i, value):
        s.gin[i * g.ch : (i + 1) * g.ch, :] = value

    conv_back(g, c, s.x, s.mod, base, s, s, s, emit)
    kernel_grads(g, c, s.mod, s, s)
    turned = s.turned
    turn(g, s.gin, pl.multiple_of(c * (HALO * g.pos), g.pos), turned)
    if base:
        s.g_keep[...] = part_of(g, turned, c)
        s.g_send[...] = part_of(g, turned, 1 - c).astype(BF)
        return
    size = g.tile * g.own
    block = turned[pl.ds(pl.multiple_of(tc * size, size), size), :]
    s.tile[...] = jnp.swapaxes(block.reshape(g.tile, g.own, g.d), 0, 1).reshape(size, g.d)


def both_cores(s):
    both = s.small[...] + s.small_recv[...]
    return jnp.where(iota(both.shape, 0) == 6, s.small[...], both)


def side_by_side(g, part):
    half = g.rp // 2
    return jnp.concatenate([part[0:half, 0:192], part[half:, 0:192]], axis=1)


def k_join(g, size, small_too, s):
    bit = s.meta[2] % 2
    half = g.rp // 2
    s.sum_a[...] = s.keep_a[...] + s.recv_a[...].astype(F32)
    if size == g.rab:
        s.sum_b[...] = s.keep_b[...] + s.recv_b[...].astype(F32)
    if small_too:
        small = both_cores(s)
        s.apart[...], s.summed[...] = small[0:8, :], small[8:SMALL, :]
        end = (g.n_dp // 2) * size
        s.send[end : end + 24, :] = small[8:SMALL, :].astype(BF)
        s.send[end + 24 : end + 32, :] = small[0:8, :].astype(BF)
    for m in range(g.n_dp // 2):
        for which, dst in ((bit, s.held), (1 - bit, s.send)):
            rows = pl.ds(pl.multiple_of((2 * m + which) * g.rp, g.rp), g.rp)
            dst[m * size : m * size + g.rp, :] = s.sum_a[rows, :].astype(dst.dtype)
            if size == g.rab:
                packed = side_by_side(g, s.sum_b[rows, :])
                rest = size - g.rp - half
                if rest:
                    packed = jnp.concatenate([packed, jnp.zeros((rest, g.d), F32)], axis=0)
                dst[m * size + g.rp : (m + 1) * size, :] = packed.astype(dst.dtype)


def k_step(g, step, size, small_too, lo, extra, s):
    parts = g.n_dp >> (step + 1)
    s.total[...] = s.got[...] + s.recv[lo : lo + parts * size, :].astype(F32)
    blocks = 8 << step
    end = lo + parts * size
    if extra:
        s.send[s.send.shape[0] - extra :, :] = s.more[...]
    if small_too:
        summed = s.was_summed[...] + s.recv[end : end + 24, :].astype(F32)
        s.summed[...] = summed
        s.apart[0:blocks, :] = s.was_apart[...]
        s.apart[blocks : 2 * blocks, :] = s.recv[end + 24 : end + 24 + blocks, :].astype(F32)
    if parts == 1:
        return
    bit = (s.meta[2] // (2 << step)) % 2
    for m in range(parts // 2):
        for which, dst in ((bit, s.held), (1 - bit, s.send)):
            rows = pl.ds(pl.multiple_of((2 * m + which) * size, size), size)
            dst[m * size : (m + 1) * size, :] = s.total[rows, :].astype(dst.dtype)
    if small_too:
        end = (parts // 2) * size
        s.send[end : end + 24, :] = summed.astype(BF)
        s.send[end + 24 : end + 24 + 2 * blocks, :] = s.apart[...].astype(BF)


def k_last(g, s):
    me = s.meta[2]
    s.sum_b[...] = s.keep_b[...] + s.recv_b[...].astype(F32)
    small = both_cores(s)
    for k in range(g.n_dp):
        rows = pl.ds(pl.multiple_of((me ^ k) * g.rp, g.rp), g.rp)
        out = s.parts[k]
        out[0:SMALL, :] = small.astype(out.dtype)
        out[SMALL:, :] = side_by_side(g, s.sum_b[rows, :]).astype(out.dtype)


def finish(g, b, s, ab, proj, summed, apart):
    c, tc, me = s.meta[0], s.meta[1], s.meta[2]
    idx = c * g.n_tc + tc
    rp, rows, half = g.rp, g.rows, g.rp // 2
    acc, acct = s.acc, s.acct
    s.up_weight[b] = ab[0:rows, 0 : g.upc]
    acc[0:rp, 0:384] = ab
    acc[0:half, 384:576] = proj[:, 0:192]
    acc[half:rp, 384:576] = proj[:, 192:384]
    for n in range(1, 5):
        acct[n * 128 : (n + 1) * 128, :] = acc[:, n * 128 : (n + 1) * 128].T
    for j in range(g.ff // g.d):
        at = 192 + g.cols * j
        s.down_weight[b, :, j * rows : (j + 1) * rows] = acct[at : at + g.cols, 0:rows]
    for j, ref in enumerate((s.query, s.key, s.value, s.proj)):
        at = 384 + g.cols * j
        ref[b] = acct[at : at + g.cols, 0:rows]
    for a in range(3):
        for e in range(3):
            at = 3 * a + e if b == 0 else 3 * e + a
            s.conv_weight[a, e, b : b + 1, :] = summed[at : at + 1, :]
    s.conv_bias[b : b + 1, :] = summed[9:10, :]
    for m in range(g.ff // g.d):
        s.up_bias[b : b + 1, m * g.d : (m + 1) * g.d] = summed[10 + m : 11 + m, :]
    s.down_bias[b : b + 1, :] = summed[14:15, :]
    for h in range(6):
        s.gate_weight[h, b : b + 1, :] = summed[15 + h : 16 + h, :]
    s.row[...] = jnp.broadcast_to(summed[21:22, :], (8, g.d))
    s.gate_bias[b : b + 1, :] = s.row[0:1, 0:6]
    width = 6 * g.d // (g.n_tr * g.n_tc)
    wide = 384
    prod = jnp.zeros((rp, wide), F32)
    total = apart[0]
    for part in apart[1:]:
        total = total + part
    for m in range(6):
        s.ada_bias[b : b + 1, m * g.d : (m + 1) * g.d] = total[m : m + 1, :]
    pieces = []
    for m in range(6):
        lines = [part[m : m + 1, :] for part in apart]
        pieces.append(jnp.concatenate(lines + [jnp.zeros((-len(apart) % 8, g.d), F32)] * (len(apart) % 8 > 0), axis=0))
    s.gms[...] = jnp.concatenate(pieces, axis=1)
    full = pltpu.roll(s.gms[...], 6 * g.d - idx * width, 1)
    for k in range(g.n_dp):
        cond = s.cond[k * rp : (k + 1) * rp, :]
        prod = prod + jnp.concatenate([cond] * (wide // 128), axis=1) * full[k : k + 1, 0:wide]
    s.ada_weight[b] = prod[0:rows, 0:width]


FINAL = names(
    lambda ada_weight, ada_bias, conv_weight, conv_bias, query, key, value, proj, gate_weight, gate_bias,
    up_weight, up_bias, down_weight, down_bias: None
)
BY_ROW = names(lambda ada_bias, conv_bias, gate_bias, up_bias, down_bias: None)
INNER = names(lambda conv_weight, gate_weight: None)


def k_final_one(g, s):
    c, tc = s.meta[0], s.meta[1]
    near = (tc * g.tile) // g.own == c

    @pl.when(near)
    def _():
        s.out[0] = s.tile_keep[...].reshape(g.own, g.tile, g.d)

    @pl.when(jnp.logical_not(near))
    def _():
        s.out[0] = s.tile_recv[...].reshape(g.own, g.tile, g.d)

    s.grad[0] = s.tile[...].reshape(g.own, g.tile, g.d)
    half = g.rp // 2
    total = s.got[...]
    apart = [s.apart[8 * n : 8 * n + 8, :] for n in range(g.n_dp)]
    for k, part in enumerate(apart):
        column = jnp.broadcast_to(part[6:7, :], (128, g.d)).T
        column = pltpu.roll(column, g.d - s.meta[2] * g.rows, 0)
        s.cond[k * g.rp : (k + 1) * g.rp, :] = column[0 : g.rp, :]
    finish(g, 1, s, total[0 : g.rp, :], total[g.rp : g.rp + half, :], s.summed[...], apart)


def k_final(g, s):
    for name in FINAL:
        src, dst = s.first[name], s[name]
        if name in BY_ROW:
            dst[1:2, :] = src[1:2, :]
        elif name in INNER:
            lead = (slice(None),) * (len(dst.shape) - 2)
            dst[lead + (slice(1, 2),)] = src[lead + (slice(1, 2),)]
        else:
            dst[1] = src[1]
    ab = s.got[...]
    proj = s.parts[0][SMALL:, :]
    summed = s.parts[0][8:SMALL, :]
    apart = []
    for k, part in enumerate(s.parts):
        wide = part[...].astype(F32)
        apart.append(wide[0:8, :])
        if k:
            summed = summed + wide[8:SMALL, :]
            proj = proj + wide[SMALL:, :]
    finish(g, 0, s, ab, proj, summed, apart)


def padded_bytes(shape, dtype):
    shape = (1,) * (2 - len(shape)) + tuple(shape)
    rows, lanes = -(-shape[-2] // 16) * 16, -(-shape[-1] // 128) * 128
    return math.prod(shape[:-2]) * rows * lanes * jnp.dtype(dtype).itemsize


def call(us, kernel, ins, outs, scratch=(), weights=(), block=0, spare=VMEM_SPARE, fetch=()):
    ins = Table(ins, **dict(weights))
    ins, outs, scratch = dict(ins), dict(outs), dict(scratch)
    sources = {n: ins.pop(n) for n in fetch}
    buffers = {n: (a.shape[1:] if n in STACKED else a.shape, a.dtype) for n, a in sources.items()}
    flat, tree = jax.tree.flatten(ins)
    spread_outs = [o if isinstance(o, list) else [o] for o in outs.values()]
    flat_outs = [o for group in spread_outs for o in group]
    meta = ins.get("meta")

    def run(*refs):
        refs = list(refs)

        def take(n):
            got = refs[:n]
            del refs[:n]
            return got

        table = Table(jax.tree.unflatten(tree, take(len(flat))))
        hbm = dict(zip(sources, take(len(sources))))
        for name, ref in table.items():
            if name in STACKED:
                table[name] = ref.at[block]
        for name, o in outs.items():
            table[name] = take(len(o)) if isinstance(o, list) else take(1)[0]
        table.update(zip(scratch, take(len(scratch))))
        held = dict(zip(buffers, take(len(buffers))))
        s = Refs(table, block, hbm, held, refs[0] if refs else None)
        kernel(s)
        s.finish()

    held = [(a.shape, a.dtype) for a in flat] + flat_outs + list(scratch.values()) + list(buffers.values())
    need = sum(padded_bytes(*h) for h in held)
    results = pl.pallas_call(
        run,
        in_specs=[pl.BlockSpec(memory_space=pltpu.SMEM if a is meta else pltpu.VMEM) for a in flat]
        + [pl.BlockSpec(memory_space=pl.ANY)] * len(sources),
        out_specs=[pl.BlockSpec(memory_space=pltpu.VMEM)] * len(flat_outs),
        out_shape=[jax.ShapeDtypeStruct(*o) for o in flat_outs],
        scratch_shapes=[pltpu.VMEM(*sc) for sc in (*scratch.values(), *buffers.values())]
        + [pltpu.SemaphoreType.DMA((len(sources),))] * bool(sources),
        compiler_params=pltpu.CompilerParams(vmem_limit_bytes=need + need // 16 + spare),
        cost_estimate=pl.CostEstimate(flops=int(us * 1e9), bytes_accessed=int(us * 3e6), transcendentals=0),
    )(*flat, *sources.values())
    results = list(results)
    found = Table()
    for name, o in outs.items():
        if isinstance(o, list):
            found[name] = results[: len(o)]
            del results[: len(o)]
        else:
            found[name] = results.pop(0)
    return found


def body(
    g,
    tokens,
    condition,
    cotangent,
    ada_weight,
    ada_bias,
    conv_weight,
    conv_bias,
    query_weight,
    key_weight,
    value_weight,
    out_weight,
    gate_weight,
    gate_bias,
    up_weight,
    up_bias,
    down_weight,
    down_bias,
):
    d, ff, t = g.d, g.ff, g.t
    meta = jnp.stack(
        [lax.axis_index("tr"), lax.axis_index("tc"), lax.axis_index("dp"), jnp.int32(0)]
    ).astype(jnp.int32)

    def xor(axis, k):
        return [(i, i ^ k) for i in range(lax.axis_size(axis))]

    def other(array):
        return lax.ppermute(array, "tr", [(0, 1), (1, 0)])

    part = functools.partial
    tile, half, deep = g.own * g.tile, g.win * g.own, g.n_dp * g.rp
    shapes, backs = save_shapes(g), back_shapes(g)
    weights = Table(
        wq=query_weight,
        wk=key_weight,
        wv=value_weight,
        wo=out_weight,
        gw=jnp.transpose(gate_weight, (2, 0, 1)),
        gb=gate_bias,
        cw=jnp.transpose(conv_weight, (1, 2, 0, 3)),
        cb=conv_bias,
        up=up_weight,
        upb=up_bias,
        down=down_weight,
        downb=down_bias,
    )

    def pick(table, names):
        return {n: table[n] for n in names}

    r = call(
        1,
        part(k_prep, g),
        Table(meta=meta, tok=tokens),
        Table(tokb=((tile, d), BF), halo=((HALO * g.tile, d), BF)),
    )
    halo = other(r.halo)
    cot = call(1, part(k_cast, g), Table(cot=cotangent), Table(low=((tile, d), BF))).low
    cot_recv = other(cot)
    ext = call(
        1,
        part(k_extend, g),
        Table(meta=meta, tokb=r.tokb, halo=halo),
        Table(ext=((half // 2, d), BF)),
    ).ext
    cot = call(
        1,
        part(k_rows, g),
        Table(meta=meta, mine=cot, theirs=cot_recv),
        Table(both=((2 * tile, d), BF)),
    ).both
    ext, condition = lax.optimization_barrier((ext, condition))
    tiles = [ext] + [lax.ppermute(ext, "tc", xor("tc", k)) for k in range(1, g.n_tc)]

    def double(array, step):
        got = lax.ppermute(array, "tc", xor("tc", 1 << step))
        shape = (2 * array.shape[0], d)
        return array, got, lambda: call(1, k_stack, Table(mine=array, theirs=got), Table(both=(shape, BF))).both

    ext_done, cot = lax.optimization_barrier((ext, cot))
    stack = double(cot, 0)[2]
    mod = call(
        1,
        part(k_modulate, g),
        Table(cond=condition, ada_w=ada_weight, ada_b=ada_bias),
        Table(mod=((16, d), F32)),
    ).mod
    base_ins = Table(meta=meta, mod=mod)
    save0 = call(
        8,
        part(k_first, g),
        Table(**base_ins, tiles=tiles),
        Table(
            keep_mid=((half, d), F32),
            send=((half, d), BF),
            **pick(shapes, SAVE),
        ),
        Table(mid=((t, d), F32), turned=((g.to, d), F32), cum=shapes.cum),
        pick(weights, FRONT_W + TAIL_W),
        0,
    )
    cot, _ = lax.optimization_barrier((stack(), save0.send))
    near, far, _ = double(cot, 1)
    save1 = call(
        8,
        part(k_second, g),
        Table(**base_ins, keep_mid=save0.keep_mid, recv=other(save0.send)),
        Table(
            tile_keep=((tile, d), F32),
            tile_send=((tile, d), F32),
            **pick(shapes, SAVE),
        ),
        Table(three=((t, d), F32), turned=((g.to, d), F32), cum=shapes.cum),
        pick(weights, FRONT_W + TAIL_W),
        1,
    )
    tile_recv = other(save1.tile_send)

    def ffn(b, save, ins):
        return call(
            4,
            part(k_ffn_back, g, 8 * b),
            Table(**base_ins, **ins, **pick(save, names(lambda gel, resid, branch, mlp, n2, hid: None))),
            Table(
                gres=backs.gres,
                gbr=backs.gbr,
                keep=((deep, d), F32),
                send=((deep, d), BF),
                small=((SMALL, d), F32),
            ),
            Table(**pick(backs, names(lambda gmlp, gpre, tmp1, tmp2, dn, upg: None)), gout=((t, d), F32), **(Table(columns=((g.n_tc * 2 * tile, d), F32)) if b else Table())),
            pick(weights, names(lambda down, up: None)),
            b,
        )

    def core(b, save, f):
        return call(
            4,
            part(k_core, g, 8 * b),
            Table(
                **base_ins,
                gbr=f.gbr,
                small_in=f.small,
                **pick(save, names(lambda q, k, v, gp, prob, decay, mixed, att: None)),
            ),
            Table(
                **pick(backs, names(lambda gqkv, ggp: None)),
                keep=((deep, 256), F32),
                send=((deep, 256), BF),
                small=((SMALL, d), F32),
            ),
            pick(backs, names(lambda gatt, dlow, wlow, ulow: None)),
            pick(weights, names(lambda wo: None)),
            b,
        )

    def conv(b, save, f, e):
        ends = Table(g_keep=((half, d), F32), g_send=((half, d), BF)) if b else Table(tile=((tile, d), F32))
        return call(
            4,
            part(k_conv, g, 8 * b),
            Table(
                **base_ins,
                gres=f.gres,
                small_in=e.small,
                **pick(e, names(lambda gqkv, ggp: None)),
                **pick(save, names(lambda x, pad: None)),
            ),
            Table(**ends, small=((SMALL, d), F32)),
            Table(
                **pick(backs, names(lambda tmp1, tmp2, gpad: None)),
                gin=((t, d), F32),
                turned=((g.to, d), F32),
            ),
            pick(weights, names(lambda wq, wk, wv, gw, cw: None)),
            b,
        )

    def projections(e):
        return Table(keep_b=e.keep, recv_b=other(e.send))

    def smalls(h):
        return Table(small=h.small, small_recv=other(h.small))

    def join(f, e, h):
        size, end = g.rab if e else g.rp, 32 if h else 0
        ins = Table(meta=meta, keep_a=f.keep, recv_a=f.recv)
        outs = Table(held=((g.n_dp // 2 * size, d), F32), send=((g.n_dp // 2 * size + end, d), BF))
        scratch = Table(sum_a=((deep, d), F32))
        if e:
            ins.update(e)
            scratch = Table(scratch, sum_b=((deep, 256), F32))
        if h:
            ins.update(h)
            outs = Table(outs, apart=((8, d), F32), summed=((24, d), F32))
        found = call(1, part(k_join, g, size, h is not None), ins, outs, scratch)
        return Table(found, size=size)

    def hop(state, step):
        return Table(state, recv=lax.ppermute(state.send, "dp", xor("dp", 1 << step)))

    def take(state, step, more=None):
        size, parts = state.size, g.n_dp >> (step + 1)
        small_too = state.get(*names(lambda apart: None)) is not None
        blocks = 16 << step
        end = -(-(24 + blocks) // 16) * 16 if small_too else 0
        outs, scratch = Table(), Table()
        total = ((parts * size, d), F32)
        extra = 0 if more is None else more.shape[0]
        if parts > 1:
            outs = Table(held=((parts // 2 * size, d), F32), send=((parts // 2 * size + end + extra, d), BF))
            scratch = Table(total=total)
        else:
            outs = Table(total=total)
        ins = Table(meta=meta, got=state.held, recv=state.recv, **({} if more is None else Table(more=more)))
        if small_too:
            ins = Table(ins, was_apart=state.apart, was_summed=state.summed)
            outs = Table(outs, apart=((blocks, d), F32), summed=((24, d), F32))
        lo = state.get("lo", 0)
        return Table(call(1, part(k_step, g, step, size, small_too, lo, extra), ins, outs, scratch), size=size)

    def spread(parts):
        return [parts[0]] + [lax.ppermute(parts[k], "dp", xor("dp", k)) for k in range(1, g.n_dp)]

    def before(table, *later):
        flat, tree = jax.tree.flatten((dict(table), later))
        return Table(jax.tree.unflatten(tree, lax.optimization_barrier(flat))[0])

    f1 = ffn(1, save1, Table(near=near, far=far))
    f1 = Table(f1, recv=other(f1.send))
    e1 = core(1, save1, f1)
    e1b = projections(e1)
    h1 = conv(1, save1, f1, e1)
    g_recv = other(h1.g_send)
    h1s = smalls(h1)
    one = join(f1, e1b, None)
    h1 = before(h1, one.send)
    one = hop(one, 0)
    f0 = ffn(0, save0, Table(g_keep=h1.g_keep, g_recv=g_recv))
    f0 = Table(f0, recv=other(f0.send))
    one = take(one, 0)
    two = join(f0, None, h1s)
    f0b = before(f0, one.get(*names(lambda send: None)), two.send)
    two = hop(two, 0)
    e0 = core(0, save0, f0b)
    e0b = projections(e0)
    two = take(two, 0, one.send if g.steps > 1 else None)
    e0 = before(e0, two.get(*names(lambda send: None)))
    if g.steps > 1:
        two = hop(two, 1)
        one = Table(one, recv=two.recv, lo=two.send.shape[0] - one.send.shape[0])
    h0 = conv(0, save0, f0, e0)
    for step in range(1, g.steps):
        one, two = take(one, step), take(two, step)
        if step + 1 < g.steps:
            one, two = hop(one, step + 1), hop(two, step + 1)
    parts0 = spread(
        call(
            1,
            part(k_last, g),
            Table(meta=meta, **e0b, **smalls(h0)),
            Table(parts=[((SMALL + g.rp // 2, d), BF if k else F32) for k in range(g.n_dp)]),
            Table(sum_b=((deep, 256), F32)),
        ).parts
    )
    n_cols = g.n_tr * g.n_tc
    shards = ((2, g.cols, g.rows), F32)
    final_shapes = dict(
        zip(
            FINAL,
            (
                ((2, g.rows, 6 * d // n_cols), F32),
                ((2, 6 * d), F32),
                ((3, 3, 2, d), F32),
                ((2, d), F32),
                shards,
                shards,
                shards,
                shards,
                ((6, 2, d), F32),
                ((2, 6), F32),
                ((2, g.rows, g.upc), F32),
                ((2, ff), F32),
                ((2, g.cols, ff // g.n_dp), F32),
                ((2, d), F32),
            ),
        )
    )
    scratch = Table(acc=((128, 640), F32), acct=((640, 128), F32), row=((8, d), F32), gms=((-(-g.n_dp // 8) * 8, 6 * d), F32))
    first = call(
        3,
        part(k_final_one, g),
        Table(
            meta=meta,
            tile_keep=save1.tile_keep,
            tile_recv=tile_recv,
            tile=h0.tile,
            got=one.total,
            apart=two.apart,
            summed=two.summed,
        ),
        Table(final_shapes, out=(tokens.shape, F32), grad=(tokens.shape, F32), cond=((deep, 128), F32)),
        scratch,
        spare=6 * VMEM_SPARE,
    )
    output = first.out
    finals = call(
        3,
        part(k_final, g),
        Table(
            meta=meta,
            got=two.total,
            parts=parts0,
            cond=first.cond,
            first={n: first[n] for n in FINAL},
        ),
        final_shapes,
        scratch,
        spare=6 * VMEM_SPARE,
    )
    finals = [finals[n] for n in FINAL]
    finals[2] = jnp.transpose(finals[2], (2, 0, 1, 3))
    finals[8] = jnp.transpose(finals[8], (1, 2, 0))
    for n in (4, 5, 6, 7, 12):
        finals[n] = jnp.swapaxes(finals[n], 1, 2)
    return (output, first.grad) + tuple(finals)


def solution(mesh):
    everywhere = P()
    tiles = P("dp", "tr", "tc", None)
    cut = P(None, "dp", ("tr", "tc"))
    in_specs = (tiles, P("dp", None), tiles) + (everywhere,) * 14
    out_specs = (tiles, tiles, cut, P(), P(), P(), cut, cut, cut, cut, P(), P(), cut, P(), cut, P())

    def program(*arrays):
        g = Geo(mesh, arrays[0].shape, arrays[13].shape)
        run = functools.partial(body, g)
        return jax.shard_map(run, mesh=mesh, in_specs=in_specs, out_specs=out_specs, check_vma=False)(*arrays)

    return program
```

```python
import functools
import inspect
import math

import jax
import jax.numpy as jnp
from jax import lax
from jax.experimental import pallas as pl
from jax.experimental.pallas import tpu as pltpu
from jax.sharding import PartitionSpec as P

BF = jnp.bfloat16
F32 = jnp.float32
EPS = 1e-06
GATE_NORM = 16.0
HALO = 2
GELU_A = 0.7978845608028654
GELU_B = 0.044715
NEG = -1e30
VMEM_SPARE = 3 * 1024 * 1024
SMALL = 32


def mm(a, b):
    return jnp.dot(a, b, preferred_element_type=F32)


def mm_rt(a, b):
    return lax.dot_general(a, b, (((1,), (1,)), ((), ())), preferred_element_type=F32)


def mm_lt(a, b):
    return lax.dot_general(a, b, (((0,), (0,)), ((), ())), preferred_element_type=F32)


def hi_lo(x):
    hi = x.astype(BF)
    return hi, (x - hi.astype(F32)).astype(BF)


def normalize(x):
    center = x - jnp.mean(x, axis=-1, keepdims=True)
    rstd = lax.rsqrt(jnp.mean(center * center, axis=-1, keepdims=True) + EPS)
    return center * rstd, rstd


def normalize_back(g_y, y, rstd):
    return rstd * (
        g_y - jnp.mean(g_y, axis=-1, keepdims=True) - y * jnp.mean(g_y * y, axis=-1, keepdims=True)
    )


def iota(shape, dim):
    return lax.broadcasted_iota(jnp.int32, shape, dim)


def names(function):
    return tuple(inspect.signature(function).parameters)


class Table(dict):
    __getattr__ = dict.__getitem__


class Geo:
    def __init__(self, mesh, tokens, up):
        self.n_dp, self.n_tr, self.n_tc = (mesh.shape[a] for a in ("dp", "tr", "tc"))
        self.images, self.own, self.tile = (tokens[0] // self.n_dp, tokens[1] // self.n_tr, tokens[2] // self.n_tc)
        self.pos = tokens[2]
        self.d = tokens[3]
        self.ff = up[2]
        self.win = self.own + HALO
        self.t = self.win * self.pos
        self.to = self.own * self.pos
        self.lt = self.d // 128
        self.pairs = self.d // 128
        self.group = 64
        self.groups = self.t // self.group
        self.ch = 3 * self.pos
        self.chunks = self.t // self.ch
        self.big = 288
        self.bigs = self.t // self.big
        self.fc = 768
        self.fcs = self.ff // self.fc
        self.shift = self.pos - self.win
        self.rows = self.d // self.n_dp
        self.rp = -(-self.rows // 16) * 16
        self.rab = -(-(self.rp + self.rp // 2) // 16) * 16
        self.steps = self.n_dp.bit_length() - 1
        self.cols = self.d // (self.n_tr * self.n_tc)
        self.upc = self.ff // (self.n_tr * self.n_tc)


def kernel_taps(w, blk):
    at = slice(blk, blk + 1)
    return [[w.cw[a, b, at, :] if blk == 0 else w.cw[b, a, at, :] for b in range(3)] for a in range(3)]


def gate_rows(g, w, blk):
    heads = w.gw.shape[0]
    rows = [w.gw[h, blk : blk + 1, :] for h in range(heads)]
    return hi_lo(jnp.concatenate(rows + [jnp.zeros((128 - heads, g.d), F32)], axis=0))


def front(g, x, mod, base, w, s):
    d, pos, ch = g.d, g.pos, g.ch
    shift, scale = mod[base : base + 1, :], 1.0 + mod[base + 1 : base + 2, :]
    zero = jnp.zeros((pos, d), BF)
    s.pad[0:pos, :] = zero
    s.pad[g.t + pos : g.t + 2 * pos, :] = zero
    for i in range(g.chunks):
        rows = slice(i * ch, (i + 1) * ch)
        y, _ = normalize(x[rows, :])
        s.pad[pos + i * ch : pos + (i + 1) * ch, :] = (y * scale + shift).astype(BF)
    at = iota((ch, 1), 0) % pos
    first, last = at == 0, at == pos - 1
    taps = kernel_taps(w, base // 8)
    blk = base // 8
    bias = w.cb[blk : blk + 1, :]
    for i in range(g.chunks):
        wide = s.pad[i * ch : i * ch + ch + 2 * pos, :].astype(F32)
        lines = [wide[a * pos : a * pos + ch, :] for a in range(3)]
        v = [sum(lines[a] * taps[a][b] for a in range(3)) for b in range(3)]
        mixed = v[1] + bias
        mixed = mixed + jnp.where(first, 0.0, pltpu.roll(v[0], 1, 0))
        mixed = mixed + jnp.where(last, 0.0, pltpu.roll(v[2], ch - 1, 0))
        s.mixed[i * ch : (i + 1) * ch, :] = mixed.astype(BF)
    for out, weight in ((s.q, w.wq), (s.k, w.wk), (s.v, w.wv)):
        out[...] = mm(s.mixed[...], weight[...]).astype(BF)
    g_hi, g_lo = gate_rows(g, w, blk)
    mixed = s.mixed[...]
    heads = w.gb.shape[1]
    bias = jnp.concatenate([w.gb[blk : blk + 1, :], jnp.zeros((1, 128 - heads), F32)], axis=1)
    pre = mm_rt(mixed, g_hi) + mm_rt(mixed, g_lo) + bias
    s.gp[...] = pre
    run = (jnp.minimum(pre, 0.0) - jnp.log1p(jnp.exp(-jnp.abs(pre)))) * (1.0 / GATE_NORM)
    at = iota((g.t, 1), 0) % pos
    step = 1
    while step < pos:
        run = run + jnp.where(at >= step, pltpu.roll(run, step, 0), 0.0)
        step *= 2
    s.cum[0 : g.t, :] = run


def decay_rows(g, s):
    lane = iota((1, 128), 1)
    found = {}
    for m in range((g.t + 127) // 128):
        full = s.cum[m * 128 : (m + 1) * 128, :].T
        for j in range(g.pairs):
            one, two = full[2 * j : 2 * j + 1, :], full[2 * j + 1 : 2 * j + 2, :]
            lo_row = jnp.where(lane < 64, one, pltpu.roll(two, 64, 1))
            hi_row = jnp.where(lane < 64, pltpu.roll(one, 64, 1), two)
            found[2 * m, j] = lo_row
            found[2 * m + 1, j] = hi_row
    return found


def pair_masks(g):
    row, lane = iota((64, 128), 0), iota((64, 128), 1)
    src = lane % 64
    same = (row // g.pos) == (src // g.pos)
    return lane < 64, same & (row >= src), same & (row > src)


def split_heads(block, low_half):
    zero = jnp.zeros_like(block)
    return jnp.concatenate([jnp.where(low_half, block, zero), jnp.where(low_half, zero, block)], axis=0)


def pair_blocks(g):
    for grp in range(g.groups):
        for j in range(g.pairs):
            yield grp, slice(grp * 64, grp * 64 + 64), j, slice(j * 128, j * 128 + 128)


def pair_decay(s, source, grp, j, low_half, causal):
    rows = slice(grp * 64, grp * 64 + 64)
    ct = jnp.where(low_half, s.cum[rows, 2 * j : 2 * j + 1], s.cum[rows, 2 * j + 1 : 2 * j + 2])
    return jnp.exp(jnp.where(causal, ct - source[grp, j], NEG)) * 0.125


def attend(g, s):
    low_half, causal, _ = pair_masks(g)
    source = decay_rows(g, s)
    for grp, rows, j, lanes in pair_blocks(g):
        scores = mm_rt(s.q[rows, lanes], split_heads(s.k[rows, lanes], low_half))
        decay = pair_decay(s, source, grp, j, low_half, causal)
        s.decay[rows, lanes] = decay.astype(BF)
        s.prob[rows, lanes] = (scores * decay).astype(BF)
    for _, rows, _, lanes in pair_blocks(g):
        s.att[rows, lanes] = mm(s.prob[rows, lanes], split_heads(s.v[rows, lanes], low_half)).astype(BF)


def tail(g, x, mod, base, w, s, emit):
    hidden(g, x, mod, base, w, s)
    finish_block(g, mod, base, w, s, emit)


def hidden(g, x, mod, base, w, s):
    gate_one = mod[base + 2 : base + 3, :]
    shift, scale = mod[base + 3 : base + 4, :], 1.0 + mod[base + 4 : base + 5, :]
    for i in range(g.bigs):
        rows = slice(i * g.big, (i + 1) * g.big)
        branch = mm(s.att[rows, :], w.wo[...])
        s.branch[rows, :] = branch.astype(BF)
        resid = x[rows, :] + gate_one * branch
        s.resid[rows, :] = resid
        y, _ = normalize(resid)
        s.n2[rows, :] = (y * scale + shift).astype(BF)
    for f in range(g.fcs):
        fl = slice(f * g.fc, (f + 1) * g.fc)
        for i in range(g.bigs):
            rows = slice(i * g.big, (i + 1) * g.big)
            pre = mm(s.n2[rows, :], w.up[:, fl]) + w.upb[base // 8 : base // 8 + 1, fl]
            sq = pre * pre
            half = 0.5 * jnp.tanh(pre * (GELU_A + (GELU_A * GELU_B) * sq)) + 0.5
            hid = pre * half
            s.hid[rows, fl] = hid.astype(BF)
            inner = 2.0 * GELU_A + (6.0 * GELU_A * GELU_B) * sq
            s.gel[rows, fl] = (half + hid * (1.0 - half) * inner).astype(s.gel.dtype)


def finish_block(g, mod, base, w, s, emit):
    gate_two = mod[base + 5 : base + 6, :]
    for i in range(g.bigs):
        rows = slice(i * g.big, (i + 1) * g.big)
        mlp = mm(s.hid[rows, :], w.down[...]) + w.downb[base // 8 : base // 8 + 1, :]
        s.mlp[rows, :] = mlp.astype(s.mlp.dtype)
        emit(i, s.resid[rows, :] + gate_two * mlp)


def select_cols(width, source, half, tc, c, n_tc, lanes):
    row, lane = iota((source, 2 * half), 0), iota((source, 2 * half), 1)
    core = jnp.where(lane < half, c, 1 - c)
    inside = lane % half - lanes
    want = (core * n_tc + tc) * width + inside
    hit = (row == want) & (inside >= 0) & (inside < width)
    return jnp.where(hit, 1.0, 0.0).astype(BF)


def own_sum(g, c, ref, lanes=None):
    start = pl.multiple_of(c * (HALO * g.pos), HALO * g.pos)
    if lanes is None:
        return ref[pl.ds(start, g.to), :]
    return ref[pl.ds(start, g.to), lanes]


def colsum(a):
    return jnp.sum(a.astype(F32), axis=0, keepdims=True)


def lay(g, dst, lane0, value):
    lanes = slice(lane0, lane0 + value.shape[1])
    if g.rp == g.rows:
        dst[:, lanes] = value.astype(dst.dtype)
        return
    for n in range(g.n_dp):
        part = value[n * g.rows : (n + 1) * g.rows, :]
        pad = jnp.zeros((g.rp - g.rows, value.shape[1]), F32)
        dst[n * g.rp : (n + 1) * g.rp, lanes] = jnp.concatenate([part, pad], axis=0).astype(dst.dtype)


def ffn_back(g, c, tc, g_out, mod, base, w, s, o):
    gate_one, gate_two = mod[base + 2 : base + 3, :], mod[base + 5 : base + 6, :]
    scale = 1.0 + mod[base + 4 : base + 5, :]
    for i in range(g.bigs):
        rows = slice(i * g.big, (i + 1) * g.big)
        s.gmlp[rows, :] = (gate_two * g_out[rows, :]).astype(BF)
    for f in range(g.fcs):
        fl = slice(f * g.fc, (f + 1) * g.fc)
        for i in range(g.bigs):
            rows = slice(i * g.big, (i + 1) * g.big)
            g_hid = mm_rt(s.gmlp[rows, :], w.down[fl, :])
            s.gpre[rows, fl] = (s.gel[rows, fl].astype(F32) * g_hid).astype(BF)
    for i in range(g.bigs):
        rows = slice(i * g.big, (i + 1) * g.big)
        g_n2 = mm_rt(s.gpre[rows, :], w.up[...])
        y, rstd = normalize(s.resid[rows, :])
        g_res = g_out[rows, :] + normalize_back(g_n2 * scale, y, rstd)
        s.gres[rows, :] = g_res
        s.tmp1[rows, :] = g_n2
        s.tmp2[rows, :] = g_n2 * y
        s.gbr[rows, :] = (gate_one * g_res).astype(BF)
    own = functools.partial(own_sum, g, c)
    small = o.small
    small[2:3, :] = colsum(own(s.gres) * own(s.branch).astype(F32))
    small[3:4, :] = colsum(own(s.tmp1))
    small[4:5, :] = colsum(own(s.tmp2))
    small[5:6, :] = colsum(own(g_out) * own(s.mlp).astype(F32))
    for f in range(g.ff // g.d):
        small[18 + f : 19 + f, :] = colsum(own(s.gpre, slice(f * g.d, (f + 1) * g.d)))
    small[22:23, :] = colsum(own(s.gmlp))
    n2 = own(s.n2)
    for at, core in ((0, c), (256, 1 - c)):
        first = (core * g.n_tc + tc) * g.upc
        lanes = pl.ds(pl.multiple_of(first // 128 * 128, 128), 256)
        grads = mm_lt(n2, own(s.gpre, lanes))
        s.upg[:, at : at + 256] = jnp.where(first % 128 == 0, grads, pltpu.roll(grads, 192, 1))
    sel = mm(own(s.gmlp), select_cols(g.cols, g.d, 64, tc, c, g.n_tc, 0)).astype(BF)
    s.dn[...] = mm_lt(own(s.hid), sel)
    lane = iota((g.rows, 128), 1)
    per = g.ff // g.d
    for dd in range(g.n_dp):
        up = slice(dd * g.rows, (dd + 1) * g.rows)
        down = [s.dn[(dd * per + j) * g.rows : (dd * per + j + 1) * g.rows, :] for j in range(per)]
        for at, shift, dst in ((0, 0, o.keep), (256, 64, o.send)):
            to = slice(dd * g.rp, dd * g.rp + g.rows)
            one, two, three, four = (
                pltpu.roll(part, (lanes - shift) % 128, 1) for part, lanes in zip(down, (64, 112, 32, 80))
            )
            mid = jnp.where(lane < 112, one, two)
            dst[to, 0:128] = s.upg[up, at : at + 128].astype(dst.dtype)
            dst[to, 128:256] = jnp.where(lane < 64, s.upg[up, at + 128 : at + 256], mid).astype(dst.dtype)
            end = jnp.where(lane < 80, three, four)
            dst[to, 256:384] = jnp.where(lane < 32, two, end).astype(dst.dtype)


def attn_core(g, w, s):
    low_half, causal, strict = pair_masks(g)
    s.gatt[...] = mm_rt(s.gbr[...], w.wo[...]).astype(BF)
    row, col = iota((64, 64), 0), iota((64, 64), 1)
    later = jnp.where((row // g.pos == col // g.pos) & (col >= row), 1.0, 0.0).astype(BF)
    head_of = iota((g.d, 128), 0) // 64
    to_head = jnp.where(head_of == iota((g.d, 128), 1), 1.0, 0.0).astype(BF)
    for _, rows, _, lanes in pair_blocks(g):
        d_p = mm_rt(s.gatt[rows, lanes], split_heads(s.v[rows, lanes], low_half))
        s.dlow[rows, lanes] = (d_p * s.decay[rows, lanes].astype(F32)).astype(BF)
        s.wlow[rows, lanes] = (d_p * s.prob[rows, lanes].astype(F32)).astype(BF)
    strict3 = jnp.concatenate([strict] * g.pairs, axis=1)
    for grp in range(g.groups):
        rows = slice(grp * 64, grp * 64 + 64)
        s.ulow[rows, :] = jnp.where(strict3, mm(later, s.wlow[rows, :]), 0.0).astype(BF)
    for _, rows, j, lanes in pair_blocks(g):
        km = split_heads(s.k[rows, lanes], low_half)
        s.gqkv[rows, j * 128 : j * 128 + 128] = mm(s.dlow[rows, lanes], km).astype(BF)
    for _, rows, j, lanes in pair_blocks(g):
        both = mm_lt(s.dlow[rows, lanes], s.q[rows, lanes])
        s.gqkv[rows, g.d + j * 128 : g.d + j * 128 + 128] = jnp.where(
            low_half, both[0:64, :], both[64:128, :]
        ).astype(BF)
    for _, rows, j, lanes in pair_blocks(g):
        both = mm_lt(s.prob[rows, lanes], s.gatt[rows, lanes])
        s.gqkv[rows, 2 * g.d + j * 128 : 2 * g.d + j * 128 + 128] = jnp.where(
            low_half, both[0:64, :], both[64:128, :]
        ).astype(BF)
    g_log = mm(s.ulow[...], to_head)
    s.ggp[...] = g_log * (jax.nn.sigmoid(-s.gp[...]) * (1.0 / GATE_NORM))


def proj_grads(g, c, tc, s, o, lane0):
    own = functools.partial(own_sum, g, c)
    small = o.small
    pick_cols = select_cols(g.cols, g.d, 64, tc, c, g.n_tc, 0)
    sel = [mm(own(s.gqkv, slice(n * g.d, (n + 1) * g.d)), pick_cols).astype(BF) for n in range(3)]
    sel_out = mm(own(s.gbr), pick_cols).astype(BF)
    grads = mm_lt(own(s.mixed), jnp.concatenate(sel, axis=1))
    three = mm_lt(own(s.att), sel_out)
    zero, one, two = (grads[:, n * 128 : (n + 1) * 128] for n in range(3))
    lane = iota((g.d, 128), 1)
    for shift, dst in ((0, o.keep), (64, o.send)):
        q, k, v, out = (
            pltpu.roll(part, (lanes - shift) % 128, 1)
            for part, lanes in ((zero, 0), (one, 48), (two, 96), (three, 16))
        )
        lay(g, dst, lane0, jnp.where(lane < 48, q, jnp.where(lane < 96, k, v)))
        lay(g, dst, lane0 + 128, jnp.where(lane < 16, v, out))
    gg = own(s.ggp)
    hi, lo = hi_lo(gg)
    mixed = own(s.mixed)
    gate = mm_lt(hi, mixed) + mm_lt(lo, mixed)
    small[23:29, :] = gate[0:6, :]
    small[29:30, 0:128] = colsum(gg)
    small[29:30, 128 : g.d] = jnp.zeros((1, g.d - 128), F32)


def mixed_back(g, blk, w, s):
    pos, d = g.pos, g.d
    w_hi, w_lo = gate_rows(g, w, blk)
    zero = jnp.zeros((pos, d), F32)
    s.gpad[0:pos, :] = zero
    s.gpad[g.t + pos : g.t + 2 * pos, :] = zero
    for i in range(g.bigs):
        rows = slice(i * g.big, (i + 1) * g.big)
        hi, lo = hi_lo(s.ggp[rows, :])
        total = mm(hi, w_hi) + mm(lo, w_hi) + mm(hi, w_lo)
        for n, weight in enumerate((w.wq, w.wk, w.wv)):
            total = total + mm_rt(s.gqkv[rows, n * d : (n + 1) * d], weight[...])
        s.gpad[pos + i * g.big : pos + (i + 1) * g.big, :] = total.astype(BF).astype(F32)


def conv_back(g, c, x, mod, base, w, s, o, emit):
    pos, ch, d = g.pos, g.ch, g.d
    own = functools.partial(own_sum, g, c)
    small = o.small
    at = iota((ch, 1), 0) % pos
    first, last = at == 0, at == pos - 1
    taps = kernel_taps(w, base // 8)
    scale = 1.0 + mod[base + 1 : base + 2, :]
    for i in range(g.chunks):
        rows = slice(i * ch, (i + 1) * ch)
        lines = [s.gpad[i * ch + a * pos : i * ch + a * pos + ch, :] for a in range(3)]
        v = [sum(lines[2 - a] * taps[a][b] for a in range(3)) for b in range(3)]
        g_n = v[1]
        g_n = g_n + jnp.where(last, 0.0, pltpu.roll(v[0], ch - 1, 0))
        g_n = g_n + jnp.where(first, 0.0, pltpu.roll(v[2], 1, 0))
        y, rstd = normalize(x[rows, :])
        s.tmp1[rows, :] = g_n
        s.tmp2[rows, :] = g_n * y
        emit(i, s.gres[rows, :] + normalize_back(g_n * scale, y, rstd))
    small[0:1, :] = colsum(own(s.tmp1))
    small[1:2, :] = colsum(own(s.tmp2))


def kernel_grads(g, c, mod, s, o):
    pos, d = g.pos, g.d
    small = o.small
    oc = 4 * pos
    at = iota((oc, 1), 0) % pos
    first, last = at == 0, at == pos - 1
    sums = [jnp.zeros((8, d), F32) for _ in range(10)]
    for i in range(g.to // oc):
        start = c * (HALO * pos) + i * oc
        mid = s.gpad[pl.ds(pl.multiple_of(start + pos, pos), oc), :]
        shifted = [
            jnp.where(last, 0.0, pltpu.roll(mid, oc - 1, 0)),
            mid,
            jnp.where(first, 0.0, pltpu.roll(mid, 1, 0)),
        ]
        for a in range(3):
            line = s.pad[pl.ds(pl.multiple_of(start + a * pos, pos), oc), :].astype(F32)
            for b in range(3):
                sums[3 * a + b] = sums[3 * a + b] + jnp.sum((line * shifted[b]).reshape(oc // 8, 8, d), axis=0)
        sums[9] = sums[9] + jnp.sum(mid.reshape(oc // 8, 8, d), axis=0)
    for n in range(10):
        small[8 + n : 9 + n, :] = jnp.sum(sums[n], axis=0, keepdims=True)
    small[6:7, :] = mod[6:7, :]
    small[7:8, :] = jnp.zeros((1, d), F32)
    small[30:SMALL, :] = jnp.zeros((SMALL - 30, d), F32)


def attn_back(g, c, tc, x, mod, base, w, s, o, lane0, emit):
    attn_core(g, w, s)
    proj_grads(g, c, tc, s, o, lane0)
    mixed_back(g, base // 8, w, s)
    conv_back(g, c, x, mod, base, w, s, o, emit)
    kernel_grads(g, c, mod, s, o)


def k_prep(g, s):
    c = s.meta[0]
    t = s.tok[0].reshape(g.own * g.tile, g.d).astype(BF)
    s.tokb[...] = t
    edge = HALO * g.tile

    @pl.when(c == 0)
    def _():
        s.halo[...] = t[g.own * g.tile - edge :, :]

    @pl.when(c == 1)
    def _():
        s.halo[...] = t[0:edge, :]


def k_cast(g, s):
    s.low[...] = s.cot[0].reshape(g.own * g.tile, g.d).astype(BF)


def k_rows(g, s):
    c, size = s.meta[0], g.own * g.tile
    s.both[pl.ds(pl.multiple_of(c * size, size), size), :] = s.mine[...]
    s.both[pl.ds(pl.multiple_of((1 - c) * size, size), size), :] = s.theirs[...]


def k_stack(s):
    rows = s.mine.shape[0]
    s.both[0:rows, :] = s.mine[...]
    s.both[rows:, :] = s.theirs[...]


def k_extend(g, s):
    c = s.meta[0]
    edge = HALO * g.tile
    own = g.own * g.tile
    s.ext[pl.ds(pl.multiple_of(c * edge, edge), own), :] = s.tokb[...]
    s.ext[pl.ds(pl.multiple_of((1 - c) * own, edge), edge), :] = s.halo[...]


def k_modulate(g, s):
    mod = s.mod
    act = jax.nn.silu(s.cond[...]).astype(BF)
    rows = jnp.broadcast_to(act, (16, g.d))
    for b in range(2):
        for n in range(6):
            lanes = slice(n * g.d, (n + 1) * g.d)
            out = mm(rows, s.ada_w[b, :, lanes])[0:1, :] + s.ada_b[b : b + 1, lanes]
            mod[b * 8 + n : b * 8 + n + 1, :] = out
        mod[b * 8 + 6 : b * 8 + 7, :] = act.astype(F32)
        mod[b * 8 + 7 : b * 8 + 8, :] = jnp.zeros((1, g.d), F32)


def place_tiles(g, s, lo, lines, dst):
    tc = s.meta[1]
    for k in range(g.n_tc):
        part = s.tiles[k][lo : lo + lines * g.tile, :].astype(F32)
        off = (tc ^ k) * g.tile
        for i in range(lines):
            dst[pl.ds(pl.multiple_of(i * g.pos + off, g.tile), g.tile), :] = part[i * g.tile : (i + 1) * g.tile, :]


def turn(g, ref, start, dst):
    block = ref[pl.ds(start, g.to), :].reshape(g.own, g.pos, g.d)
    dst[...] = jnp.swapaxes(block, 0, 1).reshape(g.to, g.d)


def part_of(g, ref, core):
    return ref[pl.ds(pl.multiple_of(core * (g.shift * g.own), g.own), g.win * g.own), :]


STACKED = names(lambda wq, wk, wv, wo, up, down: None)


class Refs:
    def __init__(self, table, block, sources, buffers, sems):
        self.__dict__.update(table)
        self.buffers, self.copies = buffers, {}
        for n, (name, src) in enumerate(sources.items()):
            src = src.at[block] if name in STACKED else src
            self.copies[name] = pltpu.make_async_copy(src, buffers[name], sems.at[n])
            self.copies[name].start()

    def __getattr__(self, name):
        copy = self.copies.pop(name, None)
        if copy is not None:
            copy.wait()
        return self.buffers[name]

    def __getitem__(self, name):
        return getattr(self, name)

    def finish(self):
        for name in list(self.copies):
            getattr(self, name)


FRONT_W = names(lambda cw, cb, wq, wk, wv, gw, gb: None)
TAIL_W = names(lambda wo, up, upb, down, downb: None)
SAVE = names(lambda x, mixed, q, k, v, gp, att, branch, resid, n2, hid, gel, mlp, prob, decay, pad: None)


def save_shapes(g):
    t, d, ff = g.t, g.d, g.ff
    return Table(
        x=((t, d), F32),
        mixed=((t, d), BF),
        q=((t, d), BF),
        k=((t, d), BF),
        v=((t, d), BF),
        gp=((t, 128), F32),
        att=((t, d), BF),
        branch=((t, d), BF),
        resid=((t, d), F32),
        n2=((t, d), BF),
        hid=((t, ff), BF),
        gel=((t, ff), BF),
        mlp=((t, d), BF),
        prob=((t, d), BF),
        decay=((t, d), BF),
        pad=((t + 2 * g.pos, d), BF),
        cum=(((t + 127) // 128 * 128, 128), F32),
    )


def back_shapes(g):
    t, d, ff = g.t, g.d, g.ff
    return Table(
        gmlp=((t, d), BF),
        gpre=((t, ff), BF),
        gres=((t, d), F32),
        tmp1=((t, d), F32),
        tmp2=((t, d), F32),
        gbr=((t, d), BF),
        dn=((ff, 128), F32),
        upg=((d, 512), F32),
        gatt=((t, d), BF),
        dlow=((t, d), BF),
        wlow=((t, d), BF),
        ulow=((t, d), BF),
        gqkv=((t, 3 * d), BF),
        ggp=((t, 128), F32),
        gpad=((t + 2 * g.pos, d), F32),
    )


def k_first(g, s):
    c = s.meta[0]
    x, mod, turned = s.x, s.mod, s.turned
    place_tiles(g, s, 0, g.win, x)
    s.cum[g.t :, :] = jnp.zeros((s.cum.shape[0] - g.t, 128), F32)
    front(g, x, mod, 0, s, s)
    attend(g, s)

    def emit(i, value):
        s.mid[i * g.big : (i + 1) * g.big, :] = value

    tail(g, x, mod, 0, s, s, emit)
    turn(g, s.mid, pl.multiple_of(c * (HALO * g.pos), g.pos), turned)
    s.keep_mid[...] = part_of(g, turned, c)
    s.send[...] = part_of(g, turned, 1 - c).astype(BF)


def weave(g, c, keep, recv, dst):
    for i in range(g.win):
        rows = slice(i * g.own, (i + 1) * g.own)
        a = pl.multiple_of(i * g.pos + c * g.own, g.own)
        b = pl.multiple_of(i * g.pos + (1 - c) * g.own, g.own)
        dst[pl.ds(a, g.own), :] = keep[rows, :].astype(F32)
        dst[pl.ds(b, g.own), :] = recv[rows, :].astype(F32)


def k_second(g, s):
    weave(g, s.meta[0], s.keep_mid, s.recv, s.x)
    s.cum[g.t :, :] = jnp.zeros((s.cum.shape[0] - g.t, 128), F32)
    front(g, s.x, s.mod, 8, s, s)
    attend(g, s)
    hidden(g, s.x, s.mod, 8, s, s)


def k_second_tail(g, s):
    c, tc = s.meta[0], s.meta[1]
    mod, turned = s.mod, s.turned

    def emit(i, value):
        s.three[i * g.big : (i + 1) * g.big, :] = value

    finish_block(g, mod, 8, s, s, emit)
    turn(g, s.three, pl.multiple_of(c * (HALO * g.pos), g.pos), turned)
    at = (tc * g.tile) % g.own
    for r in range(g.own):
        rows = slice(r * g.tile, (r + 1) * g.tile)
        mine = pl.multiple_of((c * g.own + r) * g.own + at, g.tile)
        theirs = pl.multiple_of(((1 - c) * g.own + r) * g.own + at, g.tile)
        s.tile_keep[rows, :] = turned[pl.ds(mine, g.tile), :]
        s.tile_send[rows, :] = turned[pl.ds(theirs, g.tile), :]


def k_ffn_back(g, base, s):
    c, tc = s.meta[0], s.meta[1]
    if base == 0:
        weave(g, c, s.g_keep, s.g_recv, s.gout)
    else:
        rows = g.own * g.n_tr
        size = rows * g.tile
        for k in range(g.n_tc):
            half = k < g.n_tc // 2
            for core, src in ((c, s.near if half else s.far), (1 - c, s.near_other if half else s.far_other)):
                at = k % (g.n_tc // 2) * (size // 2)
                block = src[at : at + size // 2, :].astype(F32).reshape(g.own, g.tile, g.d)
                lines = jnp.swapaxes(block, 0, 1)
                for n in range(g.tile):
                    to = ((tc ^ k) * g.tile + n) * rows + core * g.own
                    s.columns[pl.ds(pl.multiple_of(to, g.own), g.own), :] = lines[n]
        s.gout[...] = s.columns[pl.ds(pl.multiple_of(c * (g.shift * rows), rows), g.t), :]
    s.small[...] = jnp.zeros((SMALL, g.d), F32)
    ffn_back(g, c, tc, s.gout, s.mod, base, s, s, s)


def k_core(g, base, s):
    c, tc = s.meta[0], s.meta[1]
    s.small[...] = s.small_in[...]
    attn_core(g, s, s)
    proj_grads(g, c, tc, s, s, 0)


def k_conv(g, base, s):
    c, tc = s.meta[0], s.meta[1]
    mixed_back(g, base // 8, s, s)
    s.small[...] = s.small_in[...]

    def emit(i, value):
        s.gin[i * g.ch : (i + 1) * g.ch, :] = value

    conv_back(g, c, s.x, s.mod, base, s, s, s, emit)
    kernel_grads(g, c, s.mod, s, s)
    turned = s.turned
    turn(g, s.gin, pl.multiple_of(c * (HALO * g.pos), g.pos), turned)
    if base:
        s.g_keep[...] = part_of(g, turned, c)
        s.g_send[...] = part_of(g, turned, 1 - c).astype(BF)
        return
    size = g.tile * g.own
    block = turned[pl.ds(pl.multiple_of(tc * size, size), size), :]
    s.tile[...] = jnp.swapaxes(block.reshape(g.tile, g.own, g.d), 0, 1).reshape(size, g.d)


def both_cores(s):
    both = s.small[...] + s.small_recv[...]
    return jnp.where(iota(both.shape, 0) == 6, s.small[...], both)


def side_by_side(g, part):
    half = g.rp // 2
    return jnp.concatenate([part[0:half, 0:192], part[half:, 0:192]], axis=1)


def k_join(g, size, small_too, s):
    bit = s.meta[2] % 2
    half = g.rp // 2
    s.sum_a[...] = s.keep_a[...] + s.recv_a[...].astype(F32)
    if size == g.rab:
        s.sum_b[...] = s.keep_b[...] + s.recv_b[...].astype(F32)
    if small_too:
        small = both_cores(s)
        s.apart[...], s.summed[...] = small[0:8, :], small[8:SMALL, :]
        end = (g.n_dp // 2) * size
        s.send[end : end + 24, :] = small[8:SMALL, :].astype(BF)
        s.send[end + 24 : end + 32, :] = small[0:8, :].astype(BF)
    for m in range(g.n_dp // 2):
        for which, dst in ((bit, s.held), (1 - bit, s.send)):
            rows = pl.ds(pl.multiple_of((2 * m + which) * g.rp, g.rp), g.rp)
            dst[m * size : m * size + g.rp, :] = s.sum_a[rows, :].astype(dst.dtype)
            if size == g.rab:
                packed = side_by_side(g, s.sum_b[rows, :])
                rest = size - g.rp - half
                if rest:
                    packed = jnp.concatenate([packed, jnp.zeros((rest, g.d), F32)], axis=0)
                dst[m * size + g.rp : (m + 1) * size, :] = packed.astype(dst.dtype)


def k_step(g, step, size, small_too, lo, extra, s):
    parts = g.n_dp >> (step + 1)
    s.total[...] = s.got[...] + s.recv[lo : lo + parts * size, :].astype(F32)
    blocks = 8 << step
    end = lo + parts * size
    if extra:
        s.send[s.send.shape[0] - extra :, :] = s.more[...]
    if small_too:
        summed = s.was_summed[...] + s.recv[end : end + 24, :].astype(F32)
        s.summed[...] = summed
        s.apart[0:blocks, :] = s.was_apart[...]
        s.apart[blocks : 2 * blocks, :] = s.recv[end + 24 : end + 24 + blocks, :].astype(F32)
    if parts == 1:
        return
    bit = (s.meta[2] // (2 << step)) % 2
    for m in range(parts // 2):
        for which, dst in ((bit, s.held), (1 - bit, s.send)):
            rows = pl.ds(pl.multiple_of((2 * m + which) * size, size), size)
            dst[m * size : (m + 1) * size, :] = s.total[rows, :].astype(dst.dtype)
    if small_too:
        end = (parts // 2) * size
        s.send[end : end + 24, :] = summed.astype(BF)
        s.send[end + 24 : end + 24 + 2 * blocks, :] = s.apart[...].astype(BF)


def k_last(g, s):
    me = s.meta[2]
    s.sum_b[...] = s.keep_b[...] + s.recv_b[...].astype(F32)
    small = both_cores(s)
    for k in range(g.n_dp):
        rows = pl.ds(pl.multiple_of((me ^ k) * g.rp, g.rp), g.rp)
        out = s.parts[k]
        out[0:SMALL, :] = small.astype(out.dtype)
        out[SMALL:, :] = side_by_side(g, s.sum_b[rows, :]).astype(out.dtype)


def finish(g, b, s, ab, proj, summed, apart):
    c, tc, me = s.meta[0], s.meta[1], s.meta[2]
    idx = c * g.n_tc + tc
    rp, rows, half = g.rp, g.rows, g.rp // 2
    acc, acct = s.acc, s.acct
    s.up_weight[b] = ab[0:rows, 0 : g.upc]
    acc[0:rp, 0:384] = ab
    acc[0:half, 384:576] = proj[:, 0:192]
    acc[half:rp, 384:576] = proj[:, 192:384]
    for n in range(1, 5):
        acct[n * 128 : (n + 1) * 128, :] = acc[:, n * 128 : (n + 1) * 128].T
    for j in range(g.ff // g.d):
        at = 192 + g.cols * j
        s.down_weight[b, :, j * rows : (j + 1) * rows] = acct[at : at + g.cols, 0:rows]
    for j, ref in enumerate((s.query, s.key, s.value, s.proj)):
        at = 384 + g.cols * j
        ref[b] = acct[at : at + g.cols, 0:rows]
    for a in range(3):
        for e in range(3):
            at = 3 * a + e if b == 0 else 3 * e + a
            s.conv_weight[a, e, b : b + 1, :] = summed[at : at + 1, :]
    s.conv_bias[b : b + 1, :] = summed[9:10, :]
    for m in range(g.ff // g.d):
        s.up_bias[b : b + 1, m * g.d : (m + 1) * g.d] = summed[10 + m : 11 + m, :]
    s.down_bias[b : b + 1, :] = summed[14:15, :]
    for h in range(6):
        s.gate_weight[h, b : b + 1, :] = summed[15 + h : 16 + h, :]
    s.row[...] = jnp.broadcast_to(summed[21:22, :], (8, g.d))
    s.gate_bias[b : b + 1, :] = s.row[0:1, 0:6]
    width = 6 * g.d // (g.n_tr * g.n_tc)
    wide = 384
    prod = jnp.zeros((rp, wide), F32)
    total = apart[0]
    for part in apart[1:]:
        total = total + part
    for m in range(6):
        s.ada_bias[b : b + 1, m * g.d : (m + 1) * g.d] = total[m : m + 1, :]
    pieces = []
    for m in range(6):
        lines = [part[m : m + 1, :] for part in apart]
        pieces.append(jnp.concatenate(lines + [jnp.zeros((-len(apart) % 8, g.d), F32)] * (len(apart) % 8 > 0), axis=0))
    s.gms[...] = jnp.concatenate(pieces, axis=1)
    full = pltpu.roll(s.gms[...], 6 * g.d - idx * width, 1)
    for k in range(g.n_dp):
        cond = s.cond[k * rp : (k + 1) * rp, :]
        prod = prod + jnp.concatenate([cond] * (wide // 128), axis=1) * full[k : k + 1, 0:wide]
    s.ada_weight[b] = prod[0:rows, 0:width]


FINAL = names(
    lambda ada_weight, ada_bias, conv_weight, conv_bias, query, key, value, proj, gate_weight, gate_bias,
    up_weight, up_bias, down_weight, down_bias: None
)
BY_ROW = names(lambda ada_bias, conv_bias, gate_bias, up_bias, down_bias: None)
INNER = names(lambda conv_weight, gate_weight: None)


def k_final_one(g, s):
    c, tc = s.meta[0], s.meta[1]
    near = (tc * g.tile) // g.own == c

    @pl.when(near)
    def _():
        s.out[0] = s.tile_keep[...].reshape(g.own, g.tile, g.d)

    @pl.when(jnp.logical_not(near))
    def _():
        s.out[0] = s.tile_recv[...].reshape(g.own, g.tile, g.d)

    s.grad[0] = s.tile[...].reshape(g.own, g.tile, g.d)
    half = g.rp // 2
    total = s.got[...]
    apart = [s.apart[8 * n : 8 * n + 8, :] for n in range(g.n_dp)]
    for k, part in enumerate(apart):
        column = jnp.broadcast_to(part[6:7, :], (128, g.d)).T
        column = pltpu.roll(column, g.d - s.meta[2] * g.rows, 0)
        s.cond[k * g.rp : (k + 1) * g.rp, :] = column[0 : g.rp, :]
    finish(g, 1, s, total[0 : g.rp, :], total[g.rp : g.rp + half, :], s.summed[...], apart)


def k_final(g, s):
    for name in FINAL:
        src, dst = s.first[name], s[name]
        if name in BY_ROW:
            dst[1:2, :] = src[1:2, :]
        elif name in INNER:
            lead = (slice(None),) * (len(dst.shape) - 2)
            dst[lead + (slice(1, 2),)] = src[lead + (slice(1, 2),)]
        else:
            dst[1] = src[1]
    ab = s.got[...]
    proj = s.parts[0][SMALL:, :]
    summed = s.parts[0][8:SMALL, :]
    apart = []
    for k, part in enumerate(s.parts):
        wide = part[...].astype(F32)
        apart.append(wide[0:8, :])
        if k:
            summed = summed + wide[8:SMALL, :]
            proj = proj + wide[SMALL:, :]
    finish(g, 0, s, ab, proj, summed, apart)


def padded_bytes(shape, dtype):
    shape = (1,) * (2 - len(shape)) + tuple(shape)
    rows, lanes = -(-shape[-2] // 16) * 16, -(-shape[-1] // 128) * 128
    return math.prod(shape[:-2]) * rows * lanes * jnp.dtype(dtype).itemsize


def call(us, kernel, ins, outs, scratch=(), weights=(), block=0, spare=VMEM_SPARE, fetch=()):
    ins = Table(ins, **dict(weights))
    ins, outs, scratch = dict(ins), dict(outs), dict(scratch)
    sources = {n: ins.pop(n) for n in fetch}
    buffers = {n: (a.shape[1:] if n in STACKED else a.shape, a.dtype) for n, a in sources.items()}
    flat, tree = jax.tree.flatten(ins)
    spread_outs = [o if isinstance(o, list) else [o] for o in outs.values()]
    flat_outs = [o for group in spread_outs for o in group]
    meta = ins.get("meta")

    def run(*refs):
        refs = list(refs)

        def take(n):
            got = refs[:n]
            del refs[:n]
            return got

        table = Table(jax.tree.unflatten(tree, take(len(flat))))
        hbm = dict(zip(sources, take(len(sources))))
        for name, ref in table.items():
            if name in STACKED:
                table[name] = ref.at[block]
        for name, o in outs.items():
            table[name] = take(len(o)) if isinstance(o, list) else take(1)[0]
        table.update(zip(scratch, take(len(scratch))))
        held = dict(zip(buffers, take(len(buffers))))
        s = Refs(table, block, hbm, held, refs[0] if refs else None)
        kernel(s)
        s.finish()

    held = [(a.shape, a.dtype) for a in flat] + flat_outs + list(scratch.values()) + list(buffers.values())
    need = sum(padded_bytes(*h) for h in held)
    results = pl.pallas_call(
        run,
        in_specs=[pl.BlockSpec(memory_space=pltpu.SMEM if a is meta else pltpu.VMEM) for a in flat]
        + [pl.BlockSpec(memory_space=pl.ANY)] * len(sources),
        out_specs=[pl.BlockSpec(memory_space=pltpu.VMEM)] * len(flat_outs),
        out_shape=[jax.ShapeDtypeStruct(*o) for o in flat_outs],
        scratch_shapes=[pltpu.VMEM(*sc) for sc in (*scratch.values(), *buffers.values())]
        + [pltpu.SemaphoreType.DMA((len(sources),))] * bool(sources),
        compiler_params=pltpu.CompilerParams(vmem_limit_bytes=need + need // 16 + spare),
        cost_estimate=pl.CostEstimate(flops=int(us * 1e9), bytes_accessed=int(us * 3e6), transcendentals=0),
    )(*flat, *sources.values())
    results = list(results)
    found = Table()
    for name, o in outs.items():
        if isinstance(o, list):
            found[name] = results[: len(o)]
            del results[: len(o)]
        else:
            found[name] = results.pop(0)
    return found


def body(
    g,
    tokens,
    condition,
    cotangent,
    ada_weight,
    ada_bias,
    conv_weight,
    conv_bias,
    query_weight,
    key_weight,
    value_weight,
    out_weight,
    gate_weight,
    gate_bias,
    up_weight,
    up_bias,
    down_weight,
    down_bias,
):
    d, ff, t = g.d, g.ff, g.t
    meta = jnp.stack(
        [lax.axis_index("tr"), lax.axis_index("tc"), lax.axis_index("dp"), jnp.int32(0)]
    ).astype(jnp.int32)

    def xor(axis, k):
        return [(i, i ^ k) for i in range(lax.axis_size(axis))]

    def other(array):
        return lax.ppermute(array, "tr", [(0, 1), (1, 0)])

    part = functools.partial
    tile, half, deep = g.own * g.tile, g.win * g.own, g.n_dp * g.rp
    shapes, backs = save_shapes(g), back_shapes(g)
    weights = Table(
        wq=query_weight,
        wk=key_weight,
        wv=value_weight,
        wo=out_weight,
        gw=jnp.transpose(gate_weight, (2, 0, 1)),
        gb=gate_bias,
        cw=jnp.transpose(conv_weight, (1, 2, 0, 3)),
        cb=conv_bias,
        up=up_weight,
        upb=up_bias,
        down=down_weight,
        downb=down_bias,
    )

    def pick(table, names):
        return {n: table[n] for n in names}

    r = call(
        1,
        part(k_prep, g),
        Table(meta=meta, tok=tokens),
        Table(tokb=((tile, d), BF), halo=((HALO * g.tile, d), BF)),
    )
    halo = other(r.halo)
    cot = call(1, part(k_cast, g), Table(cot=cotangent), Table(low=((tile, d), BF))).low
    ext = call(
        1,
        part(k_extend, g),
        Table(meta=meta, tokb=r.tokb, halo=halo),
        Table(ext=((half // 2, d), BF)),
    ).ext
    ext, condition = lax.optimization_barrier((ext, condition))
    tiles = [ext] + [lax.ppermute(ext, "tc", xor("tc", k)) for k in range(1, g.n_tc)]

    ext_done, cot = lax.optimization_barrier((ext, cot))
    cot_next = lax.ppermute(cot, "tc", xor("tc", 1))
    mod = call(
        1,
        part(k_modulate, g),
        Table(cond=condition, ada_w=ada_weight, ada_b=ada_bias),
        Table(mod=((16, d), F32)),
    ).mod
    base_ins = Table(meta=meta, mod=mod)
    save0 = call(
        8,
        part(k_first, g),
        Table(**base_ins, tiles=tiles),
        Table(
            keep_mid=((half, d), F32),
            send=((half, d), BF),
            **pick(shapes, SAVE),
        ),
        Table(mid=((t, d), F32), turned=((g.to, d), F32), cum=shapes.cum),
        pick(weights, FRONT_W + TAIL_W),
        0,
    )
    sent, cot_next = lax.optimization_barrier((save0.send, cot_next))
    near = call(1, k_stack, Table(mine=cot, theirs=cot_next), Table(both=((2 * tile, d), BF))).both
    far = lax.ppermute(near, "tc", xor("tc", 2))
    first_part = names(lambda x, mixed, q, k, v, gp, att, prob, decay, pad, branch, resid, n2, hid, gel: None)
    save1 = call(
        4,
        part(k_second, g),
        Table(**base_ins, keep_mid=save0.keep_mid, recv=other(sent)),
        pick(shapes, first_part),
        Table(cum=shapes.cum),
        pick(weights, FRONT_W + names(lambda wo, up, upb: None)),
        1,
    )
    resid, far = lax.optimization_barrier((save1.resid, far))
    near_other, far_other = other(near), other(far)
    save1 = Table(save1, resid=resid)
    save1.update(
        call(
            4,
            part(k_second_tail, g),
            Table(**base_ins, resid=resid, hid=save1.hid),
            Table(
                tile_keep=((tile, d), F32),
                tile_send=((tile, d), F32),
                **pick(shapes, [n for n in SAVE if n not in first_part]),
            ),
            Table(three=((t, d), F32), turned=((g.to, d), F32)),
            pick(weights, names(lambda down, downb: None)),
            1,
        )
    )
    tile_recv = other(save1.tile_send)

    def ffn(b, save, ins):
        return call(
            4,
            part(k_ffn_back, g, 8 * b),
            Table(**base_ins, **ins, **pick(save, names(lambda gel, resid, branch, mlp, n2, hid: None))),
            Table(
                gres=backs.gres,
                gbr=backs.gbr,
                keep=((deep, d), F32),
                send=((deep, d), BF),
                small=((SMALL, d), F32),
            ),
            Table(**pick(backs, names(lambda gmlp, gpre, tmp1, tmp2, dn, upg: None)), gout=((t, d), F32), **(Table(columns=((g.n_tc * 2 * tile, d), F32)) if b else Table())),
            pick(weights, names(lambda down, up: None)),
            b,
        )

    def core(b, save, f):
        return call(
            4,
            part(k_core, g, 8 * b),
            Table(
                **base_ins,
                gbr=f.gbr,
                small_in=f.small,
                **pick(save, names(lambda q, k, v, gp, prob, decay, mixed, att: None)),
            ),
            Table(
                **pick(backs, names(lambda gqkv, ggp: None)),
                keep=((deep, 256), F32),
                send=((deep, 256), BF),
                small=((SMALL, d), F32),
            ),
            pick(backs, names(lambda gatt, dlow, wlow, ulow: None)),
            pick(weights, names(lambda wo: None)),
            b,
        )

    def conv(b, save, f, e):
        ends = Table(g_keep=((half, d), F32), g_send=((half, d), BF)) if b else Table(tile=((tile, d), F32))
        return call(
            4,
            part(k_conv, g, 8 * b),
            Table(
                **base_ins,
                gres=f.gres,
                small_in=e.small,
                **pick(e, names(lambda gqkv, ggp: None)),
                **pick(save, names(lambda x, pad: None)),
            ),
            Table(**ends, small=((SMALL, d), F32)),
            Table(
                **pick(backs, names(lambda tmp1, tmp2, gpad: None)),
                gin=((t, d), F32),
                turned=((g.to, d), F32),
            ),
            pick(weights, names(lambda wq, wk, wv, gw, cw: None)),
            b,
        )

    def projections(e):
        return Table(keep_b=e.keep, recv_b=other(e.send))

    def smalls(h):
        return Table(small=h.small, small_recv=other(h.small))

    def join(f, e, h):
        size, end = g.rab if e else g.rp, 32 if h else 0
        ins = Table(meta=meta, keep_a=f.keep, recv_a=f.recv)
        outs = Table(held=((g.n_dp // 2 * size, d), F32), send=((g.n_dp // 2 * size + end, d), BF))
        scratch = Table(sum_a=((deep, d), F32))
        if e:
            ins.update(e)
            scratch = Table(scratch, sum_b=((deep, 256), F32))
        if h:
            ins.update(h)
            outs = Table(outs, apart=((8, d), F32), summed=((24, d), F32))
        found = call(1, part(k_join, g, size, h is not None), ins, outs, scratch)
        return Table(found, size=size)

    def hop(state, step):
        return Table(state, recv=lax.ppermute(state.send, "dp", xor("dp", 1 << step)))

    def take(state, step, more=None):
        size, parts = state.size, g.n_dp >> (step + 1)
        small_too = state.get(*names(lambda apart: None)) is not None
        blocks = 16 << step
        end = -(-(24 + blocks) // 16) * 16 if small_too else 0
        outs, scratch = Table(), Table()
        total = ((parts * size, d), F32)
        extra = 0 if more is None else more.shape[0]
        if parts > 1:
            outs = Table(held=((parts // 2 * size, d), F32), send=((parts // 2 * size + end + extra, d), BF))
            scratch = Table(total=total)
        else:
            outs = Table(total=total)
        ins = Table(meta=meta, got=state.held, recv=state.recv, **({} if more is None else Table(more=more)))
        if small_too:
            ins = Table(ins, was_apart=state.apart, was_summed=state.summed)
            outs = Table(outs, apart=((blocks, d), F32), summed=((24, d), F32))
        lo = state.get("lo", 0)
        return Table(call(1, part(k_step, g, step, size, small_too, lo, extra), ins, outs, scratch), size=size)

    def spread(parts):
        return [parts[0]] + [lax.ppermute(parts[k], "dp", xor("dp", k)) for k in range(1, g.n_dp)]

    def before(table, *later):
        flat, tree = jax.tree.flatten((dict(table), later))
        return Table(jax.tree.unflatten(tree, lax.optimization_barrier(flat))[0])

    f1 = ffn(1, save1, Table(near=near, far=far, near_other=near_other, far_other=far_other))
    f1 = Table(f1, recv=other(f1.send))
    e1 = core(1, save1, f1)
    e1b = projections(e1)
    h1 = conv(1, save1, f1, e1)
    g_recv = other(h1.g_send)
    h1s = smalls(h1)
    one = join(f1, e1b, None)
    h1 = before(h1, one.send)
    one = hop(one, 0)
    f0 = ffn(0, save0, Table(g_keep=h1.g_keep, g_recv=g_recv))
    f0 = Table(f0, recv=other(f0.send))
    one = take(one, 0)
    two = join(f0, None, h1s)
    f0b = before(f0, one.get(*names(lambda send: None)), two.send)
    two = hop(two, 0)
    e0 = core(0, save0, f0b)
    e0b = projections(e0)
    two = take(two, 0, one.send if g.steps > 1 else None)
    e0 = before(e0, two.get(*names(lambda send: None)))
    if g.steps > 1:
        two = hop(two, 1)
        one = Table(one, recv=two.recv, lo=two.send.shape[0] - one.send.shape[0])
    h0 = conv(0, save0, f0, e0)
    for step in range(1, g.steps):
        one, two = take(one, step), take(two, step)
        if step + 1 < g.steps:
            one, two = hop(one, step + 1), hop(two, step + 1)
    parts0 = spread(
        call(
            1,
            part(k_last, g),
            Table(meta=meta, **e0b, **smalls(h0)),
            Table(parts=[((SMALL + g.rp // 2, d), BF if k else F32) for k in range(g.n_dp)]),
            Table(sum_b=((deep, 256), F32)),
        ).parts
    )
    n_cols = g.n_tr * g.n_tc
    shards = ((2, g.cols, g.rows), F32)
    final_shapes = dict(
        zip(
            FINAL,
            (
                ((2, g.rows, 6 * d // n_cols), F32),
                ((2, 6 * d), F32),
                ((3, 3, 2, d), F32),
                ((2, d), F32),
                shards,
                shards,
                shards,
                shards,
                ((6, 2, d), F32),
                ((2, 6), F32),
                ((2, g.rows, g.upc), F32),
                ((2, ff), F32),
                ((2, g.cols, ff // g.n_dp), F32),
                ((2, d), F32),
            ),
        )
    )
    scratch = Table(acc=((128, 640), F32), acct=((640, 128), F32), row=((8, d), F32), gms=((-(-g.n_dp // 8) * 8, 6 * d), F32))
    first = call(
        3,
        part(k_final_one, g),
        Table(
            meta=meta,
            tile_keep=save1.tile_keep,
            tile_recv=tile_recv,
            tile=h0.tile,
            got=one.total,
            apart=two.apart,
            summed=two.summed,
        ),
        Table(final_shapes, out=(tokens.shape, F32), grad=(tokens.shape, F32), cond=((deep, 128), F32)),
        scratch,
        spare=6 * VMEM_SPARE,
    )
    output = first.out
    finals = call(
        3,
        part(k_final, g),
        Table(
            meta=meta,
            got=two.total,
            parts=parts0,
            cond=first.cond,
            first={n: first[n] for n in FINAL},
        ),
        final_shapes,
        scratch,
        spare=6 * VMEM_SPARE,
    )
    finals = [finals[n] for n in FINAL]
    finals[2] = jnp.transpose(finals[2], (2, 0, 1, 3))
    finals[8] = jnp.transpose(finals[8], (1, 2, 0))
    for n in (4, 5, 6, 7, 12):
        finals[n] = jnp.swapaxes(finals[n], 1, 2)
    return (output, first.grad) + tuple(finals)


def solution(mesh):
    everywhere = P()
    tiles = P("dp", "tr", "tc", None)
    cut = P(None, "dp", ("tr", "tc"))
    in_specs = (tiles, P("dp", None), tiles) + (everywhere,) * 14
    out_specs = (tiles, tiles, cut, P(), P(), P(), cut, cut, cut, cut, P(), P(), cut, P(), cut, P())

    def program(*arrays):
        g = Geo(mesh, arrays[0].shape, arrays[13].shape)
        run = functools.partial(body, g)
        return jax.shard_map(run, mesh=mesh, in_specs=in_specs, out_specs=out_specs, check_vma=False)(*arrays)

    return program
```

```python
import functools
import inspect
import math

import jax
import jax.numpy as jnp
from jax import lax
from jax.experimental import pallas as pl
from jax.experimental.pallas import tpu as pltpu
from jax.sharding import PartitionSpec as P

BF = jnp.bfloat16
F32 = jnp.float32
EPS = 1e-06
GATE_NORM = 16.0
HALO = 2
GELU_A = 0.7978845608028654
GELU_B = 0.044715
NEG = -1e30
VMEM_SPARE = 3 * 1024 * 1024
SMALL = 32


def mm(a, b):
    return jnp.dot(a, b, preferred_element_type=F32)


def mm_rt(a, b):
    return lax.dot_general(a, b, (((1,), (1,)), ((), ())), preferred_element_type=F32)


def mm_lt(a, b):
    return lax.dot_general(a, b, (((0,), (0,)), ((), ())), preferred_element_type=F32)


def hi_lo(x):
    hi = x.astype(BF)
    return hi, (x - hi.astype(F32)).astype(BF)


def normalize(x):
    center = x - jnp.mean(x, axis=-1, keepdims=True)
    rstd = lax.rsqrt(jnp.mean(center * center, axis=-1, keepdims=True) + EPS)
    return center * rstd, rstd


def normalize_back(g_y, y, rstd):
    return rstd * (
        g_y - jnp.mean(g_y, axis=-1, keepdims=True) - y * jnp.mean(g_y * y, axis=-1, keepdims=True)
    )


def iota(shape, dim):
    return lax.broadcasted_iota(jnp.int32, shape, dim)


def names(function):
    return tuple(inspect.signature(function).parameters)


class Table(dict):
    __getattr__ = dict.__getitem__


class Geo:
    def __init__(self, mesh, tokens, up):
        self.n_dp, self.n_tr, self.n_tc = (mesh.shape[a] for a in ("dp", "tr", "tc"))
        self.images, self.own, self.tile = (tokens[0] // self.n_dp, tokens[1] // self.n_tr, tokens[2] // self.n_tc)
        self.pos = tokens[2]
        self.d = tokens[3]
        self.ff = up[2]
        self.win = self.own + HALO
        self.t = self.win * self.pos
        self.to = self.own * self.pos
        self.lt = self.d // 128
        self.pairs = self.d // 128
        self.group = 64
        self.groups = self.t // self.group
        self.ch = 3 * self.pos
        self.chunks = self.t // self.ch
        self.big = 288
        self.bigs = self.t // self.big
        self.fc = 768
        self.fcs = self.ff // self.fc
        self.shift = self.pos - self.win
        self.rows = self.d // self.n_dp
        self.rp = -(-self.rows // 16) * 16
        self.rab = -(-(self.rp + self.rp // 2) // 16) * 16
        self.steps = self.n_dp.bit_length() - 1
        self.cols = self.d // (self.n_tr * self.n_tc)
        self.upc = self.ff // (self.n_tr * self.n_tc)


def kernel_taps(w, blk):
    at = slice(blk, blk + 1)
    return [[w.cw[a, b, at, :] if blk == 0 else w.cw[b, a, at, :] for b in range(3)] for a in range(3)]


def gate_rows(g, w, blk):
    heads = w.gw.shape[0]
    rows = [w.gw[h, blk : blk + 1, :] for h in range(heads)]
    return hi_lo(jnp.concatenate(rows + [jnp.zeros((128 - heads, g.d), F32)], axis=0))


def front(g, x, mod, base, w, s):
    d, pos, ch = g.d, g.pos, g.ch
    shift, scale = mod[base : base + 1, :], 1.0 + mod[base + 1 : base + 2, :]
    zero = jnp.zeros((pos, d), BF)
    s.pad[0:pos, :] = zero
    s.pad[g.t + pos : g.t + 2 * pos, :] = zero
    for i in range(g.chunks):
        rows = slice(i * ch, (i + 1) * ch)
        y, _ = normalize(x[rows, :])
        s.pad[pos + i * ch : pos + (i + 1) * ch, :] = (y * scale + shift).astype(BF)
    at = iota((ch, 1), 0) % pos
    first, last = at == 0, at == pos - 1
    taps = kernel_taps(w, base // 8)
    blk = base // 8
    bias = w.cb[blk : blk + 1, :]
    for i in range(g.chunks):
        wide = s.pad[i * ch : i * ch + ch + 2 * pos, :].astype(F32)
        lines = [wide[a * pos : a * pos + ch, :] for a in range(3)]
        v = [sum(lines[a] * taps[a][b] for a in range(3)) for b in range(3)]
        mixed = v[1] + bias
        mixed = mixed + jnp.where(first, 0.0, pltpu.roll(v[0], 1, 0))
        mixed = mixed + jnp.where(last, 0.0, pltpu.roll(v[2], ch - 1, 0))
        s.mixed[i * ch : (i + 1) * ch, :] = mixed.astype(BF)
    for out, weight in ((s.q, w.wq), (s.k, w.wk), (s.v, w.wv)):
        out[...] = mm(s.mixed[...], weight[...]).astype(BF)
    g_hi, g_lo = gate_rows(g, w, blk)
    mixed = s.mixed[...]
    heads = w.gb.shape[1]
    bias = jnp.concatenate([w.gb[blk : blk + 1, :], jnp.zeros((1, 128 - heads), F32)], axis=1)
    pre = mm_rt(mixed, g_hi) + mm_rt(mixed, g_lo) + bias
    s.gp[...] = pre
    run = (jnp.minimum(pre, 0.0) - jnp.log1p(jnp.exp(-jnp.abs(pre)))) * (1.0 / GATE_NORM)
    at = iota((g.t, 1), 0) % pos
    step = 1
    while step < pos:
        run = run + jnp.where(at >= step, pltpu.roll(run, step, 0), 0.0)
        step *= 2
    s.cum[0 : g.t, :] = run


def decay_rows(g, s):
    lane = iota((1, 128), 1)
    found = {}
    for m in range((g.t + 127) // 128):
        full = s.cum[m * 128 : (m + 1) * 128, :].T
        for j in range(g.pairs):
            one, two = full[2 * j : 2 * j + 1, :], full[2 * j + 1 : 2 * j + 2, :]
            lo_row = jnp.where(lane < 64, one, pltpu.roll(two, 64, 1))
            hi_row = jnp.where(lane < 64, pltpu.roll(one, 64, 1), two)
            found[2 * m, j] = lo_row
            found[2 * m + 1, j] = hi_row
    return found


def pair_masks(g):
    row, lane = iota((64, 128), 0), iota((64, 128), 1)
    src = lane % 64
    same = (row // g.pos) == (src // g.pos)
    return lane < 64, same & (row >= src), same & (row > src)


def split_heads(block, low_half):
    zero = jnp.zeros_like(block)
    return jnp.concatenate([jnp.where(low_half, block, zero), jnp.where(low_half, zero, block)], axis=0)


def pair_blocks(g):
    for grp in range(g.groups):
        for j in range(g.pairs):
            yield grp, slice(grp * 64, grp * 64 + 64), j, slice(j * 128, j * 128 + 128)


def pair_decay(s, source, grp, j, low_half, causal):
    rows = slice(grp * 64, grp * 64 + 64)
    ct = jnp.where(low_half, s.cum[rows, 2 * j : 2 * j + 1], s.cum[rows, 2 * j + 1 : 2 * j + 2])
    return jnp.exp(jnp.where(causal, ct - source[grp, j], NEG)) * 0.125


def attend(g, s):
    low_half, causal, _ = pair_masks(g)
    source = decay_rows(g, s)
    for grp, rows, j, lanes in pair_blocks(g):
        scores = mm_rt(s.q[rows, lanes], split_heads(s.k[rows, lanes], low_half))
        decay = pair_decay(s, source, grp, j, low_half, causal)
        s.decay[rows, lanes] = decay.astype(BF)
        s.prob[rows, lanes] = (scores * decay).astype(BF)
    for _, rows, _, lanes in pair_blocks(g):
        s.att[rows, lanes] = mm(s.prob[rows, lanes], split_heads(s.v[rows, lanes], low_half)).astype(BF)


def tail(g, x, mod, base, w, s, emit):
    hidden(g, x, mod, base, w, s)
    finish_block(g, mod, base, w, s, emit)


def hidden(g, x, mod, base, w, s):
    gate_one = mod[base + 2 : base + 3, :]
    shift, scale = mod[base + 3 : base + 4, :], 1.0 + mod[base + 4 : base + 5, :]
    for i in range(g.bigs):
        rows = slice(i * g.big, (i + 1) * g.big)
        branch = mm(s.att[rows, :], w.wo[...])
        s.branch[rows, :] = branch.astype(BF)
        resid = x[rows, :] + gate_one * branch
        s.resid[rows, :] = resid
        y, _ = normalize(resid)
        s.n2[rows, :] = (y * scale + shift).astype(BF)
    for f in range(g.fcs):
        fl = slice(f * g.fc, (f + 1) * g.fc)
        for i in range(g.bigs):
            rows = slice(i * g.big, (i + 1) * g.big)
            pre = mm(s.n2[rows, :], w.up[:, fl]) + w.upb[base // 8 : base // 8 + 1, fl]
            sq = pre * pre
            half = 0.5 * jnp.tanh(pre * (GELU_A + (GELU_A * GELU_B) * sq)) + 0.5
            hid = pre * half
            s.hid[rows, fl] = hid.astype(BF)
            inner = 2.0 * GELU_A + (6.0 * GELU_A * GELU_B) * sq
            s.gel[rows, fl] = (half + hid * (1.0 - half) * inner).astype(s.gel.dtype)


def finish_block(g, mod, base, w, s, emit):
    gate_two = mod[base + 5 : base + 6, :]
    for i in range(g.bigs):
        rows = slice(i * g.big, (i + 1) * g.big)
        mlp = mm(s.hid[rows, :], w.down[...]) + w.downb[base // 8 : base // 8 + 1, :]
        s.mlp[rows, :] = mlp.astype(s.mlp.dtype)
        emit(i, s.resid[rows, :] + gate_two * mlp)


def select_cols(width, source, half, tc, c, n_tc, lanes):
    row, lane = iota((source, 2 * half), 0), iota((source, 2 * half), 1)
    core = jnp.where(lane < half, c, 1 - c)
    inside = lane % half - lanes
    want = (core * n_tc + tc) * width + inside
    hit = (row == want) & (inside >= 0) & (inside < width)
    return jnp.where(hit, 1.0, 0.0).astype(BF)


def own_sum(g, c, ref, lanes=None):
    start = pl.multiple_of(c * (HALO * g.pos), HALO * g.pos)
    if lanes is None:
        return ref[pl.ds(start, g.to), :]
    return ref[pl.ds(start, g.to), lanes]


def colsum(a):
    return jnp.sum(a.astype(F32), axis=0, keepdims=True)


def lay(g, dst, lane0, value):
    lanes = slice(lane0, lane0 + value.shape[1])
    if g.rp == g.rows:
        dst[:, lanes] = value.astype(dst.dtype)
        return
    for n in range(g.n_dp):
        part = value[n * g.rows : (n + 1) * g.rows, :]
        pad = jnp.zeros((g.rp - g.rows, value.shape[1]), F32)
        dst[n * g.rp : (n + 1) * g.rp, lanes] = jnp.concatenate([part, pad], axis=0).astype(dst.dtype)


def ffn_back(g, c, tc, g_out, mod, base, w, s, o):
    gate_one, gate_two = mod[base + 2 : base + 3, :], mod[base + 5 : base + 6, :]
    scale = 1.0 + mod[base + 4 : base + 5, :]
    for i in range(g.bigs):
        rows = slice(i * g.big, (i + 1) * g.big)
        s.gmlp[rows, :] = (gate_two * g_out[rows, :]).astype(BF)
    for f in range(g.fcs):
        fl = slice(f * g.fc, (f + 1) * g.fc)
        for i in range(g.bigs):
            rows = slice(i * g.big, (i + 1) * g.big)
            g_hid = mm_rt(s.gmlp[rows, :], w.down[fl, :])
            s.gpre[rows, fl] = (s.gel[rows, fl].astype(F32) * g_hid).astype(BF)
    for i in range(g.bigs):
        rows = slice(i * g.big, (i + 1) * g.big)
        g_n2 = mm_rt(s.gpre[rows, :], w.up[...])
        y, rstd = normalize(s.resid[rows, :])
        g_res = g_out[rows, :] + normalize_back(g_n2 * scale, y, rstd)
        s.gres[rows, :] = g_res
        s.tmp1[rows, :] = g_n2
        s.tmp2[rows, :] = g_n2 * y
        s.gbr[rows, :] = (gate_one * g_res).astype(BF)
    own = functools.partial(own_sum, g, c)
    small = o.small
    small[2:3, :] = colsum(own(s.gres) * own(s.branch).astype(F32))
    small[3:4, :] = colsum(own(s.tmp1))
    small[4:5, :] = colsum(own(s.tmp2))
    small[5:6, :] = colsum(own(g_out) * own(s.mlp).astype(F32))
    for f in range(g.ff // g.d):
        small[18 + f : 19 + f, :] = colsum(own(s.gpre, slice(f * g.d, (f + 1) * g.d)))
    small[22:23, :] = colsum(own(s.gmlp))
    n2 = own(s.n2)
    for at, core in ((0, c), (256, 1 - c)):
        first = (core * g.n_tc + tc) * g.upc
        lanes = pl.ds(pl.multiple_of(first // 128 * 128, 128), 256)
        grads = mm_lt(n2, own(s.gpre, lanes))
        s.upg[:, at : at + 256] = jnp.where(first % 128 == 0, grads, pltpu.roll(grads, 192, 1))
    sel = mm(own(s.gmlp), select_cols(g.cols, g.d, 64, tc, c, g.n_tc, 0)).astype(BF)
    s.dn[...] = mm_lt(own(s.hid), sel)
    lane = iota((g.rows, 128), 1)
    per = g.ff // g.d
    for dd in range(g.n_dp):
        up = slice(dd * g.rows, (dd + 1) * g.rows)
        down = [s.dn[(dd * per + j) * g.rows : (dd * per + j + 1) * g.rows, :] for j in range(per)]
        for at, shift, dst in ((0, 0, o.keep), (256, 64, o.send)):
            to = slice(dd * g.rp, dd * g.rp + g.rows)
            one, two, three, four = (
                pltpu.roll(part, (lanes - shift) % 128, 1) for part, lanes in zip(down, (64, 112, 32, 80))
            )
            mid = jnp.where(lane < 112, one, two)
            dst[to, 0:128] = s.upg[up, at : at + 128].astype(dst.dtype)
            dst[to, 128:256] = jnp.where(lane < 64, s.upg[up, at + 128 : at + 256], mid).astype(dst.dtype)
            end = jnp.where(lane < 80, three, four)
            dst[to, 256:384] = jnp.where(lane < 32, two, end).astype(dst.dtype)


def attn_core(g, w, s):
    low_half, causal, strict = pair_masks(g)
    s.gatt[...] = mm_rt(s.gbr[...], w.wo[...]).astype(BF)
    row, col = iota((64, 64), 0), iota((64, 64), 1)
    later = jnp.where((row // g.pos == col // g.pos) & (col >= row), 1.0, 0.0).astype(BF)
    head_of = iota((g.d, 128), 0) // 64
    to_head = jnp.where(head_of == iota((g.d, 128), 1), 1.0, 0.0).astype(BF)
    for _, rows, _, lanes in pair_blocks(g):
        d_p = mm_rt(s.gatt[rows, lanes], split_heads(s.v[rows, lanes], low_half))
        s.dlow[rows, lanes] = (d_p * s.decay[rows, lanes].astype(F32)).astype(BF)
        s.wlow[rows, lanes] = (d_p * s.prob[rows, lanes].astype(F32)).astype(BF)
    strict3 = jnp.concatenate([strict] * g.pairs, axis=1)
    for grp in range(g.groups):
        rows = slice(grp * 64, grp * 64 + 64)
        s.ulow[rows, :] = jnp.where(strict3, mm(later, s.wlow[rows, :]), 0.0).astype(BF)
    for _, rows, j, lanes in pair_blocks(g):
        km = split_heads(s.k[rows, lanes], low_half)
        s.gqkv[rows, j * 128 : j * 128 + 128] = mm(s.dlow[rows, lanes], km).astype(BF)
    for _, rows, j, lanes in pair_blocks(g):
        both = mm_lt(s.dlow[rows, lanes], s.q[rows, lanes])
        s.gqkv[rows, g.d + j * 128 : g.d + j * 128 + 128] = jnp.where(
            low_half, both[0:64, :], both[64:128, :]
        ).astype(BF)
    for _, rows, j, lanes in pair_blocks(g):
        both = mm_lt(s.prob[rows, lanes], s.gatt[rows, lanes])
        s.gqkv[rows, 2 * g.d + j * 128 : 2 * g.d + j * 128 + 128] = jnp.where(
            low_half, both[0:64, :], both[64:128, :]
        ).astype(BF)
    g_log = mm(s.ulow[...], to_head)
    s.ggp[...] = g_log * (jax.nn.sigmoid(-s.gp[...]) * (1.0 / GATE_NORM))


def proj_grads(g, c, tc, s, o, lane0):
    own = functools.partial(own_sum, g, c)
    small = o.small
    pick_cols = select_cols(g.cols, g.d, 64, tc, c, g.n_tc, 0)
    sel = [mm(own(s.gqkv, slice(n * g.d, (n + 1) * g.d)), pick_cols).astype(BF) for n in range(3)]
    sel_out = mm(own(s.gbr), pick_cols).astype(BF)
    grads = mm_lt(own(s.mixed), jnp.concatenate(sel, axis=1))
    three = mm_lt(own(s.att), sel_out)
    zero, one, two = (grads[:, n * 128 : (n + 1) * 128] for n in range(3))
    lane = iota((g.d, 128), 1)
    for shift, dst in ((0, o.keep), (64, o.send)):
        q, k, v, out = (
            pltpu.roll(part, (lanes - shift) % 128, 1)
            for part, lanes in ((zero, 0), (one, 48), (two, 96), (three, 16))
        )
        lay(g, dst, lane0, jnp.where(lane < 48, q, jnp.where(lane < 96, k, v)))
        lay(g, dst, lane0 + 128, jnp.where(lane < 16, v, out))
    gg = own(s.ggp)
    hi, lo = hi_lo(gg)
    mixed = own(s.mixed)
    gate = mm_lt(hi, mixed) + mm_lt(lo, mixed)
    small[23:29, :] = gate[0:6, :]
    small[29:30, 0:128] = colsum(gg)
    small[29:30, 128 : g.d] = jnp.zeros((1, g.d - 128), F32)


def mixed_back(g, blk, w, s):
    pos, d = g.pos, g.d
    w_hi, w_lo = gate_rows(g, w, blk)
    zero = jnp.zeros((pos, d), F32)
    s.gpad[0:pos, :] = zero
    s.gpad[g.t + pos : g.t + 2 * pos, :] = zero
    for i in range(g.bigs):
        rows = slice(i * g.big, (i + 1) * g.big)
        hi, lo = hi_lo(s.ggp[rows, :])
        total = mm(hi, w_hi) + mm(lo, w_hi) + mm(hi, w_lo)
        for n, weight in enumerate((w.wq, w.wk, w.wv)):
            total = total + mm_rt(s.gqkv[rows, n * d : (n + 1) * d], weight[...])
        s.gpad[pos + i * g.big : pos + (i + 1) * g.big, :] = total.astype(BF).astype(F32)


def conv_back(g, c, x, mod, base, w, s, o, emit):
    pos, ch, d = g.pos, g.ch, g.d
    own = functools.partial(own_sum, g, c)
    small = o.small
    at = iota((ch, 1), 0) % pos
    first, last = at == 0, at == pos - 1
    taps = kernel_taps(w, base // 8)
    scale = 1.0 + mod[base + 1 : base + 2, :]
    for i in range(g.chunks):
        rows = slice(i * ch, (i + 1) * ch)
        lines = [s.gpad[i * ch + a * pos : i * ch + a * pos + ch, :] for a in range(3)]
        v = [sum(lines[2 - a] * taps[a][b] for a in range(3)) for b in range(3)]
        g_n = v[1]
        g_n = g_n + jnp.where(last, 0.0, pltpu.roll(v[0], ch - 1, 0))
        g_n = g_n + jnp.where(first, 0.0, pltpu.roll(v[2], 1, 0))
        y, rstd = normalize(x[rows, :])
        s.tmp1[rows, :] = g_n
        s.tmp2[rows, :] = g_n * y
        emit(i, s.gres[rows, :] + normalize_back(g_n * scale, y, rstd))
    small[0:1, :] = colsum(own(s.tmp1))
    small[1:2, :] = colsum(own(s.tmp2))


def kernel_grads(g, c, mod, s, o):
    pos, d = g.pos, g.d
    small = o.small
    oc = 4 * pos
    at = iota((oc, 1), 0) % pos
    first, last = at == 0, at == pos - 1
    sums = [jnp.zeros((8, d), F32) for _ in range(10)]
    for i in range(g.to // oc):
        start = c * (HALO * pos) + i * oc
        mid = s.gpad[pl.ds(pl.multiple_of(start + pos, pos), oc), :]
        shifted = [
            jnp.where(last, 0.0, pltpu.roll(mid, oc - 1, 0)),
            mid,
            jnp.where(first, 0.0, pltpu.roll(mid, 1, 0)),
        ]
        for a in range(3):
            line = s.pad[pl.ds(pl.multiple_of(start + a * pos, pos), oc), :].astype(F32)
            for b in range(3):
                sums[3 * a + b] = sums[3 * a + b] + jnp.sum((line * shifted[b]).reshape(oc // 8, 8, d), axis=0)
        sums[9] = sums[9] + jnp.sum(mid.reshape(oc // 8, 8, d), axis=0)
    for n in range(10):
        small[8 + n : 9 + n, :] = jnp.sum(sums[n], axis=0, keepdims=True)
    small[6:7, :] = mod[6:7, :]
    small[7:8, :] = jnp.zeros((1, d), F32)
    small[30:SMALL, :] = jnp.zeros((SMALL - 30, d), F32)


def attn_back(g, c, tc, x, mod, base, w, s, o, lane0, emit):
    attn_core(g, w, s)
    proj_grads(g, c, tc, s, o, lane0)
    mixed_back(g, base // 8, w, s)
    conv_back(g, c, x, mod, base, w, s, o, emit)
    kernel_grads(g, c, mod, s, o)


def k_prep(g, s):
    c = s.meta[0]
    t = s.tok[0].reshape(g.own * g.tile, g.d).astype(BF)
    s.tokb[...] = t
    edge = HALO * g.tile

    @pl.when(c == 0)
    def _():
        s.halo[...] = t[g.own * g.tile - edge :, :]

    @pl.when(c == 1)
    def _():
        s.halo[...] = t[0:edge, :]


def k_cast(g, s):
    s.low[...] = s.cot[0].reshape(g.own * g.tile, g.d).astype(BF)


def k_rows(g, s):
    c, size = s.meta[0], g.own * g.tile
    s.both[pl.ds(pl.multiple_of(c * size, size), size), :] = s.mine[...]
    s.both[pl.ds(pl.multiple_of((1 - c) * size, size), size), :] = s.theirs[...]


def k_stack(s):
    rows = s.mine.shape[0]
    s.both[0:rows, :] = s.mine[...]
    s.both[rows:, :] = s.theirs[...]


def k_extend(g, s):
    c = s.meta[0]
    edge = HALO * g.tile
    own = g.own * g.tile
    s.ext[pl.ds(pl.multiple_of(c * edge, edge), own), :] = s.tokb[...]
    s.ext[pl.ds(pl.multiple_of((1 - c) * own, edge), edge), :] = s.halo[...]


def k_modulate(g, s):
    mod = s.mod
    act = jax.nn.silu(s.cond[...]).astype(BF)
    rows = jnp.broadcast_to(act, (16, g.d))
    for b in range(2):
        for n in range(6):
            lanes = slice(n * g.d, (n + 1) * g.d)
            out = mm(rows, s.ada_w[b, :, lanes])[0:1, :] + s.ada_b[b : b + 1, lanes]
            mod[b * 8 + n : b * 8 + n + 1, :] = out
        mod[b * 8 + 6 : b * 8 + 7, :] = act.astype(F32)
        mod[b * 8 + 7 : b * 8 + 8, :] = jnp.zeros((1, g.d), F32)


def place_tiles(g, s, lo, lines, dst):
    tc = s.meta[1]
    for k in range(g.n_tc):
        part = s.tiles[k][lo : lo + lines * g.tile, :].astype(F32)
        off = (tc ^ k) * g.tile
        for i in range(lines):
            dst[pl.ds(pl.multiple_of(i * g.pos + off, g.tile), g.tile), :] = part[i * g.tile : (i + 1) * g.tile, :]


def turn(g, ref, start, dst):
    block = ref[pl.ds(start, g.to), :].reshape(g.own, g.pos, g.d)
    dst[...] = jnp.swapaxes(block, 0, 1).reshape(g.to, g.d)


def part_of(g, ref, core):
    return ref[pl.ds(pl.multiple_of(core * (g.shift * g.own), g.own), g.win * g.own), :]


STACKED = names(lambda wq, wk, wv, wo, up, down: None)


class Refs:
    def __init__(self, table, block, sources, buffers, sems):
        self.__dict__.update(table)
        self.buffers, self.copies = buffers, {}
        for n, (name, src) in enumerate(sources.items()):
            src = src.at[block] if name in STACKED else src
            self.copies[name] = pltpu.make_async_copy(src, buffers[name], sems.at[n])
            self.copies[name].start()

    def __getattr__(self, name):
        copy = self.copies.pop(name, None)
        if copy is not None:
            copy.wait()
        return self.buffers[name]

    def __getitem__(self, name):
        return getattr(self, name)

    def finish(self):
        for name in list(self.copies):
            getattr(self, name)


FRONT_W = names(lambda cw, cb, wq, wk, wv, gw, gb: None)
TAIL_W = names(lambda wo, up, upb, down, downb: None)
SAVE = names(lambda x, mixed, q, k, v, gp, att, branch, resid, n2, hid, gel, mlp, prob, decay, pad: None)


def save_shapes(g):
    t, d, ff = g.t, g.d, g.ff
    return Table(
        x=((t, d), F32),
        mixed=((t, d), BF),
        q=((t, d), BF),
        k=((t, d), BF),
        v=((t, d), BF),
        gp=((t, 128), F32),
        att=((t, d), BF),
        branch=((t, d), BF),
        resid=((t, d), F32),
        n2=((t, d), BF),
        hid=((t, ff), BF),
        gel=((t, ff), BF),
        mlp=((t, d), BF),
        prob=((t, d), BF),
        decay=((t, d), BF),
        pad=((t + 2 * g.pos, d), BF),
        cum=(((t + 127) // 128 * 128, 128), F32),
    )


def back_shapes(g):
    t, d, ff = g.t, g.d, g.ff
    return Table(
        gmlp=((t, d), BF),
        gpre=((t, ff), BF),
        gres=((t, d), F32),
        tmp1=((t, d), F32),
        tmp2=((t, d), F32),
        gbr=((t, d), BF),
        dn=((ff, 128), F32),
        upg=((d, 512), F32),
        gatt=((t, d), BF),
        dlow=((t, d), BF),
        wlow=((t, d), BF),
        ulow=((t, d), BF),
        gqkv=((t, 3 * d), BF),
        ggp=((t, 128), F32),
        gpad=((t + 2 * g.pos, d), F32),
    )


def k_first(g, s):
    c = s.meta[0]
    x, mod, turned = s.x, s.mod, s.turned
    place_tiles(g, s, 0, g.win, x)
    s.cum[g.t :, :] = jnp.zeros((s.cum.shape[0] - g.t, 128), F32)
    front(g, x, mod, 0, s, s)
    attend(g, s)

    def emit(i, value):
        s.mid[i * g.big : (i + 1) * g.big, :] = value

    tail(g, x, mod, 0, s, s, emit)
    turn(g, s.mid, pl.multiple_of(c * (HALO * g.pos), g.pos), turned)
    s.keep_mid[...] = part_of(g, turned, c)
    s.send[...] = part_of(g, turned, 1 - c).astype(BF)


def weave(g, c, keep, recv, dst):
    for i in range(g.win):
        rows = slice(i * g.own, (i + 1) * g.own)
        a = pl.multiple_of(i * g.pos + c * g.own, g.own)
        b = pl.multiple_of(i * g.pos + (1 - c) * g.own, g.own)
        dst[pl.ds(a, g.own), :] = keep[rows, :].astype(F32)
        dst[pl.ds(b, g.own), :] = recv[rows, :].astype(F32)


def k_second(g, s):
    weave(g, s.meta[0], s.keep_mid, s.recv, s.x)
    s.cum[g.t :, :] = jnp.zeros((s.cum.shape[0] - g.t, 128), F32)
    front(g, s.x, s.mod, 8, s, s)
    attend(g, s)
    hidden(g, s.x, s.mod, 8, s, s)


def k_second_tail(g, s):
    c, tc = s.meta[0], s.meta[1]
    mod, turned = s.mod, s.turned

    def emit(i, value):
        s.three[i * g.big : (i + 1) * g.big, :] = value

    finish_block(g, mod, 8, s, s, emit)
    turn(g, s.three, pl.multiple_of(c * (HALO * g.pos), g.pos), turned)
    at = (tc * g.tile) % g.own
    for r in range(g.own):
        rows = slice(r * g.tile, (r + 1) * g.tile)
        mine = pl.multiple_of((c * g.own + r) * g.own + at, g.tile)
        theirs = pl.multiple_of(((1 - c) * g.own + r) * g.own + at, g.tile)
        s.tile_keep[rows, :] = turned[pl.ds(mine, g.tile), :]
        s.tile_send[rows, :] = turned[pl.ds(theirs, g.tile), :]


def k_ffn_back(g, base, s):
    c, tc = s.meta[0], s.meta[1]
    if base == 0:
        weave(g, c, s.g_keep, s.g_recv, s.gout)
    else:
        rows = g.own * g.n_tr
        size = rows * g.tile
        for k in range(g.n_tc):
            half = k < g.n_tc // 2
            for core, src in ((c, s.near if half else s.far), (1 - c, s.near_other if half else s.far_other)):
                at = k % (g.n_tc // 2) * (size // 2)
                block = src[at : at + size // 2, :].astype(F32).reshape(g.own, g.tile, g.d)
                lines = jnp.swapaxes(block, 0, 1)
                for n in range(g.tile):
                    to = ((tc ^ k) * g.tile + n) * rows + core * g.own
                    s.columns[pl.ds(pl.multiple_of(to, g.own), g.own), :] = lines[n]
        s.gout[...] = s.columns[pl.ds(pl.multiple_of(c * (g.shift * rows), rows), g.t), :]
    s.small[...] = jnp.zeros((SMALL, g.d), F32)
    ffn_back(g, c, tc, s.gout, s.mod, base, s, s, s)


def k_core(g, base, s):
    c, tc = s.meta[0], s.meta[1]
    s.small[...] = s.small_in[...]
    attn_core(g, s, s)
    proj_grads(g, c, tc, s, s, 0)


def k_conv(g, base, s):
    c, tc = s.meta[0], s.meta[1]
    mixed_back(g, base // 8, s, s)
    s.small[...] = s.small_in[...]

    def emit(i, value):
        s.gin[i * g.ch : (i + 1) * g.ch, :] = value

    conv_back(g, c, s.x, s.mod, base, s, s, s, emit)
    kernel_grads(g, c, s.mod, s, s)
    turned = s.turned
    turn(g, s.gin, pl.multiple_of(c * (HALO * g.pos), g.pos), turned)
    if base:
        s.g_keep[...] = part_of(g, turned, c)
        s.g_send[...] = part_of(g, turned, 1 - c).astype(BF)
        return
    size = g.tile * g.own
    block = turned[pl.ds(pl.multiple_of(tc * size, size), size), :]
    s.tile[...] = jnp.swapaxes(block.reshape(g.tile, g.own, g.d), 0, 1).reshape(size, g.d)


def both_cores(s):
    both = s.small[...] + s.small_recv[...]
    return jnp.where(iota(both.shape, 0) == 6, s.small[...], both)


def side_by_side(g, part):
    half = g.rp // 2
    return jnp.concatenate([part[0:half, 0:192], part[half:, 0:192]], axis=1)


def k_join(g, size, small_too, s):
    bit = s.meta[2] % 2
    half = g.rp // 2
    s.sum_a[...] = s.keep_a[...] + s.recv_a[...].astype(F32)
    if size == g.rab:
        s.sum_b[...] = s.keep_b[...] + s.recv_b[...].astype(F32)
    if small_too:
        small = both_cores(s)
        s.apart[...], s.summed[...] = small[0:8, :], small[8:SMALL, :]
        end = (g.n_dp // 2) * size
        s.send[end : end + 24, :] = small[8:SMALL, :].astype(BF)
        s.send[end + 24 : end + 32, :] = small[0:8, :].astype(BF)
    for m in range(g.n_dp // 2):
        for which, dst in ((bit, s.held), (1 - bit, s.send)):
            rows = pl.ds(pl.multiple_of((2 * m + which) * g.rp, g.rp), g.rp)
            dst[m * size : m * size + g.rp, :] = s.sum_a[rows, :].astype(dst.dtype)
            if size == g.rab:
                packed = side_by_side(g, s.sum_b[rows, :])
                rest = size - g.rp - half
                if rest:
                    packed = jnp.concatenate([packed, jnp.zeros((rest, g.d), F32)], axis=0)
                dst[m * size + g.rp : (m + 1) * size, :] = packed.astype(dst.dtype)


def k_step(g, step, size, small_too, lo, extra, s):
    parts = g.n_dp >> (step + 1)
    s.total[...] = s.got[...] + s.recv[lo : lo + parts * size, :].astype(F32)
    blocks = 8 << step
    end = lo + parts * size
    if extra:
        s.send[s.send.shape[0] - extra :, :] = s.more[...]
    if small_too:
        summed = s.was_summed[...] + s.recv[end : end + 24, :].astype(F32)
        s.summed[...] = summed
        s.apart[0:blocks, :] = s.was_apart[...]
        s.apart[blocks : 2 * blocks, :] = s.recv[end + 24 : end + 24 + blocks, :].astype(F32)
    if parts == 1:
        return
    bit = (s.meta[2] // (2 << step)) % 2
    for m in range(parts // 2):
        for which, dst in ((bit, s.held), (1 - bit, s.send)):
            rows = pl.ds(pl.multiple_of((2 * m + which) * size, size), size)
            dst[m * size : (m + 1) * size, :] = s.total[rows, :].astype(dst.dtype)
    if small_too:
        end = (parts // 2) * size
        s.send[end : end + 24, :] = summed.astype(BF)
        s.send[end + 24 : end + 24 + 2 * blocks, :] = s.apart[...].astype(BF)


def k_last(g, s):
    me = s.meta[2]
    s.sum_b[...] = s.keep_b[...] + s.recv_b[...].astype(F32)
    small = both_cores(s)
    for k in range(g.n_dp):
        rows = pl.ds(pl.multiple_of((me ^ k) * g.rp, g.rp), g.rp)
        out = s.parts[k]
        out[0:SMALL, :] = small.astype(out.dtype)
        out[SMALL:, :] = side_by_side(g, s.sum_b[rows, :]).astype(out.dtype)


def finish(g, b, s, ab, proj, summed, apart):
    c, tc, me = s.meta[0], s.meta[1], s.meta[2]
    idx = c * g.n_tc + tc
    rp, rows, half = g.rp, g.rows, g.rp // 2
    acc, acct = s.acc, s.acct
    s.up_weight[b] = ab[0:rows, 0 : g.upc]
    acc[0:rp, 0:384] = ab
    acc[0:half, 384:576] = proj[:, 0:192]
    acc[half:rp, 384:576] = proj[:, 192:384]
    for n in range(1, 5):
        acct[n * 128 : (n + 1) * 128, :] = acc[:, n * 128 : (n + 1) * 128].T
    for j in range(g.ff // g.d):
        at = 192 + g.cols * j
        s.down_weight[b, :, j * rows : (j + 1) * rows] = acct[at : at + g.cols, 0:rows]
    for j, ref in enumerate((s.query, s.key, s.value, s.proj)):
        at = 384 + g.cols * j
        ref[b] = acct[at : at + g.cols, 0:rows]
    for a in range(3):
        for e in range(3):
            at = 3 * a + e if b == 0 else 3 * e + a
            s.conv_weight[a, e, b : b + 1, :] = summed[at : at + 1, :]
    s.conv_bias[b : b + 1, :] = summed[9:10, :]
    for m in range(g.ff // g.d):
        s.up_bias[b : b + 1, m * g.d : (m + 1) * g.d] = summed[10 + m : 11 + m, :]
    s.down_bias[b : b + 1, :] = summed[14:15, :]
    for h in range(6):
        s.gate_weight[h, b : b + 1, :] = summed[15 + h : 16 + h, :]
    s.row[...] = jnp.broadcast_to(summed[21:22, :], (8, g.d))
    s.gate_bias[b : b + 1, :] = s.row[0:1, 0:6]
    width = 6 * g.d // (g.n_tr * g.n_tc)
    wide = 384
    prod = jnp.zeros((rp, wide), F32)
    total = apart[0]
    for part in apart[1:]:
        total = total + part
    for m in range(6):
        s.ada_bias[b : b + 1, m * g.d : (m + 1) * g.d] = total[m : m + 1, :]
    pieces = []
    for m in range(6):
        lines = [part[m : m + 1, :] for part in apart]
        pieces.append(jnp.concatenate(lines + [jnp.zeros((-len(apart) % 8, g.d), F32)] * (len(apart) % 8 > 0), axis=0))
    s.gms[...] = jnp.concatenate(pieces, axis=1)
    full = pltpu.roll(s.gms[...], 6 * g.d - idx * width, 1)
    for k in range(g.n_dp):
        cond = s.cond[k * rp : (k + 1) * rp, :]
        prod = prod + jnp.concatenate([cond] * (wide // 128), axis=1) * full[k : k + 1, 0:wide]
    s.ada_weight[b] = prod[0:rows, 0:width]


FINAL = names(
    lambda ada_weight, ada_bias, conv_weight, conv_bias, query, key, value, proj, gate_weight, gate_bias,
    up_weight, up_bias, down_weight, down_bias: None
)
BY_ROW = names(lambda ada_bias, conv_bias, gate_bias, up_bias, down_bias: None)
INNER = names(lambda conv_weight, gate_weight: None)


def k_final_one(g, s):
    c, tc = s.meta[0], s.meta[1]
    near = (tc * g.tile) // g.own == c

    @pl.when(near)
    def _():
        s.out[0] = s.tile_keep[...].reshape(g.own, g.tile, g.d)

    @pl.when(jnp.logical_not(near))
    def _():
        s.out[0] = s.tile_recv[...].reshape(g.own, g.tile, g.d)

    s.grad[0] = s.tile[...].reshape(g.own, g.tile, g.d)
    half = g.rp // 2
    total = s.got[...]
    apart = [s.apart[8 * n : 8 * n + 8, :] for n in range(g.n_dp)]
    for k, part in enumerate(apart):
        column = jnp.broadcast_to(part[6:7, :], (128, g.d)).T
        column = pltpu.roll(column, g.d - s.meta[2] * g.rows, 0)
        s.cond[k * g.rp : (k + 1) * g.rp, :] = column[0 : g.rp, :]
    finish(g, 1, s, total[0 : g.rp, :], total[g.rp : g.rp + half, :], s.summed[...], apart)


def k_final(g, s):
    for name in FINAL:
        src, dst = s.first[name], s[name]
        if name in BY_ROW:
            dst[1:2, :] = src[1:2, :]
        elif name in INNER:
            lead = (slice(None),) * (len(dst.shape) - 2)
            dst[lead + (slice(1, 2),)] = src[lead + (slice(1, 2),)]
        else:
            dst[1] = src[1]
    ab = s.got[...]
    proj = s.parts[0][SMALL:, :]
    summed = s.parts[0][8:SMALL, :]
    apart = []
    for k, part in enumerate(s.parts):
        wide = part[...].astype(F32)
        apart.append(wide[0:8, :])
        if k:
            summed = summed + wide[8:SMALL, :]
            proj = proj + wide[SMALL:, :]
    finish(g, 0, s, ab, proj, summed, apart)


def padded_bytes(shape, dtype):
    shape = (1,) * (2 - len(shape)) + tuple(shape)
    rows, lanes = -(-shape[-2] // 16) * 16, -(-shape[-1] // 128) * 128
    return math.prod(shape[:-2]) * rows * lanes * jnp.dtype(dtype).itemsize


def call(us, kernel, ins, outs, scratch=(), weights=(), block=0, spare=VMEM_SPARE, fetch=()):
    ins = Table(ins, **dict(weights))
    ins, outs, scratch = dict(ins), dict(outs), dict(scratch)
    sources = {n: ins.pop(n) for n in fetch}
    buffers = {n: (a.shape[1:] if n in STACKED else a.shape, a.dtype) for n, a in sources.items()}
    flat, tree = jax.tree.flatten(ins)
    spread_outs = [o if isinstance(o, list) else [o] for o in outs.values()]
    flat_outs = [o for group in spread_outs for o in group]
    meta = ins.get("meta")

    def run(*refs):
        refs = list(refs)

        def take(n):
            got = refs[:n]
            del refs[:n]
            return got

        table = Table(jax.tree.unflatten(tree, take(len(flat))))
        hbm = dict(zip(sources, take(len(sources))))
        for name, ref in table.items():
            if name in STACKED:
                table[name] = ref.at[block]
        for name, o in outs.items():
            table[name] = take(len(o)) if isinstance(o, list) else take(1)[0]
        table.update(zip(scratch, take(len(scratch))))
        held = dict(zip(buffers, take(len(buffers))))
        s = Refs(table, block, hbm, held, refs[0] if refs else None)
        kernel(s)
        s.finish()

    held = [(a.shape, a.dtype) for a in flat] + flat_outs + list(scratch.values()) + list(buffers.values())
    need = sum(padded_bytes(*h) for h in held)
    results = pl.pallas_call(
        run,
        in_specs=[pl.BlockSpec(memory_space=pltpu.SMEM if a is meta else pltpu.VMEM) for a in flat]
        + [pl.BlockSpec(memory_space=pl.ANY)] * len(sources),
        out_specs=[pl.BlockSpec(memory_space=pltpu.VMEM)] * len(flat_outs),
        out_shape=[jax.ShapeDtypeStruct(*o) for o in flat_outs],
        scratch_shapes=[pltpu.VMEM(*sc) for sc in (*scratch.values(), *buffers.values())]
        + [pltpu.SemaphoreType.DMA((len(sources),))] * bool(sources),
        compiler_params=pltpu.CompilerParams(vmem_limit_bytes=need + need // 16 + spare),
        cost_estimate=pl.CostEstimate(flops=int(us * 1e9), bytes_accessed=int(us * 3e6), transcendentals=0),
    )(*flat, *sources.values())
    results = list(results)
    found = Table()
    for name, o in outs.items():
        if isinstance(o, list):
            found[name] = results[: len(o)]
            del results[: len(o)]
        else:
            found[name] = results.pop(0)
    return found


def body(
    g,
    tokens,
    condition,
    cotangent,
    ada_weight,
    ada_bias,
    conv_weight,
    conv_bias,
    query_weight,
    key_weight,
    value_weight,
    out_weight,
    gate_weight,
    gate_bias,
    up_weight,
    up_bias,
    down_weight,
    down_bias,
):
    d, ff, t = g.d, g.ff, g.t
    meta = jnp.stack(
        [lax.axis_index("tr"), lax.axis_index("tc"), lax.axis_index("dp"), jnp.int32(0)]
    ).astype(jnp.int32)

    def xor(axis, k):
        return [(i, i ^ k) for i in range(lax.axis_size(axis))]

    def other(array):
        return lax.ppermute(array, "tr", [(0, 1), (1, 0)])

    part = functools.partial
    tile, half, deep = g.own * g.tile, g.win * g.own, g.n_dp * g.rp
    shapes, backs = save_shapes(g), back_shapes(g)
    weights = Table(
        wq=query_weight,
        wk=key_weight,
        wv=value_weight,
        wo=out_weight,
        gw=jnp.transpose(gate_weight, (2, 0, 1)),
        gb=gate_bias,
        cw=jnp.transpose(conv_weight, (1, 2, 0, 3)),
        cb=conv_bias,
        up=up_weight,
        upb=up_bias,
        down=down_weight,
        downb=down_bias,
    )

    def pick(table, names):
        return {n: table[n] for n in names}

    r = call(
        1,
        part(k_prep, g),
        Table(meta=meta, tok=tokens),
        Table(tokb=((tile, d), BF), halo=((HALO * g.tile, d), BF)),
    )
    halo = other(r.halo)
    cot = call(1, part(k_cast, g), Table(cot=cotangent), Table(low=((tile, d), BF))).low
    ext = call(
        1,
        part(k_extend, g),
        Table(meta=meta, tokb=r.tokb, halo=halo),
        Table(ext=((half // 2, d), BF)),
    ).ext
    ext, condition = lax.optimization_barrier((ext, condition))
    tiles = [ext] + [lax.ppermute(ext, "tc", xor("tc", k)) for k in range(1, g.n_tc)]

    ext_done, cot = lax.optimization_barrier((ext, cot))
    cot_next = lax.ppermute(cot, "tc", xor("tc", 1))
    mod = call(
        1,
        part(k_modulate, g),
        Table(cond=condition, ada_w=ada_weight, ada_b=ada_bias),
        Table(mod=((16, d), F32)),
    ).mod
    base_ins = Table(meta=meta, mod=mod)
    save0 = call(
        8,
        part(k_first, g),
        Table(**base_ins, tiles=tiles),
        Table(
            keep_mid=((half, d), F32),
            send=((half, d), BF),
            **pick(shapes, SAVE),
        ),
        Table(mid=((t, d), F32), turned=((g.to, d), F32), cum=shapes.cum),
        pick(weights, FRONT_W + TAIL_W),
        0,
    )
    sent, cot_next = lax.optimization_barrier((save0.send, cot_next))
    near = call(1, k_stack, Table(mine=cot, theirs=cot_next), Table(both=((2 * tile, d), BF))).both
    far = lax.ppermute(near, "tc", xor("tc", 2))
    first_part = names(lambda x, mixed, q, k, v, gp, att, prob, decay, pad, branch, resid, n2, hid, gel: None)
    save1 = call(
        4,
        part(k_second, g),
        Table(**base_ins, keep_mid=save0.keep_mid, recv=other(sent)),
        pick(shapes, first_part),
        Table(cum=shapes.cum),
        pick(weights, FRONT_W + names(lambda wo, up, upb: None)),
        1,
    )
    resid, far = lax.optimization_barrier((save1.resid, far))
    near_other, far_other = other(near), other(far)
    save1 = Table(save1, resid=resid)
    save1.update(
        call(
            4,
            part(k_second_tail, g),
            Table(**base_ins, resid=resid, hid=save1.hid),
            Table(
                tile_keep=((tile, d), F32),
                tile_send=((tile, d), F32),
                **pick(shapes, [n for n in SAVE if n not in first_part]),
            ),
            Table(three=((t, d), F32), turned=((g.to, d), F32)),
            pick(weights, names(lambda down, downb: None)),
            1,
        )
    )
    tile_recv = other(save1.tile_send)

    def ffn(b, save, ins):
        return call(
            4,
            part(k_ffn_back, g, 8 * b),
            Table(**base_ins, **ins, **pick(save, names(lambda gel, resid, branch, mlp, n2, hid: None))),
            Table(
                gres=backs.gres,
                gbr=backs.gbr,
                keep=((deep, d), F32),
                send=((deep, d), BF),
                small=((SMALL, d), F32),
            ),
            Table(**pick(backs, names(lambda gmlp, gpre, tmp1, tmp2, dn, upg: None)), gout=((t, d), F32), **(Table(columns=((g.n_tc * 2 * tile, d), F32)) if b else Table())),
            pick(weights, names(lambda down, up: None)),
            b,
        )

    def core(b, save, f):
        return call(
            4,
            part(k_core, g, 8 * b),
            Table(
                **base_ins,
                gbr=f.gbr,
                small_in=f.small,
                **pick(save, names(lambda q, k, v, gp, prob, decay, mixed, att: None)),
            ),
            Table(
                **pick(backs, names(lambda gqkv, ggp: None)),
                keep=((deep, 256), F32),
                send=((deep, 256), BF),
                small=((SMALL, d), F32),
            ),
            pick(backs, names(lambda gatt, dlow, wlow, ulow: None)),
            pick(weights, names(lambda wo: None)),
            b,
        )

    def conv(b, save, f, e):
        ends = Table(g_keep=((half, d), F32), g_send=((half, d), BF)) if b else Table(tile=((tile, d), F32))
        return call(
            4,
            part(k_conv, g, 8 * b),
            Table(
                **base_ins,
                gres=f.gres,
                small_in=e.small,
                **pick(e, names(lambda gqkv, ggp: None)),
                **pick(save, names(lambda x, pad: None)),
            ),
            Table(**ends, small=((SMALL, d), F32)),
            Table(
                **pick(backs, names(lambda tmp1, tmp2, gpad: None)),
                gin=((t, d), F32),
                turned=((g.to, d), F32),
            ),
            pick(weights, names(lambda wq, wk, wv, gw, cw: None)),
            b,
        )

    def projections(e):
        return Table(keep_b=e.keep, recv_b=other(e.send))

    def smalls(h):
        return Table(small=h.small, small_recv=other(h.small))

    def join(f, e, h):
        size, end = g.rab if e else g.rp, 32 if h else 0
        ins = Table(meta=meta, keep_a=f.keep, recv_a=f.recv)
        outs = Table(held=((g.n_dp // 2 * size, d), F32), send=((g.n_dp // 2 * size + end, d), BF))
        scratch = Table(sum_a=((deep, d), F32))
        if e:
            ins.update(e)
            scratch = Table(scratch, sum_b=((deep, 256), F32))
        if h:
            ins.update(h)
            outs = Table(outs, apart=((8, d), F32), summed=((24, d), F32))
        found = call(1, part(k_join, g, size, h is not None), ins, outs, scratch)
        return Table(found, size=size)

    def hop(state, step):
        return Table(state, recv=lax.ppermute(state.send, "dp", xor("dp", 1 << step)))

    def take(state, step, more=None):
        size, parts = state.size, g.n_dp >> (step + 1)
        small_too = state.get(*names(lambda apart: None)) is not None
        blocks = 16 << step
        end = -(-(24 + blocks) // 16) * 16 if small_too else 0
        outs, scratch = Table(), Table()
        total = ((parts * size, d), F32)
        extra = 0 if more is None else more.shape[0]
        if parts > 1:
            outs = Table(held=((parts // 2 * size, d), F32), send=((parts // 2 * size + end + extra, d), BF))
            scratch = Table(total=total)
        else:
            outs = Table(total=total)
        ins = Table(meta=meta, got=state.held, recv=state.recv, **({} if more is None else Table(more=more)))
        if small_too:
            ins = Table(ins, was_apart=state.apart, was_summed=state.summed)
            outs = Table(outs, apart=((blocks, d), F32), summed=((24, d), F32))
        lo = state.get("lo", 0)
        return Table(call(1, part(k_step, g, step, size, small_too, lo, extra), ins, outs, scratch), size=size)

    def spread(parts):
        far_first = [lax.ppermute(parts[k], "dp", xor("dp", k)) for k in range(g.n_dp - 1, 0, -1)]
        return [parts[0]] + far_first[::-1]

    def before(table, *later):
        flat, tree = jax.tree.flatten((dict(table), later))
        return Table(jax.tree.unflatten(tree, lax.optimization_barrier(flat))[0])

    f1 = ffn(1, save1, Table(near=near, far=far, near_other=near_other, far_other=far_other))
    f1 = Table(f1, recv=other(f1.send))
    e1 = core(1, save1, f1)
    e1b = projections(e1)
    h1 = conv(1, save1, f1, e1)
    g_recv = other(h1.g_send)
    h1s = smalls(h1)
    one = join(f1, e1b, None)
    h1 = before(h1, one.send)
    one = hop(one, 0)
    f0 = ffn(0, save0, Table(g_keep=h1.g_keep, g_recv=g_recv))
    f0 = Table(f0, recv=other(f0.send))
    one = take(one, 0)
    two = join(f0, None, h1s)
    f0b = before(f0, one.get(*names(lambda send: None)), two.send)
    two = hop(two, 0)
    e0 = core(0, save0, f0b)
    e0b = projections(e0)
    two = take(two, 0, one.send if g.steps > 1 else None)
    e0 = before(e0, two.get(*names(lambda send: None)))
    if g.steps > 1:
        two = hop(two, 1)
        one = Table(one, recv=two.recv, lo=two.send.shape[0] - one.send.shape[0])
    h0 = conv(0, save0, f0, e0)
    for step in range(1, g.steps):
        one, two = take(one, step), take(two, step)
        if step + 1 < g.steps:
            one, two = hop(one, step + 1), hop(two, step + 1)
    parts0 = spread(
        call(
            1,
            part(k_last, g),
            Table(meta=meta, **e0b, **smalls(h0)),
            Table(parts=[((SMALL + g.rp // 2, d), BF if k else F32) for k in range(g.n_dp)]),
            Table(sum_b=((deep, 256), F32)),
        ).parts
    )
    n_cols = g.n_tr * g.n_tc
    shards = ((2, g.cols, g.rows), F32)
    final_shapes = dict(
        zip(
            FINAL,
            (
                ((2, g.rows, 6 * d // n_cols), F32),
                ((2, 6 * d), F32),
                ((3, 3, 2, d), F32),
                ((2, d), F32),
                shards,
                shards,
                shards,
                shards,
                ((6, 2, d), F32),
                ((2, 6), F32),
                ((2, g.rows, g.upc), F32),
                ((2, ff), F32),
                ((2, g.cols, ff // g.n_dp), F32),
                ((2, d), F32),
            ),
        )
    )
    scratch = Table(acc=((128, 640), F32), acct=((640, 128), F32), row=((8, d), F32), gms=((-(-g.n_dp // 8) * 8, 6 * d), F32))
    first = call(
        3,
        part(k_final_one, g),
        Table(
            meta=meta,
            tile_keep=save1.tile_keep,
            tile_recv=tile_recv,
            tile=h0.tile,
            got=one.total,
            apart=two.apart,
            summed=two.summed,
        ),
        Table(final_shapes, out=(tokens.shape, F32), grad=(tokens.shape, F32), cond=((deep, 128), F32)),
        scratch,
        spare=6 * VMEM_SPARE,
    )
    output = first.out
    finals = call(
        3,
        part(k_final, g),
        Table(
            meta=meta,
            got=two.total,
            parts=parts0,
            cond=first.cond,
            first={n: first[n] for n in FINAL},
        ),
        final_shapes,
        scratch,
        spare=6 * VMEM_SPARE,
    )
    finals = [finals[n] for n in FINAL]
    finals[2] = jnp.transpose(finals[2], (2, 0, 1, 3))
    finals[8] = jnp.transpose(finals[8], (1, 2, 0))
    for n in (4, 5, 6, 7, 12):
        finals[n] = jnp.swapaxes(finals[n], 1, 2)
    return (output, first.grad) + tuple(finals)


def solution(mesh):
    everywhere = P()
    tiles = P("dp", "tr", "tc", None)
    cut = P(None, "dp", ("tr", "tc"))
    in_specs = (tiles, P("dp", None), tiles) + (everywhere,) * 14
    out_specs = (tiles, tiles, cut, P(), P(), P(), cut, cut, cut, cut, P(), P(), cut, P(), cut, P())

    def program(*arrays):
        g = Geo(mesh, arrays[0].shape, arrays[13].shape)
        run = functools.partial(body, g)
        return jax.shard_map(run, mesh=mesh, in_specs=in_specs, out_specs=out_specs, check_vma=False)(*arrays)

    return program
```

```python
import functools
import inspect
import math

import jax
import jax.numpy as jnp
from jax import lax
from jax.experimental import pallas as pl
from jax.experimental.pallas import tpu as pltpu
from jax.sharding import PartitionSpec as P

BF = jnp.bfloat16
F32 = jnp.float32
EPS = 1e-06
GATE_NORM = 16.0
HALO = 2
GELU_A = 0.7978845608028654
GELU_B = 0.044715
NEG = -1e30
VMEM_SPARE = 3 * 1024 * 1024
SMALL = 32


def mm(a, b):
    return jnp.dot(a, b, preferred_element_type=F32)


def mm_rt(a, b):
    return lax.dot_general(a, b, (((1,), (1,)), ((), ())), preferred_element_type=F32)


def mm_lt(a, b):
    return lax.dot_general(a, b, (((0,), (0,)), ((), ())), preferred_element_type=F32)


def hi_lo(x):
    hi = x.astype(BF)
    return hi, (x - hi.astype(F32)).astype(BF)


def normalize(x):
    center = x - jnp.mean(x, axis=-1, keepdims=True)
    rstd = lax.rsqrt(jnp.mean(center * center, axis=-1, keepdims=True) + EPS)
    return center * rstd, rstd


def normalize_back(g_y, y, rstd):
    return rstd * (
        g_y - jnp.mean(g_y, axis=-1, keepdims=True) - y * jnp.mean(g_y * y, axis=-1, keepdims=True)
    )


def iota(shape, dim):
    return lax.broadcasted_iota(jnp.int32, shape, dim)


def names(function):
    return tuple(inspect.signature(function).parameters)


class Table(dict):
    __getattr__ = dict.__getitem__


class Geo:
    def __init__(self, mesh, tokens, up):
        self.n_dp, self.n_tr, self.n_tc = (mesh.shape[a] for a in ("dp", "tr", "tc"))
        self.images, self.own, self.tile = (tokens[0] // self.n_dp, tokens[1] // self.n_tr, tokens[2] // self.n_tc)
        self.pos = tokens[2]
        self.d = tokens[3]
        self.ff = up[2]
        self.win = self.own + HALO
        self.t = self.win * self.pos
        self.to = self.own * self.pos
        self.lt = self.d // 128
        self.pairs = self.d // 128
        self.group = 64
        self.groups = self.t // self.group
        self.ch = 3 * self.pos
        self.chunks = self.t // self.ch
        self.big = 288
        self.bigs = self.t // self.big
        self.fc = 768
        self.fcs = self.ff // self.fc
        self.shift = self.pos - self.win
        self.rows = self.d // self.n_dp
        self.rp = -(-self.rows // 16) * 16
        self.rab = -(-(self.rp + self.rp // 2) // 16) * 16
        self.steps = self.n_dp.bit_length() - 1
        self.cols = self.d // (self.n_tr * self.n_tc)
        self.upc = self.ff // (self.n_tr * self.n_tc)


def kernel_taps(w, blk):
    at = slice(blk, blk + 1)
    return [[w.cw[a, b, at, :] if blk == 0 else w.cw[b, a, at, :] for b in range(3)] for a in range(3)]


def gate_rows(g, w, blk):
    heads = w.gw.shape[0]
    rows = [w.gw[h, blk : blk + 1, :] for h in range(heads)]
    return hi_lo(jnp.concatenate(rows + [jnp.zeros((128 - heads, g.d), F32)], axis=0))


def front(g, x, mod, base, w, s):
    d, pos, ch = g.d, g.pos, g.ch
    shift, scale = mod[base : base + 1, :], 1.0 + mod[base + 1 : base + 2, :]
    zero = jnp.zeros((pos, d), BF)
    s.pad[0:pos, :] = zero
    s.pad[g.t + pos : g.t + 2 * pos, :] = zero
    for i in range(g.chunks):
        rows = slice(i * ch, (i + 1) * ch)
        y, _ = normalize(x[rows, :])
        s.pad[pos + i * ch : pos + (i + 1) * ch, :] = (y * scale + shift).astype(BF)
    at = iota((ch, 1), 0) % pos
    first, last = at == 0, at == pos - 1
    taps = kernel_taps(w, base // 8)
    blk = base // 8
    bias = w.cb[blk : blk + 1, :]
    for i in range(g.chunks):
        wide = s.pad[i * ch : i * ch + ch + 2 * pos, :].astype(F32)
        lines = [wide[a * pos : a * pos + ch, :] for a in range(3)]
        v = [sum(lines[a] * taps[a][b] for a in range(3)) for b in range(3)]
        mixed = v[1] + bias
        mixed = mixed + jnp.where(first, 0.0, pltpu.roll(v[0], 1, 0))
        mixed = mixed + jnp.where(last, 0.0, pltpu.roll(v[2], ch - 1, 0))
        s.mixed[i * ch : (i + 1) * ch, :] = mixed.astype(BF)
    for out, weight in ((s.q, w.wq), (s.k, w.wk), (s.v, w.wv)):
        out[...] = mm(s.mixed[...], weight[...]).astype(BF)
    g_hi, g_lo = gate_rows(g, w, blk)
    mixed = s.mixed[...]
    heads = w.gb.shape[1]
    bias = jnp.concatenate([w.gb[blk : blk + 1, :], jnp.zeros((1, 128 - heads), F32)], axis=1)
    both = mm_rt(mixed, jnp.concatenate([g_hi, g_lo], axis=0))
    pre = both[:, 0:128] + both[:, 128:256] + bias
    s.gp[...] = pre
    run = (jnp.minimum(pre, 0.0) - jnp.log1p(jnp.exp(-jnp.abs(pre)))) * (1.0 / GATE_NORM)
    at = iota((g.t, 1), 0) % pos
    step = 1
    while step < pos:
        run = run + jnp.where(at >= step, pltpu.roll(run, step, 0), 0.0)
        step *= 2
    s.cum[0 : g.t, :] = run


def decay_rows(g, s):
    lane = iota((1, 128), 1)
    found = {}
    for m in range((g.t + 127) // 128):
        full = s.cum[m * 128 : (m + 1) * 128, :].T
        for j in range(g.pairs):
            one, two = full[2 * j : 2 * j + 1, :], full[2 * j + 1 : 2 * j + 2, :]
            lo_row = jnp.where(lane < 64, one, pltpu.roll(two, 64, 1))
            hi_row = jnp.where(lane < 64, pltpu.roll(one, 64, 1), two)
            found[2 * m, j] = lo_row
            found[2 * m + 1, j] = hi_row
    return found


def pair_masks(g):
    row, lane = iota((64, 128), 0), iota((64, 128), 1)
    src = lane % 64
    same = (row // g.pos) == (src // g.pos)
    return lane < 64, same & (row >= src), same & (row > src)


def split_heads(block, low_half):
    zero = jnp.zeros_like(block)
    return jnp.concatenate([jnp.where(low_half, block, zero), jnp.where(low_half, zero, block)], axis=0)


def pair_blocks(g):
    for grp in range(g.groups):
        for j in range(g.pairs):
            yield grp, slice(grp * 64, grp * 64 + 64), j, slice(j * 128, j * 128 + 128)


def pair_decay(s, source, grp, j, low_half, causal):
    rows = slice(grp * 64, grp * 64 + 64)
    ct = jnp.where(low_half, s.cum[rows, 2 * j : 2 * j + 1], s.cum[rows, 2 * j + 1 : 2 * j + 2])
    return jnp.exp(jnp.where(causal, ct - source[grp, j], NEG)) * 0.125


def attend(g, s):
    low_half, causal, _ = pair_masks(g)
    source = decay_rows(g, s)
    for grp, rows, j, lanes in pair_blocks(g):
        scores = mm_rt(s.q[rows, lanes], split_heads(s.k[rows, lanes], low_half))
        decay = pair_decay(s, source, grp, j, low_half, causal)
        s.decay[rows, lanes] = decay.astype(BF)
        s.prob[rows, lanes] = (scores * decay).astype(BF)
    for _, rows, _, lanes in pair_blocks(g):
        s.att[rows, lanes] = mm(s.prob[rows, lanes], split_heads(s.v[rows, lanes], low_half)).astype(BF)


def tail(g, x, mod, base, w, s, emit):
    hidden(g, x, mod, base, w, s)
    finish_block(g, mod, base, w, s, emit)


def hidden(g, x, mod, base, w, s):
    gate_one = mod[base + 2 : base + 3, :]
    shift, scale = mod[base + 3 : base + 4, :], 1.0 + mod[base + 4 : base + 5, :]
    for i in range(g.bigs):
        rows = slice(i * g.big, (i + 1) * g.big)
        branch = mm(s.att[rows, :], w.wo[...])
        s.branch[rows, :] = branch.astype(BF)
        resid = x[rows, :] + gate_one * branch
        s.resid[rows, :] = resid
        y, _ = normalize(resid)
        s.n2[rows, :] = (y * scale + shift).astype(BF)
    for f in range(g.fcs):
        fl = slice(f * g.fc, (f + 1) * g.fc)
        for i in range(g.bigs):
            rows = slice(i * g.big, (i + 1) * g.big)
            pre = mm(s.n2[rows, :], w.up[:, fl]) + w.upb[base // 8 : base // 8 + 1, fl]
            sq = pre * pre
            half = 0.5 * jnp.tanh(pre * (GELU_A + (GELU_A * GELU_B) * sq)) + 0.5
            hid = pre * half
            s.hid[rows, fl] = hid.astype(BF)
            inner = 2.0 * GELU_A + (6.0 * GELU_A * GELU_B) * sq
            s.gel[rows, fl] = (half + hid * (1.0 - half) * inner).astype(s.gel.dtype)


def finish_block(g, mod, base, w, s, emit):
    gate_two = mod[base + 5 : base + 6, :]
    for i in range(g.bigs):
        rows = slice(i * g.big, (i + 1) * g.big)
        mlp = mm(s.hid[rows, :], w.down[...]) + w.downb[base // 8 : base // 8 + 1, :]
        s.mlp[rows, :] = mlp.astype(s.mlp.dtype)
        emit(i, s.resid[rows, :] + gate_two * mlp)


def select_cols(width, source, half, tc, c, n_tc, lanes):
    row, lane = iota((source, 2 * half), 0), iota((source, 2 * half), 1)
    core = jnp.where(lane < half, c, 1 - c)
    inside = lane % half - lanes
    want = (core * n_tc + tc) * width + inside
    hit = (row == want) & (inside >= 0) & (inside < width)
    return jnp.where(hit, 1.0, 0.0).astype(BF)


def own_sum(g, c, ref, lanes=None):
    start = pl.multiple_of(c * (HALO * g.pos), HALO * g.pos)
    if lanes is None:
        return ref[pl.ds(start, g.to), :]
    return ref[pl.ds(start, g.to), lanes]


def colsum(a):
    return jnp.sum(a.astype(F32), axis=0, keepdims=True)


def lay(g, dst, lane0, value):
    lanes = slice(lane0, lane0 + value.shape[1])
    if g.rp == g.rows:
        dst[:, lanes] = value.astype(dst.dtype)
        return
    for n in range(g.n_dp):
        part = value[n * g.rows : (n + 1) * g.rows, :]
        pad = jnp.zeros((g.rp - g.rows, value.shape[1]), F32)
        dst[n * g.rp : (n + 1) * g.rp, lanes] = jnp.concatenate([part, pad], axis=0).astype(dst.dtype)


def ffn_back(g, c, tc, g_out, mod, base, w, s, o):
    gate_one, gate_two = mod[base + 2 : base + 3, :], mod[base + 5 : base + 6, :]
    scale = 1.0 + mod[base + 4 : base + 5, :]
    for i in range(g.bigs):
        rows = slice(i * g.big, (i + 1) * g.big)
        s.gmlp[rows, :] = (gate_two * g_out[rows, :]).astype(BF)
    for f in range(g.fcs):
        fl = slice(f * g.fc, (f + 1) * g.fc)
        for i in range(g.bigs):
            rows = slice(i * g.big, (i + 1) * g.big)
            g_hid = mm_rt(s.gmlp[rows, :], w.down[fl, :])
            s.gpre[rows, fl] = (s.gel[rows, fl].astype(F32) * g_hid).astype(BF)
    for i in range(g.bigs):
        rows = slice(i * g.big, (i + 1) * g.big)
        g_n2 = mm_rt(s.gpre[rows, :], w.up[...])
        y, rstd = normalize(s.resid[rows, :])
        g_res = g_out[rows, :] + normalize_back(g_n2 * scale, y, rstd)
        s.gres[rows, :] = g_res
        s.tmp1[rows, :] = g_n2
        s.tmp2[rows, :] = g_n2 * y
        s.gbr[rows, :] = (gate_one * g_res).astype(BF)
    own = functools.partial(own_sum, g, c)
    small = o.small
    small[2:3, :] = colsum(own(s.gres) * own(s.branch).astype(F32))
    small[3:4, :] = colsum(own(s.tmp1))
    small[4:5, :] = colsum(own(s.tmp2))
    small[5:6, :] = colsum(own(g_out) * own(s.mlp).astype(F32))
    for f in range(g.ff // g.d):
        small[18 + f : 19 + f, :] = colsum(own(s.gpre, slice(f * g.d, (f + 1) * g.d)))
    small[22:23, :] = colsum(own(s.gmlp))
    n2 = own(s.n2)
    for at, core in ((0, c), (256, 1 - c)):
        first = (core * g.n_tc + tc) * g.upc
        lanes = pl.ds(pl.multiple_of(first // 128 * 128, 128), 256)
        grads = mm_lt(n2, own(s.gpre, lanes))
        s.upg[:, at : at + 256] = jnp.where(first % 128 == 0, grads, pltpu.roll(grads, 192, 1))
    sel = mm(own(s.gmlp), select_cols(g.cols, g.d, 64, tc, c, g.n_tc, 0)).astype(BF)
    s.dn[...] = mm_lt(own(s.hid), sel)
    lane = iota((g.rows, 128), 1)
    per = g.ff // g.d
    for dd in range(g.n_dp):
        up = slice(dd * g.rows, (dd + 1) * g.rows)
        down = [s.dn[(dd * per + j) * g.rows : (dd * per + j + 1) * g.rows, :] for j in range(per)]
        for at, shift, dst in ((0, 0, o.keep), (256, 64, o.send)):
            to = slice(dd * g.rp, dd * g.rp + g.rows)
            one, two, three, four = (
                pltpu.roll(part, (lanes - shift) % 128, 1) for part, lanes in zip(down, (64, 112, 32, 80))
            )
            mid = jnp.where(lane < 112, one, two)
            dst[to, 0:128] = s.upg[up, at : at + 128].astype(dst.dtype)
            dst[to, 128:256] = jnp.where(lane < 64, s.upg[up, at + 128 : at + 256], mid).astype(dst.dtype)
            end = jnp.where(lane < 80, three, four)
            dst[to, 256:384] = jnp.where(lane < 32, two, end).astype(dst.dtype)


def attn_core(g, w, s):
    low_half, causal, strict = pair_masks(g)
    s.gatt[...] = mm_rt(s.gbr[...], w.wo[...]).astype(BF)
    row, col = iota((64, 64), 0), iota((64, 64), 1)
    later = jnp.where((row // g.pos == col // g.pos) & (col >= row), 1.0, 0.0).astype(BF)
    head_of = iota((g.d, 128), 0) // 64
    to_head = jnp.where(head_of == iota((g.d, 128), 1), 1.0, 0.0).astype(BF)
    for _, rows, _, lanes in pair_blocks(g):
        d_p = mm_rt(s.gatt[rows, lanes], split_heads(s.v[rows, lanes], low_half))
        s.dlow[rows, lanes] = (d_p * s.decay[rows, lanes].astype(F32)).astype(BF)
        s.wlow[rows, lanes] = (d_p * s.prob[rows, lanes].astype(F32)).astype(BF)
    strict3 = jnp.concatenate([strict] * g.pairs, axis=1)
    for grp in range(g.groups):
        rows = slice(grp * 64, grp * 64 + 64)
        s.ulow[rows, :] = jnp.where(strict3, mm(later, s.wlow[rows, :]), 0.0).astype(BF)
    for _, rows, j, lanes in pair_blocks(g):
        km = split_heads(s.k[rows, lanes], low_half)
        s.gqkv[rows, j * 128 : j * 128 + 128] = mm(s.dlow[rows, lanes], km).astype(BF)
    for _, rows, j, lanes in pair_blocks(g):
        both = mm_lt(s.dlow[rows, lanes], s.q[rows, lanes])
        s.gqkv[rows, g.d + j * 128 : g.d + j * 128 + 128] = jnp.where(
            low_half, both[0:64, :], both[64:128, :]
        ).astype(BF)
    for _, rows, j, lanes in pair_blocks(g):
        both = mm_lt(s.prob[rows, lanes], s.gatt[rows, lanes])
        s.gqkv[rows, 2 * g.d + j * 128 : 2 * g.d + j * 128 + 128] = jnp.where(
            low_half, both[0:64, :], both[64:128, :]
        ).astype(BF)
    g_log = mm(s.ulow[...], to_head)
    s.ggp[...] = g_log * (jax.nn.sigmoid(-s.gp[...]) * (1.0 / GATE_NORM))


def proj_grads(g, c, tc, s, o, lane0):
    own = functools.partial(own_sum, g, c)
    small = o.small
    pick_cols = select_cols(g.cols, g.d, 64, tc, c, g.n_tc, 0)
    sel = [mm(own(s.gqkv, slice(n * g.d, (n + 1) * g.d)), pick_cols).astype(BF) for n in range(3)]
    sel_out = mm(own(s.gbr), pick_cols).astype(BF)
    grads = mm_lt(own(s.mixed), jnp.concatenate(sel, axis=1))
    three = mm_lt(own(s.att), sel_out)
    zero, one, two = (grads[:, n * 128 : (n + 1) * 128] for n in range(3))
    lane = iota((g.d, 128), 1)
    for shift, dst in ((0, o.keep), (64, o.send)):
        q, k, v, out = (
            pltpu.roll(part, (lanes - shift) % 128, 1)
            for part, lanes in ((zero, 0), (one, 48), (two, 96), (three, 16))
        )
        lay(g, dst, lane0, jnp.where(lane < 48, q, jnp.where(lane < 96, k, v)))
        lay(g, dst, lane0 + 128, jnp.where(lane < 16, v, out))
    gg = own(s.ggp)
    hi, lo = hi_lo(gg)
    mixed = own(s.mixed)
    gate = mm_lt(hi, mixed) + mm_lt(lo, mixed)
    small[23:29, :] = gate[0:6, :]
    small[29:30, 0:128] = colsum(gg)
    small[29:30, 128 : g.d] = jnp.zeros((1, g.d - 128), F32)


def mixed_back(g, blk, w, s):
    pos, d = g.pos, g.d
    w_hi, w_lo = gate_rows(g, w, blk)
    w_gates = jnp.concatenate([w_hi, w_hi, w_lo], axis=0)
    zero = jnp.zeros((pos, d), F32)
    s.gpad[0:pos, :] = zero
    s.gpad[g.t + pos : g.t + 2 * pos, :] = zero
    for i in range(g.bigs):
        rows = slice(i * g.big, (i + 1) * g.big)
        hi, lo = hi_lo(s.ggp[rows, :])
        total = mm(jnp.concatenate([hi, lo, hi], axis=1), w_gates)
        for n, weight in enumerate((w.wq, w.wk, w.wv)):
            total = total + mm_rt(s.gqkv[rows, n * d : (n + 1) * d], weight[...])
        s.gpad[pos + i * g.big : pos + (i + 1) * g.big, :] = total.astype(BF).astype(F32)


def conv_back(g, c, x, mod, base, w, s, o, emit):
    pos, ch, d = g.pos, g.ch, g.d
    own = functools.partial(own_sum, g, c)
    small = o.small
    at = iota((ch, 1), 0) % pos
    first, last = at == 0, at == pos - 1
    taps = kernel_taps(w, base // 8)
    scale = 1.0 + mod[base + 1 : base + 2, :]
    for i in range(g.chunks):
        rows = slice(i * ch, (i + 1) * ch)
        lines = [s.gpad[i * ch + a * pos : i * ch + a * pos + ch, :] for a in range(3)]
        v = [sum(lines[2 - a] * taps[a][b] for a in range(3)) for b in range(3)]
        g_n = v[1]
        g_n = g_n + jnp.where(last, 0.0, pltpu.roll(v[0], ch - 1, 0))
        g_n = g_n + jnp.where(first, 0.0, pltpu.roll(v[2], 1, 0))
        y, rstd = normalize(x[rows, :])
        s.tmp1[rows, :] = g_n
        s.tmp2[rows, :] = g_n * y
        emit(i, s.gres[rows, :] + normalize_back(g_n * scale, y, rstd))
    small[0:1, :] = colsum(own(s.tmp1))
    small[1:2, :] = colsum(own(s.tmp2))


def kernel_grads(g, c, mod, s, o):
    pos, d = g.pos, g.d
    small = o.small
    oc = 4 * pos
    at = iota((oc, 1), 0) % pos
    first, last = at == 0, at == pos - 1
    sums = [jnp.zeros((8, d), F32) for _ in range(10)]
    for i in range(g.to // oc):
        start = c * (HALO * pos) + i * oc
        mid = s.gpad[pl.ds(pl.multiple_of(start + pos, pos), oc), :]
        shifted = [
            jnp.where(last, 0.0, pltpu.roll(mid, oc - 1, 0)),
            mid,
            jnp.where(first, 0.0, pltpu.roll(mid, 1, 0)),
        ]
        for a in range(3):
            line = s.pad[pl.ds(pl.multiple_of(start + a * pos, pos), oc), :].astype(F32)
            for b in range(3):
                sums[3 * a + b] = sums[3 * a + b] + jnp.sum((line * shifted[b]).reshape(oc // 8, 8, d), axis=0)
        sums[9] = sums[9] + jnp.sum(mid.reshape(oc // 8, 8, d), axis=0)
    for n in range(10):
        small[8 + n : 9 + n, :] = jnp.sum(sums[n], axis=0, keepdims=True)
    small[6:7, :] = mod[6:7, :]
    small[7:8, :] = jnp.zeros((1, d), F32)
    small[30:SMALL, :] = jnp.zeros((SMALL - 30, d), F32)


def attn_back(g, c, tc, x, mod, base, w, s, o, lane0, emit):
    attn_core(g, w, s)
    proj_grads(g, c, tc, s, o, lane0)
    mixed_back(g, base // 8, w, s)
    conv_back(g, c, x, mod, base, w, s, o, emit)
    kernel_grads(g, c, mod, s, o)


def k_prep(g, s):
    c = s.meta[0]
    t = s.tok[0].reshape(g.own * g.tile, g.d).astype(BF)
    s.tokb[...] = t
    edge = HALO * g.tile

    @pl.when(c == 0)
    def _():
        s.halo[...] = t[g.own * g.tile - edge :, :]

    @pl.when(c == 1)
    def _():
        s.halo[...] = t[0:edge, :]


def k_cast(g, s):
    s.low[...] = s.cot[0].reshape(g.own * g.tile, g.d).astype(BF)


def k_rows(g, s):
    c, size = s.meta[0], g.own * g.tile
    s.both[pl.ds(pl.multiple_of(c * size, size), size), :] = s.mine[...]
    s.both[pl.ds(pl.multiple_of((1 - c) * size, size), size), :] = s.theirs[...]


def k_stack(s):
    rows = s.mine.shape[0]
    s.both[0:rows, :] = s.mine[...]
    s.both[rows:, :] = s.theirs[...]


def k_extend(g, s):
    c = s.meta[0]
    edge = HALO * g.tile
    own = g.own * g.tile
    s.ext[pl.ds(pl.multiple_of(c * edge, edge), own), :] = s.tokb[...]
    s.ext[pl.ds(pl.multiple_of((1 - c) * own, edge), edge), :] = s.halo[...]


def k_modulate(g, s):
    mod = s.mod
    act = jax.nn.silu(s.cond[...]).astype(BF)
    rows = jnp.broadcast_to(act, (16, g.d))
    for b in range(2):
        for n in range(6):
            lanes = slice(n * g.d, (n + 1) * g.d)
            out = mm(rows, s.ada_w[b, :, lanes])[0:1, :] + s.ada_b[b : b + 1, lanes]
            mod[b * 8 + n : b * 8 + n + 1, :] = out
        mod[b * 8 + 6 : b * 8 + 7, :] = act.astype(F32)
        mod[b * 8 + 7 : b * 8 + 8, :] = jnp.zeros((1, g.d), F32)


def place_tiles(g, s, lo, lines, dst):
    tc = s.meta[1]
    for k in range(g.n_tc):
        part = s.tiles[k][lo : lo + lines * g.tile, :].astype(F32)
        off = (tc ^ k) * g.tile
        for i in range(lines):
            dst[pl.ds(pl.multiple_of(i * g.pos + off, g.tile), g.tile), :] = part[i * g.tile : (i + 1) * g.tile, :]


def turn(g, ref, start, dst):
    block = ref[pl.ds(start, g.to), :].reshape(g.own, g.pos, g.d)
    dst[...] = jnp.swapaxes(block, 0, 1).reshape(g.to, g.d)


def part_of(g, ref, core):
    return ref[pl.ds(pl.multiple_of(core * (g.shift * g.own), g.own), g.win * g.own), :]


STACKED = names(lambda wq, wk, wv, wo, up, down: None)


class Refs:
    def __init__(self, table, block, sources, buffers, sems):
        self.__dict__.update(table)
        self.buffers, self.copies = buffers, {}
        for n, (name, src) in enumerate(sources.items()):
            src = src.at[block] if name in STACKED else src
            self.copies[name] = pltpu.make_async_copy(src, buffers[name], sems.at[n])
            self.copies[name].start()

    def __getattr__(self, name):
        copy = self.copies.pop(name, None)
        if copy is not None:
            copy.wait()
        return self.buffers[name]

    def __getitem__(self, name):
        return getattr(self, name)

    def finish(self):
        for name in list(self.copies):
            getattr(self, name)


FRONT_W = names(lambda cw, cb, wq, wk, wv, gw, gb: None)
TAIL_W = names(lambda wo, up, upb, down, downb: None)
SAVE = names(lambda x, mixed, q, k, v, gp, att, branch, resid, n2, hid, gel, mlp, prob, decay, pad: None)


def save_shapes(g):
    t, d, ff = g.t, g.d, g.ff
    return Table(
        x=((t, d), F32),
        mixed=((t, d), BF),
        q=((t, d), BF),
        k=((t, d), BF),
        v=((t, d), BF),
        gp=((t, 128), F32),
        att=((t, d), BF),
        branch=((t, d), BF),
        resid=((t, d), F32),
        n2=((t, d), BF),
        hid=((t, ff), BF),
        gel=((t, ff), BF),
        mlp=((t, d), BF),
        prob=((t, d), BF),
        decay=((t, d), BF),
        pad=((t + 2 * g.pos, d), BF),
        cum=(((t + 127) // 128 * 128, 128), F32),
    )


def back_shapes(g):
    t, d, ff = g.t, g.d, g.ff
    return Table(
        gmlp=((t, d), BF),
        gpre=((t, ff), BF),
        gres=((t, d), F32),
        tmp1=((t, d), F32),
        tmp2=((t, d), F32),
        gbr=((t, d), BF),
        dn=((ff, 128), F32),
        upg=((d, 512), F32),
        gatt=((t, d), BF),
        dlow=((t, d), BF),
        wlow=((t, d), BF),
        ulow=((t, d), BF),
        gqkv=((t, 3 * d), BF),
        ggp=((t, 128), F32),
        gpad=((t + 2 * g.pos, d), F32),
    )


def k_first(g, s):
    c = s.meta[0]
    x, mod, turned = s.x, s.mod, s.turned
    place_tiles(g, s, 0, g.win, x)
    s.cum[g.t :, :] = jnp.zeros((s.cum.shape[0] - g.t, 128), F32)
    front(g, x, mod, 0, s, s)
    attend(g, s)

    def emit(i, value):
        s.mid[i * g.big : (i + 1) * g.big, :] = value

    tail(g, x, mod, 0, s, s, emit)
    turn(g, s.mid, pl.multiple_of(c * (HALO * g.pos), g.pos), turned)
    s.keep_mid[...] = part_of(g, turned, c)
    s.send[...] = part_of(g, turned, 1 - c).astype(BF)


def weave(g, c, keep, recv, dst):
    for i in range(g.win):
        rows = slice(i * g.own, (i + 1) * g.own)
        a = pl.multiple_of(i * g.pos + c * g.own, g.own)
        b = pl.multiple_of(i * g.pos + (1 - c) * g.own, g.own)
        dst[pl.ds(a, g.own), :] = keep[rows, :].astype(F32)
        dst[pl.ds(b, g.own), :] = recv[rows, :].astype(F32)


def k_second(g, s):
    weave(g, s.meta[0], s.keep_mid, s.recv, s.x)
    s.cum[g.t :, :] = jnp.zeros((s.cum.shape[0] - g.t, 128), F32)
    front(g, s.x, s.mod, 8, s, s)
    attend(g, s)
    hidden(g, s.x, s.mod, 8, s, s)


def k_second_tail(g, s):
    c, tc = s.meta[0], s.meta[1]
    mod, turned = s.mod, s.turned

    def emit(i, value):
        s.three[i * g.big : (i + 1) * g.big, :] = value

    finish_block(g, mod, 8, s, s, emit)
    turn(g, s.three, pl.multiple_of(c * (HALO * g.pos), g.pos), turned)
    at = (tc * g.tile) % g.own
    for r in range(g.own):
        rows = slice(r * g.tile, (r + 1) * g.tile)
        mine = pl.multiple_of((c * g.own + r) * g.own + at, g.tile)
        theirs = pl.multiple_of(((1 - c) * g.own + r) * g.own + at, g.tile)
        s.tile_keep[rows, :] = turned[pl.ds(mine, g.tile), :]
        s.tile_send[rows, :] = turned[pl.ds(theirs, g.tile), :]


def k_ffn_back(g, base, s):
    c, tc = s.meta[0], s.meta[1]
    if base == 0:
        weave(g, c, s.g_keep, s.g_recv, s.gout)
    else:
        rows = g.own * g.n_tr
        size = rows * g.tile
        for k in range(g.n_tc):
            half = k < g.n_tc // 2
            for core, src in ((c, s.near if half else s.far), (1 - c, s.near_other if half else s.far_other)):
                at = k % (g.n_tc // 2) * (size // 2)
                block = src[at : at + size // 2, :].astype(F32).reshape(g.own, g.tile, g.d)
                lines = jnp.swapaxes(block, 0, 1)
                for n in range(g.tile):
                    to = ((tc ^ k) * g.tile + n) * rows + core * g.own
                    s.columns[pl.ds(pl.multiple_of(to, g.own), g.own), :] = lines[n]
        s.gout[...] = s.columns[pl.ds(pl.multiple_of(c * (g.shift * rows), rows), g.t), :]
    s.small[...] = jnp.zeros((SMALL, g.d), F32)
    ffn_back(g, c, tc, s.gout, s.mod, base, s, s, s)


def k_core(g, base, s):
    c, tc = s.meta[0], s.meta[1]
    s.small[...] = s.small_in[...]
    attn_core(g, s, s)
    proj_grads(g, c, tc, s, s, 0)


def k_conv(g, base, s):
    c, tc = s.meta[0], s.meta[1]
    mixed_back(g, base // 8, s, s)
    s.small[...] = s.small_in[...]

    def emit(i, value):
        s.gin[i * g.ch : (i + 1) * g.ch, :] = value

    conv_back(g, c, s.x, s.mod, base, s, s, s, emit)
    kernel_grads(g, c, s.mod, s, s)
    turned = s.turned
    turn(g, s.gin, pl.multiple_of(c * (HALO * g.pos), g.pos), turned)
    if base:
        s.g_keep[...] = part_of(g, turned, c)
        s.g_send[...] = part_of(g, turned, 1 - c).astype(BF)
        return
    size = g.tile * g.own
    block = turned[pl.ds(pl.multiple_of(tc * size, size), size), :]
    s.tile[...] = jnp.swapaxes(block.reshape(g.tile, g.own, g.d), 0, 1).reshape(size, g.d)


def both_cores(s):
    both = s.small[...] + s.small_recv[...]
    return jnp.where(iota(both.shape, 0) == 6, s.small[...], both)


def side_by_side(g, part):
    half = g.rp // 2
    return jnp.concatenate([part[0:half, 0:192], part[half:, 0:192]], axis=1)


def k_join(g, size, small_too, s):
    bit = s.meta[2] % 2
    half = g.rp // 2
    s.sum_a[...] = s.keep_a[...] + s.recv_a[...].astype(F32)
    if size == g.rab:
        s.sum_b[...] = s.keep_b[...] + s.recv_b[...].astype(F32)
    if small_too:
        small = both_cores(s)
        s.apart[...], s.summed[...] = small[0:8, :], small[8:SMALL, :]
        end = (g.n_dp // 2) * size
        s.send[end : end + 24, :] = small[8:SMALL, :].astype(BF)
        s.send[end + 24 : end + 32, :] = small[0:8, :].astype(BF)
    for m in range(g.n_dp // 2):
        for which, dst in ((bit, s.held), (1 - bit, s.send)):
            rows = pl.ds(pl.multiple_of((2 * m + which) * g.rp, g.rp), g.rp)
            dst[m * size : m * size + g.rp, :] = s.sum_a[rows, :].astype(dst.dtype)
            if size == g.rab:
                packed = side_by_side(g, s.sum_b[rows, :])
                rest = size - g.rp - half
                if rest:
                    packed = jnp.concatenate([packed, jnp.zeros((rest, g.d), F32)], axis=0)
                dst[m * size + g.rp : (m + 1) * size, :] = packed.astype(dst.dtype)


def k_step(g, step, size, small_too, lo, extra, s):
    parts = g.n_dp >> (step + 1)
    s.total[...] = s.got[...] + s.recv[lo : lo + parts * size, :].astype(F32)
    blocks = 8 << step
    end = lo + parts * size
    if extra:
        s.send[s.send.shape[0] - extra :, :] = s.more[...]
    if small_too:
        summed = s.was_summed[...] + s.recv[end : end + 24, :].astype(F32)
        s.summed[...] = summed
        s.apart[0:blocks, :] = s.was_apart[...]
        s.apart[blocks : 2 * blocks, :] = s.recv[end + 24 : end + 24 + blocks, :].astype(F32)
    if parts == 1:
        return
    bit = (s.meta[2] // (2 << step)) % 2
    for m in range(parts // 2):
        for which, dst in ((bit, s.held), (1 - bit, s.send)):
            rows = pl.ds(pl.multiple_of((2 * m + which) * size, size), size)
            dst[m * size : (m + 1) * size, :] = s.total[rows, :].astype(dst.dtype)
    if small_too:
        end = (parts // 2) * size
        s.send[end : end + 24, :] = summed.astype(BF)
        s.send[end + 24 : end + 24 + 2 * blocks, :] = s.apart[...].astype(BF)


def k_last(g, s):
    me = s.meta[2]
    s.sum_b[...] = s.keep_b[...] + s.recv_b[...].astype(F32)
    small = both_cores(s)
    for k in range(g.n_dp):
        rows = pl.ds(pl.multiple_of((me ^ k) * g.rp, g.rp), g.rp)
        out = s.parts[k]
        out[0:SMALL, :] = small.astype(out.dtype)
        out[SMALL:, :] = side_by_side(g, s.sum_b[rows, :]).astype(out.dtype)


def finish(g, b, s, ab, proj, summed, apart):
    c, tc, me = s.meta[0], s.meta[1], s.meta[2]
    idx = c * g.n_tc + tc
    rp, rows, half = g.rp, g.rows, g.rp // 2
    acc, acct = s.acc, s.acct
    s.up_weight[b] = ab[0:rows, 0 : g.upc]
    acc[0:rp, 0:384] = ab
    acc[0:half, 384:576] = proj[:, 0:192]
    acc[half:rp, 384:576] = proj[:, 192:384]
    for n in range(1, 5):
        acct[n * 128 : (n + 1) * 128, :] = acc[:, n * 128 : (n + 1) * 128].T
    for j in range(g.ff // g.d):
        at = 192 + g.cols * j
        s.down_weight[b, :, j * rows : (j + 1) * rows] = acct[at : at + g.cols, 0:rows]
    for j, ref in enumerate((s.query, s.key, s.value, s.proj)):
        at = 384 + g.cols * j
        ref[b] = acct[at : at + g.cols, 0:rows]
    for a in range(3):
        for e in range(3):
            at = 3 * a + e if b == 0 else 3 * e + a
            s.conv_weight[a, e, b : b + 1, :] = summed[at : at + 1, :]
    s.conv_bias[b : b + 1, :] = summed[9:10, :]
    for m in range(g.ff // g.d):
        s.up_bias[b : b + 1, m * g.d : (m + 1) * g.d] = summed[10 + m : 11 + m, :]
    s.down_bias[b : b + 1, :] = summed[14:15, :]
    for h in range(6):
        s.gate_weight[h, b : b + 1, :] = summed[15 + h : 16 + h, :]
    s.row[...] = jnp.broadcast_to(summed[21:22, :], (8, g.d))
    s.gate_bias[b : b + 1, :] = s.row[0:1, 0:6]
    width = 6 * g.d // (g.n_tr * g.n_tc)
    wide = 384
    prod = jnp.zeros((rp, wide), F32)
    total = apart[0]
    for part in apart[1:]:
        total = total + part
    for m in range(6):
        s.ada_bias[b : b + 1, m * g.d : (m + 1) * g.d] = total[m : m + 1, :]
    pieces = []
    for m in range(6):
        lines = [part[m : m + 1, :] for part in apart]
        pieces.append(jnp.concatenate(lines + [jnp.zeros((-len(apart) % 8, g.d), F32)] * (len(apart) % 8 > 0), axis=0))
    s.gms[...] = jnp.concatenate(pieces, axis=1)
    full = pltpu.roll(s.gms[...], 6 * g.d - idx * width, 1)
    for k in range(g.n_dp):
        cond = s.cond[k * rp : (k + 1) * rp, :]
        prod = prod + jnp.concatenate([cond] * (wide // 128), axis=1) * full[k : k + 1, 0:wide]
    s.ada_weight[b] = prod[0:rows, 0:width]


FINAL = names(
    lambda ada_weight, ada_bias, conv_weight, conv_bias, query, key, value, proj, gate_weight, gate_bias,
    up_weight, up_bias, down_weight, down_bias: None
)
BY_ROW = names(lambda ada_bias, conv_bias, gate_bias, up_bias, down_bias: None)
INNER = names(lambda conv_weight, gate_weight: None)


def k_final_one(g, s):
    c, tc = s.meta[0], s.meta[1]
    near = (tc * g.tile) // g.own == c

    @pl.when(near)
    def _():
        s.out[0] = s.tile_keep[...].reshape(g.own, g.tile, g.d)

    @pl.when(jnp.logical_not(near))
    def _():
        s.out[0] = s.tile_recv[...].reshape(g.own, g.tile, g.d)

    s.grad[0] = s.tile[...].reshape(g.own, g.tile, g.d)
    half = g.rp // 2
    total = s.got[...]
    apart = [s.apart[8 * n : 8 * n + 8, :] for n in range(g.n_dp)]
    for k, part in enumerate(apart):
        column = jnp.broadcast_to(part[6:7, :], (128, g.d)).T
        column = pltpu.roll(column, g.d - s.meta[2] * g.rows, 0)
        s.cond[k * g.rp : (k + 1) * g.rp, :] = column[0 : g.rp, :]
    finish(g, 1, s, total[0 : g.rp, :], total[g.rp : g.rp + half, :], s.summed[...], apart)


def k_final(g, s):
    for name in FINAL:
        src, dst = s.first[name], s[name]
        if name in BY_ROW:
            dst[1:2, :] = src[1:2, :]
        elif name in INNER:
            lead = (slice(None),) * (len(dst.shape) - 2)
            dst[lead + (slice(1, 2),)] = src[lead + (slice(1, 2),)]
        else:
            dst[1] = src[1]
    ab = s.got[...]
    proj = s.parts[0][SMALL:, :]
    summed = s.parts[0][8:SMALL, :]
    apart = []
    for k, part in enumerate(s.parts):
        wide = part[...].astype(F32)
        apart.append(wide[0:8, :])
        if k:
            summed = summed + wide[8:SMALL, :]
            proj = proj + wide[SMALL:, :]
    finish(g, 0, s, ab, proj, summed, apart)


def padded_bytes(shape, dtype):
    shape = (1,) * (2 - len(shape)) + tuple(shape)
    rows, lanes = -(-shape[-2] // 16) * 16, -(-shape[-1] // 128) * 128
    return math.prod(shape[:-2]) * rows * lanes * jnp.dtype(dtype).itemsize


def call(us, kernel, ins, outs, scratch=(), weights=(), block=0, spare=VMEM_SPARE, fetch=()):
    ins = Table(ins, **dict(weights))
    ins, outs, scratch = dict(ins), dict(outs), dict(scratch)
    sources = {n: ins.pop(n) for n in fetch}
    buffers = {n: (a.shape[1:] if n in STACKED else a.shape, a.dtype) for n, a in sources.items()}
    flat, tree = jax.tree.flatten(ins)
    spread_outs = [o if isinstance(o, list) else [o] for o in outs.values()]
    flat_outs = [o for group in spread_outs for o in group]
    meta = ins.get("meta")

    def run(*refs):
        refs = list(refs)

        def take(n):
            got = refs[:n]
            del refs[:n]
            return got

        table = Table(jax.tree.unflatten(tree, take(len(flat))))
        hbm = dict(zip(sources, take(len(sources))))
        for name, ref in table.items():
            if name in STACKED:
                table[name] = ref.at[block]
        for name, o in outs.items():
            table[name] = take(len(o)) if isinstance(o, list) else take(1)[0]
        table.update(zip(scratch, take(len(scratch))))
        held = dict(zip(buffers, take(len(buffers))))
        s = Refs(table, block, hbm, held, refs[0] if refs else None)
        kernel(s)
        s.finish()

    held = [(a.shape, a.dtype) for a in flat] + flat_outs + list(scratch.values()) + list(buffers.values())
    need = sum(padded_bytes(*h) for h in held)
    results = pl.pallas_call(
        run,
        in_specs=[pl.BlockSpec(memory_space=pltpu.SMEM if a is meta else pltpu.VMEM) for a in flat]
        + [pl.BlockSpec(memory_space=pl.ANY)] * len(sources),
        out_specs=[pl.BlockSpec(memory_space=pltpu.VMEM)] * len(flat_outs),
        out_shape=[jax.ShapeDtypeStruct(*o) for o in flat_outs],
        scratch_shapes=[pltpu.VMEM(*sc) for sc in (*scratch.values(), *buffers.values())]
        + [pltpu.SemaphoreType.DMA((len(sources),))] * bool(sources),
        compiler_params=pltpu.CompilerParams(vmem_limit_bytes=need + need // 16 + spare),
        cost_estimate=pl.CostEstimate(flops=int(us * 1e9), bytes_accessed=int(us * 3e6), transcendentals=0),
    )(*flat, *sources.values())
    results = list(results)
    found = Table()
    for name, o in outs.items():
        if isinstance(o, list):
            found[name] = results[: len(o)]
            del results[: len(o)]
        else:
            found[name] = results.pop(0)
    return found


def body(
    g,
    tokens,
    condition,
    cotangent,
    ada_weight,
    ada_bias,
    conv_weight,
    conv_bias,
    query_weight,
    key_weight,
    value_weight,
    out_weight,
    gate_weight,
    gate_bias,
    up_weight,
    up_bias,
    down_weight,
    down_bias,
):
    d, ff, t = g.d, g.ff, g.t
    meta = jnp.stack(
        [lax.axis_index("tr"), lax.axis_index("tc"), lax.axis_index("dp"), jnp.int32(0)]
    ).astype(jnp.int32)

    def xor(axis, k):
        return [(i, i ^ k) for i in range(lax.axis_size(axis))]

    def other(array):
        return lax.ppermute(array, "tr", [(0, 1), (1, 0)])

    part = functools.partial
    tile, half, deep = g.own * g.tile, g.win * g.own, g.n_dp * g.rp
    shapes, backs = save_shapes(g), back_shapes(g)
    weights = Table(
        wq=query_weight,
        wk=key_weight,
        wv=value_weight,
        wo=out_weight,
        gw=jnp.transpose(gate_weight, (2, 0, 1)),
        gb=gate_bias,
        cw=jnp.transpose(conv_weight, (1, 2, 0, 3)),
        cb=conv_bias,
        up=up_weight,
        upb=up_bias,
        down=down_weight,
        downb=down_bias,
    )

    def pick(table, names):
        return {n: table[n] for n in names}

    r = call(
        1,
        part(k_prep, g),
        Table(meta=meta, tok=tokens),
        Table(tokb=((tile, d), BF), halo=((HALO * g.tile, d), BF)),
    )
    halo = other(r.halo)
    cot = call(1, part(k_cast, g), Table(cot=cotangent), Table(low=((tile, d), BF))).low
    ext = call(
        1,
        part(k_extend, g),
        Table(meta=meta, tokb=r.tokb, halo=halo),
        Table(ext=((half // 2, d), BF)),
    ).ext
    ext, condition = lax.optimization_barrier((ext, condition))
    tiles = [ext] + [lax.ppermute(ext, "tc", xor("tc", k)) for k in range(1, g.n_tc)]

    ext_done, cot = lax.optimization_barrier((ext, cot))
    cot_next = lax.ppermute(cot, "tc", xor("tc", 1))
    mod = call(
        1,
        part(k_modulate, g),
        Table(cond=condition, ada_w=ada_weight, ada_b=ada_bias),
        Table(mod=((16, d), F32)),
    ).mod
    base_ins = Table(meta=meta, mod=mod)
    save0 = call(
        8,
        part(k_first, g),
        Table(**base_ins, tiles=tiles),
        Table(
            keep_mid=((half, d), F32),
            send=((half, d), BF),
            **pick(shapes, SAVE),
        ),
        Table(mid=((t, d), F32), turned=((g.to, d), F32), cum=shapes.cum),
        pick(weights, FRONT_W + TAIL_W),
        0,
    )
    sent, cot_next = lax.optimization_barrier((save0.send, cot_next))
    near = call(1, k_stack, Table(mine=cot, theirs=cot_next), Table(both=((2 * tile, d), BF))).both
    far = lax.ppermute(near, "tc", xor("tc", 2))
    first_part = names(lambda x, mixed, q, k, v, gp, att, prob, decay, pad, branch, resid, n2, hid, gel: None)
    save1 = call(
        4,
        part(k_second, g),
        Table(**base_ins, keep_mid=save0.keep_mid, recv=other(sent)),
        pick(shapes, first_part),
        Table(cum=shapes.cum),
        pick(weights, FRONT_W + names(lambda wo, up, upb: None)),
        1,
    )
    resid, far = lax.optimization_barrier((save1.resid, far))
    near_other, far_other = other(near), other(far)
    save1 = Table(save1, resid=resid)
    save1.update(
        call(
            4,
            part(k_second_tail, g),
            Table(**base_ins, resid=resid, hid=save1.hid),
            Table(
                tile_keep=((tile, d), F32),
                tile_send=((tile, d), F32),
                **pick(shapes, [n for n in SAVE if n not in first_part]),
            ),
            Table(three=((t, d), F32), turned=((g.to, d), F32)),
            pick(weights, names(lambda down, downb: None)),
            1,
        )
    )
    tile_recv = other(save1.tile_send)

    def ffn(b, save, ins):
        return call(
            4,
            part(k_ffn_back, g, 8 * b),
            Table(**base_ins, **ins, **pick(save, names(lambda gel, resid, branch, mlp, n2, hid: None))),
            Table(
                gres=backs.gres,
                gbr=backs.gbr,
                keep=((deep, d), F32),
                send=((deep, d), BF),
                small=((SMALL, d), F32),
            ),
            Table(**pick(backs, names(lambda gmlp, gpre, tmp1, tmp2, dn, upg: None)), gout=((t, d), F32), **(Table(columns=((g.n_tc * 2 * tile, d), F32)) if b else Table())),
            pick(weights, names(lambda down, up: None)),
            b,
        )

    def core(b, save, f):
        return call(
            4,
            part(k_core, g, 8 * b),
            Table(
                **base_ins,
                gbr=f.gbr,
                small_in=f.small,
                **pick(save, names(lambda q, k, v, gp, prob, decay, mixed, att: None)),
            ),
            Table(
                **pick(backs, names(lambda gqkv, ggp: None)),
                keep=((deep, 256), F32),
                send=((deep, 256), BF),
                small=((SMALL, d), F32),
            ),
            pick(backs, names(lambda gatt, dlow, wlow, ulow: None)),
            pick(weights, names(lambda wo: None)),
            b,
        )

    def conv(b, save, f, e):
        ends = Table(g_keep=((half, d), F32), g_send=((half, d), BF)) if b else Table(tile=((tile, d), F32))
        return call(
            4,
            part(k_conv, g, 8 * b),
            Table(
                **base_ins,
                gres=f.gres,
                small_in=e.small,
                **pick(e, names(lambda gqkv, ggp: None)),
                **pick(save, names(lambda x, pad: None)),
            ),
            Table(**ends, small=((SMALL, d), F32)),
            Table(
                **pick(backs, names(lambda tmp1, tmp2, gpad: None)),
                gin=((t, d), F32),
                turned=((g.to, d), F32),
            ),
            pick(weights, names(lambda wq, wk, wv, gw, cw: None)),
            b,
        )

    def projections(e):
        return Table(keep_b=e.keep, recv_b=other(e.send))

    def smalls(h):
        return Table(small=h.small, small_recv=other(h.small))

    def join(f, e, h):
        size, end = g.rab if e else g.rp, 32 if h else 0
        ins = Table(meta=meta, keep_a=f.keep, recv_a=f.recv)
        outs = Table(held=((g.n_dp // 2 * size, d), F32), send=((g.n_dp // 2 * size + end, d), BF))
        scratch = Table(sum_a=((deep, d), F32))
        if e:
            ins.update(e)
            scratch = Table(scratch, sum_b=((deep, 256), F32))
        if h:
            ins.update(h)
            outs = Table(outs, apart=((8, d), F32), summed=((24, d), F32))
        found = call(1, part(k_join, g, size, h is not None), ins, outs, scratch)
        return Table(found, size=size)

    def hop(state, step):
        return Table(state, recv=lax.ppermute(state.send, "dp", xor("dp", 1 << step)))

    def take(state, step, more=None):
        size, parts = state.size, g.n_dp >> (step + 1)
        small_too = state.get(*names(lambda apart: None)) is not None
        blocks = 16 << step
        end = -(-(24 + blocks) // 16) * 16 if small_too else 0
        outs, scratch = Table(), Table()
        total = ((parts * size, d), F32)
        extra = 0 if more is None else more.shape[0]
        if parts > 1:
            outs = Table(held=((parts // 2 * size, d), F32), send=((parts // 2 * size + end + extra, d), BF))
            scratch = Table(total=total)
        else:
            outs = Table(total=total)
        ins = Table(meta=meta, got=state.held, recv=state.recv, **({} if more is None else Table(more=more)))
        if small_too:
            ins = Table(ins, was_apart=state.apart, was_summed=state.summed)
            outs = Table(outs, apart=((blocks, d), F32), summed=((24, d), F32))
        lo = state.get("lo", 0)
        return Table(call(1, part(k_step, g, step, size, small_too, lo, extra), ins, outs, scratch), size=size)

    def spread(parts):
        far_first = [lax.ppermute(parts[k], "dp", xor("dp", k)) for k in range(g.n_dp - 1, 0, -1)]
        return [parts[0]] + far_first[::-1]

    def before(table, *later):
        flat, tree = jax.tree.flatten((dict(table), later))
        return Table(jax.tree.unflatten(tree, lax.optimization_barrier(flat))[0])

    f1 = ffn(1, save1, Table(near=near, far=far, near_other=near_other, far_other=far_other))
    f1 = Table(f1, recv=other(f1.send))
    e1 = core(1, save1, f1)
    e1b = projections(e1)
    h1 = conv(1, save1, f1, e1)
    g_recv = other(h1.g_send)
    h1s = smalls(h1)
    one = join(f1, e1b, None)
    h1 = before(h1, one.send)
    one = hop(one, 0)
    f0 = ffn(0, save0, Table(g_keep=h1.g_keep, g_recv=g_recv))
    f0 = Table(f0, recv=other(f0.send))
    one = take(one, 0)
    two = join(f0, None, h1s)
    f0b = before(f0, one.get(*names(lambda send: None)), two.send)
    two = hop(two, 0)
    e0 = core(0, save0, f0b)
    e0b = projections(e0)
    two = take(two, 0, one.send if g.steps > 1 else None)
    e0 = before(e0, two.get(*names(lambda send: None)))
    if g.steps > 1:
        two = hop(two, 1)
        one = Table(one, recv=two.recv, lo=two.send.shape[0] - one.send.shape[0])
    h0 = conv(0, save0, f0, e0)
    for step in range(1, g.steps):
        one, two = take(one, step), take(two, step)
        if step + 1 < g.steps:
            one, two = hop(one, step + 1), hop(two, step + 1)
    parts0 = spread(
        call(
            1,
            part(k_last, g),
            Table(meta=meta, **e0b, **smalls(h0)),
            Table(parts=[((SMALL + g.rp // 2, d), BF if k else F32) for k in range(g.n_dp)]),
            Table(sum_b=((deep, 256), F32)),
        ).parts
    )
    n_cols = g.n_tr * g.n_tc
    shards = ((2, g.cols, g.rows), F32)
    final_shapes = dict(
        zip(
            FINAL,
            (
                ((2, g.rows, 6 * d // n_cols), F32),
                ((2, 6 * d), F32),
                ((3, 3, 2, d), F32),
                ((2, d), F32),
                shards,
                shards,
                shards,
                shards,
                ((6, 2, d), F32),
                ((2, 6), F32),
                ((2, g.rows, g.upc), F32),
                ((2, ff), F32),
                ((2, g.cols, ff // g.n_dp), F32),
                ((2, d), F32),
            ),
        )
    )
    scratch = Table(acc=((128, 640), F32), acct=((640, 128), F32), row=((8, d), F32), gms=((-(-g.n_dp // 8) * 8, 6 * d), F32))
    first = call(
        3,
        part(k_final_one, g),
        Table(
            meta=meta,
            tile_keep=save1.tile_keep,
            tile_recv=tile_recv,
            tile=h0.tile,
            got=one.total,
            apart=two.apart,
            summed=two.summed,
        ),
        Table(final_shapes, out=(tokens.shape, F32), grad=(tokens.shape, F32), cond=((deep, 128), F32)),
        scratch,
        spare=6 * VMEM_SPARE,
    )
    output = first.out
    finals = call(
        3,
        part(k_final, g),
        Table(
            meta=meta,
            got=two.total,
            parts=parts0,
            cond=first.cond,
            first={n: first[n] for n in FINAL},
        ),
        final_shapes,
        scratch,
        spare=6 * VMEM_SPARE,
    )
    finals = [finals[n] for n in FINAL]
    finals[2] = jnp.transpose(finals[2], (2, 0, 1, 3))
    finals[8] = jnp.transpose(finals[8], (1, 2, 0))
    for n in (4, 5, 6, 7, 12):
        finals[n] = jnp.swapaxes(finals[n], 1, 2)
    return (output, first.grad) + tuple(finals)


def solution(mesh):
    everywhere = P()
    tiles = P("dp", "tr", "tc", None)
    cut = P(None, "dp", ("tr", "tc"))
    in_specs = (tiles, P("dp", None), tiles) + (everywhere,) * 14
    out_specs = (tiles, tiles, cut, P(), P(), P(), cut, cut, cut, cut, P(), P(), cut, P(), cut, P())

    def program(*arrays):
        g = Geo(mesh, arrays[0].shape, arrays[13].shape)
        run = functools.partial(body, g)
        return jax.shard_map(run, mesh=mesh, in_specs=in_specs, out_specs=out_specs, check_vma=False)(*arrays)

    return program
```
